32 devices in a mesh: dp: 8 (over z, x), mp: 4 (over y, core).
Axes of the slice: x: 2, y: 2, z: 4, core: 2. Of those that a mesh axis runs over, the one named last changes fastest.
Arguments:
- decoder_in: bfloat16 [8, 512, 768], P('dp', 'mp'), may hold values from -6 to 6
- encoder_states: bfloat16 [8, 512, 768], P('dp', 'mp'), may hold values from -6 to 6
- dec_segments: int32 [8, 512], P('dp'), may hold values from 0 to 3, never falling along the last dimension, each value on 1 to 386 neighbouring positions
- enc_segments: int32 [8, 512], P('dp'), may hold values from 0 to 3, never falling along the last dimension, each value on 1 to 386 neighbouring positions
- offset_buckets: int32 [512], replicated, may hold values from 0 to 31
- norm_gains: float32 [3, 768], replicated, may hold values from 0.5 to 1.5
- bias_table: float32 [32, 12], P(None, 'mp'), may hold values from -6 to 6
- self_query: bfloat16 [768, 768], P(None, 'mp'), may hold values from -0.21875 to 0.21875
- self_key: bfloat16 [768, 768], P(None, 'mp'), may hold values from -0.21875 to 0.21875
- self_value: bfloat16 [768, 768], P(None, 'mp'), may hold values from -0.21875 to 0.21875
- self_out: bfloat16 [768, 768], P(None, 'mp'), may hold values from -1.25 to 1.25
- cross_query: bfloat16 [768, 768], P(None, 'mp'), may hold values from -0.21875 to 0.21875
- cross_key: bfloat16 [768, 768], P(None, 'mp'), may hold values from -0.21875 to 0.21875
- cross_value: bfloat16 [768, 768], P(None, 'mp'), may hold values from -0.21875 to 0.21875
- cross_out: bfloat16 [768, 768], P(None, 'mp'), may hold values from -1.25 to 1.25
- ffn_up: bfloat16 [768, 3072], P(None, 'mp'), may hold values from -0.21875 to 0.21875
- ffn_down: bfloat16 [768, 3072], P(None, 'mp'), may hold values from -0.15625 to 0.15625
- out_grad: bfloat16 [8, 512, 768], P('dp', 'mp'), may hold values from -8 to 8
Outputs:
- output: bfloat16 [8, 512, 768], P('dp', 'mp')
- grad_decoder: bfloat16 [8, 512, 768], P('dp', 'mp')
- grad_encoder: bfloat16 [8, 512, 768], P('dp', 'mp')
- grad_self_query: float32 [768, 768], P('dp', 'mp')
- grad_self_key: float32 [768, 768], P('dp', 'mp')
- grad_self_value: float32 [768, 768], P('dp', 'mp')
- grad_self_out: float32 [768, 768], P('dp', 'mp')
- grad_cross_query: float32 [768, 768], P('dp', 'mp')
- grad_cross_key: float32 [768, 768], P('dp', 'mp')
- grad_cross_value: float32 [768, 768], P('dp', 'mp')
- grad_cross_out: float32 [768, 768], P('dp', 'mp')
- grad_ffn_up: float32 [768, 3072], P('dp', 'mp')
- grad_ffn_down: float32 [768, 3072], P('dp', 'mp')
- grad_gains: float32 [3, 768], replicated
- grad_table: float32 [32, 12], replicated
The draws below stay inside these ranges and needn't reach their ends.
Inputs may be any that keep to these rules, and one draw needn't show every extreme that they name: `dec_segments`: in every row the numbers never fall, every number appears, and one document has exactly 386 positions, none more; equal numbers in dec_segments and enc_segments of a row mark one document. `enc_segments`: in every row the numbers never fall, every number appears, and one document has exactly 386 positions, none more.
All inputs are finite; a program needn't handle non-finite values.
Results may differ from the reference program's by a relative error of at most 0.023.
Values may be sent and summed in bfloat16 or wider, within the bound.
No kernel may reach another device: no remote copies, remote signals or barrier semaphores. Data moves between devices by JAX's collectives and lax.ppermute only.
A program may use at most 128 MiB of HBM per device.

```python
import math
import jax
import jax.numpy as jnp
import numpy as np
from jax import lax

D = 768
HEADS = 12
HEAD_DIM = 64
FF = 3072
NB = 32
LD = 512
LE = 512
DOCS = 4
ROWS = 8
LONGEST = 386
LONGEST_ENC = 386


def plant(values, own_key, smallest, top_value):
    index_at = [jax.random.randint(jax.random.fold_in(own_key, axis), (), 0, length) for axis, length in enumerate(values.shape)]
    widest = values.shape.index(max(values.shape))
    next_to = index_at[:widest] + [(index_at[widest] + 1) % values.shape[widest]] + index_at[widest + 1:]
    return values.at[tuple(index_at)].set(smallest).at[tuple(next_to)].set(top_value)


def raised(values, rng, source, target, parts, factor):
    owner, partner = [(jnp.arange(values.shape[axis_at]) // (values.shape[axis_at] // parts)).reshape([-1 if axis == axis_at else 1 for axis in range(values.ndim)]) for axis_at in (source, target)]
    chosen = jax.random.permutation(rng, parts)[partner]
    strong = (owner == chosen) | (owner == (partner + parts // 2) % parts)
    return jnp.where(strong, factor * values, values)


def level_of(rng, extent, split, low, high):
    loudness, own = 1.0, jax.random.fold_in(rng, 6)
    for position, shards_of in split:
        steps = jnp.exp(jax.random.uniform(jax.random.fold_in(own, position), (shards_of,), jnp.float32, low / len(split), high / len(split)))
        loudness = loudness * jnp.repeat(steps, extent[position] // shards_of).reshape([-1 if axis == position else 1 for axis in range(len(extent))])
    return loudness


def length_profile(count, total, limit, slope):
    loads = [(1 << 20) // math.isqrt(standing ** slope) + 1 for standing in range(2, count + 1)]
    spare, holding = total - limit - (count - 1), [1] * (count - 1)
    while spare > 0:
        movable = [i for i in range(count - 1) if holding[i] < limit]
        pool, remaining = sum([loads[i] for i in movable]), spare
        for i in movable:
            extra = min(limit - holding[i], max(1, remaining * loads[i] // pool), spare)
            holding[i] = holding[i] + extra
            spare = spare - extra
    return np.array([limit] + holding)


def uneven_parts(rng, count, total, bound, slope):
    if count == 2:
        one = jax.random.randint(rng, (), max(1, total - bound), min(bound, total - 1) + 1)
        return jnp.stack([one, total - one])
    sizes = jnp.asarray(length_profile(count, total, bound, slope), jnp.int32)
    twos = (count - 1) // 2
    giver, receiver = sizes[1:1 + 2 * twos:2], sizes[2:2 + 2 * twos:2]
    room = jnp.minimum(giver - 1, bound - receiver)
    moved = jax.random.randint(jax.random.fold_in(rng, 1), (twos,), 0, 1 << 20) % (room + 1)
    sizes = sizes.at[1:1 + 2 * twos:2].set(giver - moved).at[2:2 + 2 * twos:2].set(receiver + moved)
    return sizes[jax.random.permutation(jax.random.fold_in(rng, 2), count)]


def noise(rng, extent, deviation, limit, split=(), held_as=jnp.bfloat16):
    drawn = deviation * jax.random.normal(rng, extent, jnp.float32)
    if split:
        drawn = drawn * level_of(rng, extent, split, -0.22, 0.18)
    return jnp.clip(drawn, -limit, limit).astype(held_as)


def heavy_noise(rng, dims, deviation, most, shards, heavy, held_as=jnp.bfloat16):
    array = deviation * jax.random.normal(rng, dims, jnp.float32)
    if shards:
        array = array * level_of(rng, dims, shards, -0.22, 0.18)
    return jnp.clip(raised(array, jax.random.fold_in(rng, 3), *heavy), -most, most).astype(held_as)


def setup_inputs(seed: int = 0) -> dict:
    arg_keys = jax.random.split(jax.random.key(seed), 19)
    decoder_in = noise(arg_keys[0], (ROWS, LD, D), 1.0, 6.0, ((0, 8), (1, 4)))
    encoder_states = noise(arg_keys[1], (ROWS, LE, D), 1.0, 6.0, ((0, 8), (1, 4)))
    dec_segments = jax.vmap(lambda own: jnp.searchsorted(jnp.cumsum(uneven_parts(own, DOCS, LD, LONGEST, 0)), jnp.arange(LD), side="right"))(jax.random.split(arg_keys[2], ROWS)).reshape((ROWS, LD)).astype(jnp.int32)
    enc_segments = jax.vmap(lambda own: jnp.searchsorted(jnp.cumsum(uneven_parts(own, DOCS, LE, LONGEST_ENC, 0)), jnp.arange(LE), side="right"))(jax.random.split(arg_keys[3], ROWS)).reshape((ROWS, LE)).astype(jnp.int32)
    offset_buckets = plant(jax.random.randint(arg_keys[4], (LD,), 0, NB), jax.random.fold_in(arg_keys[4], 1), 0, NB - 1).astype(jnp.int32)
    norm_gains = jnp.clip(1.0 + 0.1 * jax.random.normal(arg_keys[5], (3, D), jnp.float32), 0.5, 1.5)
    bias_table = noise(arg_keys[6], (NB, HEADS), 1.0, 6.0, ((1, 4),), jnp.float32)
    self_query = noise(arg_keys[7], (D, D), D ** -0.5, 0.21875, ((1, 4),))
    self_key = noise(arg_keys[8], (D, D), D ** -0.5, 0.21875, ((1, 4),))
    self_value = noise(arg_keys[9], (D, D), D ** -0.5, 0.21875, ((1, 4),))
    self_out = noise(arg_keys[10], (D, D), (D // 32) ** -0.5, 1.25, ((1, 4),))
    cross_query = noise(arg_keys[11], (D, D), D ** -0.5, 0.21875, ((1, 4),))
    cross_key = noise(arg_keys[12], (D, D), D ** -0.5, 0.21875, ((1, 4),))
    cross_value = noise(arg_keys[13], (D, D), D ** -0.5, 0.21875, ((1, 4),))
    cross_out = noise(arg_keys[14], (D, D), (D // 32) ** -0.5, 1.25, ((1, 4),))
    ffn_up = noise(arg_keys[15], (D, FF), D ** -0.5, 0.21875, ((1, 4),))
    ffn_down = noise(arg_keys[16], (D, FF), (FF // 2) ** -0.5, 0.15625, ((1, 4),))
    out_grad = heavy_noise(arg_keys[17], (ROWS, LD, D), 1.0, 8.0, ((0, 8), (1, 4)), (0, 2, 8, 2.0))
    return {"decoder_in": decoder_in, "encoder_states": encoder_states, "dec_segments": dec_segments, "enc_segments": enc_segments, "offset_buckets": offset_buckets, "norm_gains": norm_gains, "bias_table": bias_table, "self_query": self_query, "self_key": self_key, "self_value": self_value, "self_out": self_out, "cross_query": cross_query, "cross_key": cross_key, "cross_value": cross_value, "cross_out": cross_out, "ffn_up": ffn_up, "ffn_down": ffn_down, "out_grad": out_grad}


epsilon = 1e-06
key_scale = 0.125
masked_score = -1e+30
highest = lax.Precision.HIGHEST

@jax.custom_vjp
def low(v):
    return lax.optimization_barrier(v.astype(jnp.bfloat16)).astype(jnp.float32)

@jax.custom_vjp
def low_back(v):
    return v

def low_keep(v):
    return (low(v), None)

def low_pass(kept, grad):
    return (grad,)

def back_keep(v):
    return (v, None)

def back_low(kept, grad):
    return (low(grad),)
low.defvjp(low_keep, low_pass)
low_back.defvjp(back_keep, back_low)

def rms_scaled(values_in, gain_row):
    return values_in * lax.rsqrt(lax.optimization_barrier(jnp.mean(values_in * values_in, axis=-1, keepdims=True)) + epsilon) * gain_row

def to_heads(values_in, weight):
    return jnp.einsum('rtd,dh->rth', values_in, weight, precision=highest)

def from_heads(values_in, weight):
    return jnp.einsum('rth,dh->rtd', values_in, weight, precision=highest)

def split_heads(values_in):
    return values_in.reshape(values_in.shape[0], values_in.shape[1] // HEAD_DIM, HEAD_DIM)

def both_round(values_in):
    return low_back(low(values_in))

def attend_row(query_row, key_row, value_row, allowed, extra_bias):
    scores = jnp.einsum('qhd,khd->hqk', split_heads(query_row), split_heads(key_row), precision=highest) * key_scale + extra_bias
    scores = low_back(scores)
    scores = jnp.where(allowed[None], scores, masked_score)
    soft_weights = jax.nn.softmax(scores, axis=-1)
    mixed_row = jnp.einsum('hqk,khd->qhd', low(soft_weights), split_heads(value_row), precision=highest)
    return mixed_row.reshape(query_row.shape)

def reference(decoder_in, encoder_states, dec_segments, enc_segments, offset_buckets, norm_gains, bias_table, self_query, self_key, self_value, self_out, cross_query, cross_key, cross_value, cross_out, ffn_up, ffn_down, out_grad):
    length = dec_segments.shape[1]
    places = jnp.arange(length)
    distance = jnp.clip(places[:, None] - places[None, :], 0, length - 1)
    ordered = places[:, None] >= places[None, :]

    def layer(stream_in, encoder_f, gains_f, table_f, self_query_f, self_key_f, self_value_f, self_out_f, cross_query_f, cross_key_f, cross_value_f, cross_out_f, ffn_up_f, ffn_down_f):
        near_bias = jnp.transpose(table_f[offset_buckets][distance], (2, 0, 1))
        normed_one = low(rms_scaled(stream_in, gains_f[0]))
        query_one = both_round(to_heads(normed_one, self_query_f))
        key_one = both_round(to_heads(normed_one, self_key_f))
        value_one = both_round(to_heads(normed_one, self_value_f))

        def self_row(row_items):
            query_row, key_row, value_row, seg_row = row_items
            allowed = (seg_row[:, None] == seg_row[None, :]) & ordered
            return attend_row(query_row, key_row, value_row, allowed, near_bias)
        mixed_one = both_round(lax.map(jax.checkpoint(self_row), (query_one, key_one, value_one, dec_segments)))
        stream_mid = stream_in + low_back(from_heads(mixed_one, self_out_f))
        normed_two = low(rms_scaled(stream_mid, gains_f[1]))
        query_two = both_round(to_heads(normed_two, cross_query_f))
        key_two = both_round(to_heads(encoder_f, cross_key_f))
        value_two = both_round(to_heads(encoder_f, cross_value_f))

        def cross_row(row_items):
            query_row, key_row, value_row, seg_row, enc_row = row_items
            allowed = seg_row[:, None] == enc_row[None, :]
            return attend_row(query_row, key_row, value_row, allowed, 0.0)
        mixed_two = both_round(lax.map(jax.checkpoint(cross_row), (query_two, key_two, value_two, dec_segments, enc_segments)))
        stream_end = stream_mid + low_back(from_heads(mixed_two, cross_out_f))
        normed_three = low(rms_scaled(stream_end, gains_f[2]))
        hidden_pre = low_back(to_heads(normed_three, ffn_up_f))
        hidden_act = low(jax.nn.gelu(hidden_pre, approximate=True))
        return stream_end + low_back(from_heads(hidden_act, ffn_down_f))
    primals = (decoder_in.astype(jnp.float32), encoder_states.astype(jnp.float32), norm_gains, bias_table, self_query.astype(jnp.float32), self_key.astype(jnp.float32), self_value.astype(jnp.float32), self_out.astype(jnp.float32), cross_query.astype(jnp.float32), cross_key.astype(jnp.float32), cross_value.astype(jnp.float32), cross_out.astype(jnp.float32), ffn_up.astype(jnp.float32), ffn_down.astype(jnp.float32))
    result, pullback = jax.vjp(layer, *primals)
    grads = pullback(out_grad.astype(jnp.float32))
    return (result.astype(jnp.bfloat16), grads[0].astype(jnp.bfloat16), grads[1].astype(jnp.bfloat16), grads[4], grads[5], grads[6], grads[7], grads[8], grads[9], grads[10], grads[11], grads[12], grads[13], grads[2], grads[3])
```

```python
import functools

import jax
import jax.numpy as jnp
from jax import lax
from jax.experimental import pallas as pl
from jax.experimental.pallas import tpu as pltpu
from jax.sharding import PartitionSpec as P

HEAD_DIM = 64
epsilon = 1e-06
key_scale = 0.125
masked_score = -1e30
highest = lax.Precision.HIGHEST
bf16 = jnp.bfloat16
f32 = jnp.float32


def dot(a, b):
    return lax.dot_general(a, b, (((1,), (0,)), ((), ())), preferred_element_type=f32)


def dot_nt(a, b):
    return lax.dot_general(a, b, (((1,), (1,)), ((), ())), preferred_element_type=f32)


def dot_tn(a, b):
    return lax.dot_general(a, b, (((0,), (0,)), ((), ())), preferred_element_type=f32)


def norm_parts(rows):
    inv = lax.rsqrt(jnp.mean(rows * rows, axis=-1, keepdims=True) + epsilon)
    return rows * inv, inv


def norm_back(rows, gain, grad):
    unit, inv = norm_parts(rows)
    grad_unit = grad * gain
    grad_rows = inv * (grad_unit - unit * jnp.mean(grad_unit * unit, axis=-1, keepdims=True))
    return grad_rows, jnp.sum(grad * unit, axis=0, keepdims=True)


def at(index, size):
    return pl.ds(pl.multiple_of(index * size, size), size)


def kernel_call(body, name, outs, *args, scratch=(), limit=40):
    specs = [pl.BlockSpec(memory_space=pltpu.SMEM)]
    specs += [pl.BlockSpec(memory_space=pltpu.VMEM)] * (len(args) - 1)
    moved = sum(v.size * v.dtype.itemsize for v in args)
    moved += sum(v.size * v.dtype.itemsize for v in outs)
    return pl.pallas_call(
        body,
        out_shape=outs,
        in_specs=specs,
        out_specs=[pl.BlockSpec(memory_space=pltpu.VMEM)] * len(outs),
        scratch_shapes=list(scratch),
        compiler_params=pltpu.CompilerParams(vmem_limit_bytes=limit * 1024 * 1024),
        cost_estimate=pl.CostEstimate(flops=moved * 400, bytes_accessed=moved, transcendentals=0),
        name=name,
    )(*args)


def shape(dims, dtype=bf16):
    return jax.ShapeDtypeStruct(dims, dtype)


def head_masks(width, dtype):
    lane = lax.broadcasted_iota(jnp.int32, (1, width), 1) // HEAD_DIM
    return [(lane == h).astype(f32).astype(dtype) for h in range(width // HEAD_DIM)]


def bias_body(idx, u_ref, segc_ref, segr_ref, enc_ref, bias_ref, cross_ref, *, Q):
    core = idx[1]
    L = 4 * Q
    heads = bias_ref.shape[0]
    order = (core, 2 + core, 1 - core, 3 - core)
    enc = jnp.concatenate([enc_ref[:, at(o, Q)] for o in order], axis=1)
    for b in range(2):
        own = at(2 * b + core, Q)
        segc = segc_ref[own, :]
        rows = pl.ds(b * Q, Q)
        cross_ref[rows, :] = jnp.where(segc == enc, 0.0, masked_score)
        place = (2 * b + core) * Q + lax.broadcasted_iota(jnp.int32, (Q, L), 0)
        col = lax.broadcasted_iota(jnp.int32, (Q, L), 1)
        allowed = (segc == segr_ref[...]) & (col <= place)
        turned = pltpu.roll(u_ref[...], (2 * b + core) * Q, 1)
        for h in range(heads):
            line = jnp.broadcast_to(turned[h : h + 1, :], (Q, L))
            line = pltpu.roll(line, 0, 1, stride=1, stride_axis=0)
            bias_ref[h, rows, :] = jnp.where(allowed, line, masked_score)


def soft_mix(q, k, v, extra, masks, masks_f, p_ref, first, rows, nk):
    mixed = None
    for h in range(len(masks)):
        s = dot_nt(q * masks[h], k) * key_scale + extra(h)
        top = jnp.max(s, axis=-1, keepdims=True)
        e = jnp.exp(s - top)
        p = (e * (1.0 / jnp.sum(e, axis=-1, keepdims=True))).astype(bf16)
        p_ref[first + h, rows, pl.ds(0, nk)] = p
        term = dot(p, v) * masks_f[h]
        mixed = term if mixed is None else mixed + term
    return mixed.astype(bf16)


def self_forward(idx, x_ref, g_ref, wo_ref, wp_ref, bias_ref, part_ref, h_ref, q_ref, k_ref, v_ref, p_ref, o_ref, *, Q):
    core = idx[1]
    L = 4 * Q
    W = wo_ref.shape[2]
    heads = W // HEAD_DIM
    masks, masks_f = head_masks(W, bf16), head_masks(W, f32)
    gain = g_ref[0:1, :]
    for t in range(4):
        rows = pl.ds(t * Q, Q)
        unit, _ = norm_parts(x_ref[rows, :].astype(f32))
        h_ref[rows, :] = (unit * gain).astype(bf16)
    ws = (wo_ref, wp_ref)
    for grp in range(2):
        k_ref[grp] = dot(h_ref[...], ws[grp][1]).astype(bf16)
        v_ref[grp] = dot(h_ref[...], ws[grp][2]).astype(bf16)
    for b in range(2):
        hb = h_ref[at(2 * b + core, Q), :]
        nk = 2 * Q * (b + 1)
        rows = pl.ds(b * Q, Q)
        part = None
        for grp in range(2):
            q = dot(hb, ws[grp][0]).astype(bf16)
            q_ref[grp, rows, :] = q
            mixed = soft_mix(
                q,
                k_ref[grp, pl.ds(0, nk), :],
                v_ref[grp, pl.ds(0, nk), :],
                lambda h: bias_ref[grp * heads + h, rows, pl.ds(0, nk)],
                masks,
                masks_f,
                p_ref,
                grp * heads,
                rows,
                nk,
            )
            o_ref[grp, rows, :] = mixed
            term = dot_nt(mixed, ws[grp][3])
            part = term if part is None else part + term
        part_ref[rows, :] = part.astype(bf16)
    for i in range(2 * heads):
        p_ref[i, pl.ds(0, Q), pl.ds(2 * Q, 2 * Q)] = jnp.zeros((Q, 2 * Q), bf16)


def encoder_keys(idx, eo_ref, ep_ref, wo_ref, wp_ref, k_ref, v_ref, *, Q):
    for grp, w in enumerate((wo_ref, wp_ref)):
        for half, e in enumerate((eo_ref, ep_ref)):
            rows = pl.ds(half * 2 * Q, 2 * Q)
            k_ref[grp, rows, :] = dot(e[...], w[1]).astype(bf16)
            v_ref[grp, rows, :] = dot(e[...], w[2]).astype(bf16)


def cross_forward(idx, x_ref, part_ref, recv_ref, g_ref, wo_ref, wp_ref, k_ref, v_ref, mask_ref, out_ref, x1_ref, h_ref, q_ref, p_ref, o_ref, *, Q):
    core = idx[1]
    W = wo_ref.shape[2]
    heads = W // HEAD_DIM
    masks, masks_f = head_masks(W, bf16), head_masks(W, f32)
    ws = (wo_ref, wp_ref)
    for b in range(2):
        rows = pl.ds(b * Q, Q)
        x1 = x_ref[at(2 * b + core, Q), :].astype(f32) + (
            part_ref[rows, :].astype(f32) + recv_ref[rows, :].astype(f32)
        )
        x1_ref[rows, :] = x1
        unit, _ = norm_parts(x1)
        hb = (unit * g_ref[1:2, :]).astype(bf16)
        h_ref[rows, :] = hb
        part = None
        for grp in range(2):
            q = dot(hb, ws[grp][0]).astype(bf16)
            q_ref[grp, rows, :] = q
            mixed = soft_mix(
                q, k_ref[grp], v_ref[grp], lambda h: mask_ref[rows, :], masks, masks_f, p_ref, grp * heads, rows, 4 * Q
            )
            o_ref[grp, rows, :] = mixed
            term = dot_nt(mixed, ws[grp][3])
            part = term if part is None else part + term
        out_ref[rows, :] = part.astype(bf16)


gelu_c = 0.7978845608028654
gelu_k = 0.044715


def ffn_both(idx, x1_ref, part_ref, recv_ref, g_ref, uo_ref, up_ref, do_ref, dp_ref, gr_ref, out_ref, x2_ref, a_ref, du_ref, send_ref, *, Q):
    for b in range(2):
        rows = pl.ds(b * Q, Q)
        x2 = x1_ref[rows, :] + (part_ref[rows, :].astype(f32) + recv_ref[rows, :].astype(f32))
        x2_ref[rows, :] = x2
        unit, _ = norm_parts(x2)
        send_ref[0, rows, :] = (unit * g_ref[2:3, :]).astype(bf16)
    for grp, (up, down) in enumerate(((uo_ref, do_ref), (up_ref, dp_ref))):
        u = dot(send_ref[0], up[...])
        t = jnp.tanh(gelu_c * (u + gelu_k * (u * u * u)))
        half = 0.5 * (1.0 + t)
        a = (u * half).astype(bf16)
        slope = half + 0.5 * u * (1.0 - t * t) * (gelu_c * (1.0 + 3.0 * gelu_k * (u * u)))
        du = (dot(gr_ref[...], down[...]) * slope).astype(bf16)
        if grp == 0:
            a_ref[...] = a
            du_ref[...] = du
        else:
            send_ref[1] = a
            send_ref[2] = du
    out_ref[...] = (dot_nt(du_ref[...], uo_ref[...]) + dot_nt(send_ref[2], up_ref[...])).astype(bf16)


def ffn_out(idx, a_ref, send_ref, do_ref, dp_ref, keep_ref, out_ref, sum_ref, *, Q):
    y = idx[0]
    sum_ref[...] = dot_nt(a_ref[...], do_ref[...]) + dot_nt(send_ref[1], dp_ref[...])
    keep_ref[...] = sum_ref[at(y, Q), :]
    out_ref[...] = sum_ref[at(1 - y, Q), :].astype(bf16)


def output_body(idx, x2_ref, keep_ref, recv_ref, out_ref, *, Q):
    out_ref[...] = (x2_ref[at(idx[0], Q), :] + (keep_ref[...] + recv_ref[...].astype(f32))).astype(bf16)


def attend_back(q, k, v, go, p_ref, ds_ref, first, rows, nk, masks, masks_f):
    grad_q = None
    for h in range(len(masks)):
        p = p_ref[first + h, rows, pl.ds(0, nk)].astype(f32)
        gp = dot_nt(go * masks[h], v)
        ds = (p * (gp - jnp.sum(p * gp, axis=-1, keepdims=True))).astype(bf16)
        ds_ref[first + h, rows, pl.ds(0, nk)] = ds
        term = dot(ds, k) * masks_f[h]
        grad_q = term if grad_q is None else grad_q + term
    return (grad_q * key_scale).astype(bf16)


def cross_back(idx, gr_ref, part_ref, recv_ref, x2_ref, g_ref, wo_ref, wp_ref, k_ref, v_ref, p_ref, h2_ref, out_ref, dx_ref, sendh_ref, do_ref, ds_ref, dqo_ref, dqp_ref, gain_ref, *, Q):
    W = wo_ref.shape[2]
    heads = W // HEAD_DIM
    masks, masks_f = head_masks(W, bf16), head_masks(W, f32)
    ws = (wo_ref, wp_ref)
    sendh_ref[1] = h2_ref[...]
    total = None
    for b in range(2):
        rows = pl.ds(b * Q, Q)
        dh = part_ref[rows, :].astype(f32) + recv_ref[rows, :].astype(f32)
        grad_rows, grad_gain = norm_back(x2_ref[rows, :], g_ref[2:3, :], dh)
        dx = gr_ref[rows, :].astype(f32) + grad_rows
        dx_ref[rows, :] = dx
        total = grad_gain if total is None else total + grad_gain
        gc = dx.astype(bf16)
        sendh_ref[0, rows, :] = gc
        part = None
        for grp in range(2):
            go = dot(gc, ws[grp][3]).astype(bf16)
            do_ref[grp, rows, :] = go
            dq = attend_back(
                None, k_ref[grp], v_ref[grp], go, p_ref, ds_ref, grp * heads, rows, 4 * Q, masks, masks_f
            )
            if grp == 0:
                dqo_ref[rows, :] = dq
            else:
                dqp_ref[rows, :] = dq
            term = dot_nt(dq, ws[grp][0])
            part = term if part is None else part + term
        out_ref[rows, :] = part.astype(bf16)
    gain_ref[...] = jnp.broadcast_to(total * 0.5, gain_ref.shape)


def key_grads(ds_ref, p_ref, q_ref, do_ref, grp, heads, masks):
    first = grp * heads
    n, m = ds_ref.shape[1:]
    q, go = q_ref[grp], do_ref[grp]
    qs = jnp.concatenate([q * masks[h] for h in range(heads)], axis=0)
    gs = jnp.concatenate([go * masks[h] for h in range(heads)], axis=0)
    ds = ds_ref[first : first + heads].reshape(heads * n, m)
    p = p_ref[first : first + heads].reshape(heads * n, m)
    return dot_tn(ds, qs) * key_scale, dot_tn(p, gs)


def keys_body(idx, ds_ref, p_ref, q_ref, do_ref, dqp_ref, o_ref, dk_ref, dv_ref, send_ref, *, Q):
    W = q_ref.shape[2]
    heads = W // HEAD_DIM
    masks = head_masks(W, bf16)
    dk, dv = key_grads(ds_ref, p_ref, q_ref, do_ref, 0, heads, masks)
    dk_ref[...] = dk
    dv_ref[...] = dv
    dk, dv = key_grads(ds_ref, p_ref, q_ref, do_ref, 1, heads, masks)
    send_ref[pl.ds(0, 2 * Q), :] = dqp_ref[...]
    send_ref[pl.ds(2 * Q, 4 * Q), :] = dk.astype(bf16)
    send_ref[pl.ds(6 * Q, 4 * Q), :] = dv.astype(bf16)
    send_ref[pl.ds(10 * Q, 2 * Q), :] = o_ref[1]


def self_back(idx, dx_ref, part_ref, recv_ref, x1_ref, g_ref, wo_ref, wp_ref, k_ref, v_ref, p_ref, q_ref, o_ref, dx1_ref, gs_ref, dqo_ref, dk_ref, dv_ref, send_ref, gain_ref, dist_ref, ds_ref, do_ref, *, Q):
    core = idx[1]
    L = 4 * Q
    W = wo_ref.shape[2]
    heads = W // HEAD_DIM
    masks, masks_f = head_masks(W, bf16), head_masks(W, f32)
    ws = (wo_ref, wp_ref)
    total = None
    for i in range(2 * heads):
        ds_ref[i, pl.ds(0, Q), pl.ds(2 * Q, 2 * Q)] = jnp.zeros((Q, 2 * Q), bf16)
    for b in range(2):
        rows = pl.ds(b * Q, Q)
        nk = 2 * Q * (b + 1)
        dh = part_ref[rows, :].astype(f32) + recv_ref[rows, :].astype(f32)
        grad_rows, grad_gain = norm_back(x1_ref[rows, :], g_ref[1:2, :], dh)
        dx = dx_ref[rows, :] + grad_rows
        dx1_ref[rows, :] = dx
        total = grad_gain if total is None else total + grad_gain
        gs = dx.astype(bf16)
        gs_ref[rows, :] = gs
        for grp in range(2):
            go = dot(gs, ws[grp][3]).astype(bf16)
            do_ref[grp, rows, :] = go
            dq = attend_back(
                None,
                k_ref[grp, pl.ds(0, nk), :],
                v_ref[grp, pl.ds(0, nk), :],
                go,
                p_ref,
                ds_ref,
                grp * heads,
                rows,
                nk,
                masks,
                masks_f,
            )
            if grp == 0:
                dqo_ref[rows, :] = dq
            else:
                send_ref[rows, :] = dq
    gain_ref[...] = jnp.broadcast_to(total * 0.5, gain_ref.shape)
    dk, dv = key_grads(ds_ref, p_ref, q_ref, do_ref, 0, heads, masks)
    dk_ref[...] = dk
    dv_ref[...] = dv
    dk, dv = key_grads(ds_ref, p_ref, q_ref, do_ref, 1, heads, masks)
    send_ref[pl.ds(2 * Q, 4 * Q), :] = dk.astype(bf16)
    send_ref[pl.ds(6 * Q, 4 * Q), :] = dv.astype(bf16)
    send_ref[pl.ds(10 * Q, 2 * Q), :] = o_ref[1]
    for h in range(2 * heads):
        line = ds_ref[h, pl.ds(0, Q), :].astype(f32) + pltpu.roll(
            ds_ref[h, pl.ds(Q, Q), :].astype(f32), L - 2 * Q, 1
        )
        n = Q // 2
        while n >= 1:
            line = line[:n] + pltpu.roll(line[n : 2 * n], L - n, 1)
            n //= 2
        dist_ref[h : h + 1, :] = line
    dist_ref[2 * heads :, :] = jnp.zeros((dist_ref.shape[0] - 2 * heads, L), f32)
    dist_ref[...] = pltpu.roll(dist_ref[...], (4 - core) * Q, 1)


def self_weights(idx, h_ref, gs_ref, gsr_ref, o_ref, dqo_ref, dk_ref, dv_ref, recv_ref, w_ref, g_ref, *rest, Q, split):
    core = idx[1]
    if split:
        keep_ref, send_ref, dq_ref, dkf_ref, dvf_ref, gain_ref, sum_ref, d_ref = rest
    else:
        sum_ref, dq_ref, dkf_ref, dvf_ref, gain_ref, d_ref = rest
    W = dqo_ref.shape[1]
    for b in range(2):
        rows = pl.ds(b * Q, Q)
        dq_ref[at(2 * b + core, Q), :] = dqo_ref[rows, :]
        dq_ref[at(2 * b + 1 - core, Q), :] = recv_ref[rows, :]
    dkf_ref[...] = (dk_ref[...] + recv_ref[pl.ds(2 * Q, 4 * Q), :].astype(f32)).astype(bf16)
    dvf_ref[...] = (dv_ref[...] + recv_ref[pl.ds(6 * Q, 4 * Q), :].astype(f32)).astype(bf16)
    d_ref[:, 0:W] = dq_ref[...]
    d_ref[:, W : 2 * W] = dkf_ref[...]
    d_ref[:, 2 * W : 3 * W] = dvf_ref[...]
    sum_ref[:, 0 : 3 * W] = dot_tn(h_ref[...], d_ref[...])
    sum_ref[:, 3 * W : 4 * W] = dot_tn(gs_ref[...], o_ref[0]) + dot_tn(gsr_ref[...], recv_ref[pl.ds(10 * Q, 2 * Q), :])
    prod = None
    for i in range(3):
        term = sum_ref[:, i * W : (i + 1) * W] * w_ref[i].astype(f32)
        prod = term if prod is None else prod + term
    line = lax.dot_general(
        jnp.ones((8, W), f32), prod, (((1,), (1,)), ((), ())), precision=highest, preferred_element_type=f32
    )
    gain_ref[...] = line / g_ref[0:1, :]
    if split:
        split_rows(idx, sum_ref, keep_ref, send_ref)


def split_rows(idx, sum_ref, keep_ref, send_ref):
    x = idx[2]
    n = keep_ref.shape[1]
    for z in range(keep_ref.shape[0]):
        keep_ref[z] = sum_ref[at(2 * z + x, n), :].astype(keep_ref.dtype)
        send_ref[z] = sum_ref[at(2 * z + 1 - x, n), :].astype(send_ref.dtype)


def cross_weights(idx, sendh_ref, recvh_ref, eo_ref, ep_ref, dqo_ref, dk_ref, dv_ref, o_ref, recv_ref, *rest, Q, split):
    if split:
        keep_ref, send_ref, sum_ref = rest
    else:
        (sum_ref,) = rest
    W = dqo_ref.shape[1]
    sum_ref[:, 0:W] = dot_tn(sendh_ref[1], dqo_ref[...]) + dot_tn(recvh_ref[1], recv_ref[pl.ds(0, 2 * Q), :])
    for i, d in enumerate((dk_ref, dv_ref)):
        sum_ref[:, (i + 1) * W : (i + 2) * W] = dot_tn(eo_ref[...], d[pl.ds(0, 2 * Q), :]) + dot_tn(
            ep_ref[...], d[pl.ds(2 * Q, 2 * Q), :]
        )
    sum_ref[:, 3 * W : 4 * W] = dot_tn(sendh_ref[0], o_ref[0]) + dot_tn(recvh_ref[0], recv_ref[pl.ds(10 * Q, 2 * Q), :])
    if split:
        split_rows(idx, sum_ref, keep_ref, send_ref)


def ffn_weights(idx, lo_ref, lr_ref, ro_ref, rr_ref, *rest, Q, split, left, right):
    if split:
        keep_ref, send_ref, sum_ref = rest
    else:
        (sum_ref,) = rest
    lo = lo_ref[...] if left is None else lo_ref[left]
    lr = lr_ref[...] if left is None else lr_ref[left]
    sum_ref[...] = dot_tn(lo, ro_ref[...]) + dot_tn(lr, rr_ref[right])
    if split:
        split_rows(idx, sum_ref, keep_ref, send_ref)


def encoder_grad(idx, dk_ref, dv_ref, recv_ref, w_ref, keep_ref, send_ref, dkf_ref, dvf_ref, *, Q):
    for half, out in enumerate((keep_ref, send_ref)):
        rows = pl.ds(half * 2 * Q, 2 * Q)
        from_k, from_v = pl.ds((4 - 2 * half) * Q, 2 * Q), pl.ds((8 - 2 * half) * Q, 2 * Q)
        dkf_ref[rows, :] = (dk_ref[rows, :] + recv_ref[from_k, :].astype(f32)).astype(bf16)
        dvf_ref[rows, :] = (dv_ref[rows, :] + recv_ref[from_v, :].astype(f32)).astype(bf16)
        out[...] = (dot_nt(dkf_ref[rows, :], w_ref[1]) + dot_nt(dvf_ref[rows, :], w_ref[2])).astype(out.dtype)


def input_grad(idx, dq_ref, dk_ref, dv_ref, w_ref, keep_ref, send_ref, *, Q):
    core = idx[1]
    for b in range(2):
        rows = pl.ds(b * Q, Q)
        for out, place in ((keep_ref, 2 * b + core), (send_ref, 2 * b + 1 - core)):
            take = at(place, Q)
            total = dot_nt(dq_ref[take, :], w_ref[0]) + dot_nt(dk_ref[take, :], w_ref[1])
            out[rows, :] = (total + dot_nt(dv_ref[take, :], w_ref[2])).astype(out.dtype)


def halve_body(idx, keep_ref, recv_ref, own_ref, send_ref, *, Q):
    y = idx[0]
    mine, theirs = at(y, Q), at(1 - y, Q)
    own_ref[...] = keep_ref[mine, :] + recv_ref[mine, :].astype(f32)
    send_ref[...] = (keep_ref[theirs, :] + recv_ref[theirs, :].astype(f32)).astype(bf16)


def add_body(idx, own_ref, recv_ref, out_ref, *, Q):
    out_ref[...] = (own_ref[...] + recv_ref[...].astype(f32)).astype(out_ref.dtype)


def decoder_grad(idx, own_ref, recv_ref, x_ref, dx_ref, g_ref, out_ref, *, Q):
    y, core = idx[0], idx[1]
    dh = own_ref[...] + recv_ref[...].astype(f32)
    grad_rows, _ = norm_back(x_ref[at(2 * y + core, Q), :].astype(f32), g_ref[0:1, :], dh)
    out_ref[...] = (dx_ref[at(y, Q), :] + grad_rows).astype(bf16)


def pair_sum(idx, keep_ref, recv_ref, own_ref, *send_refs):
    z = idx[3]
    own_ref[...] = keep_ref[z].astype(f32) + recv_ref[z].astype(f32)
    for i, out in enumerate(send_refs):
        place = lax.bitwise_xor(z, i + 1)
        out[...] = (keep_ref[place].astype(f32) + recv_ref[place].astype(f32)).astype(bf16)


def last_sum(idx, own_ref, *rest):
    recvs, outs = rest[:3], rest[3:]
    total = own_ref[...]
    for r in recvs:
        total = total + r[...].astype(f32)
    width = outs[0].shape[1]
    for i, out in enumerate(outs):
        out[...] = total[:, i * width : (i + 1) * width]


def local(
    decoder_in,
    encoder_states,
    dec_segments,
    enc_segments,
    offset_buckets,
    norm_gains,
    bias_table,
    self_query,
    self_key,
    self_value,
    self_out,
    cross_query,
    cross_key,
    cross_value,
    cross_out,
    ffn_up,
    ffn_down,
    out_grad,
    dp_size,
):
    Q, D = decoder_in.shape[1:]
    L = 4 * Q
    W = self_query.shape[1]
    F = ffn_up.shape[1]
    heads = bias_table.shape[1]
    buckets = bias_table.shape[0]
    split = dp_size == 8
    mp = lax.axis_index("mp")
    dp = lax.axis_index("dp")
    y, core = mp // 2, mp % 2
    idx = jnp.stack([y, core, dp % 2, dp // 2]).astype(jnp.int32)

    def over_mp(v, flip):
        return lax.ppermute(v, "mp", [(i, i ^ flip) for i in range(4)])

    def over_dp(v, flip):
        return lax.ppermute(v, "dp", [(i, i ^ flip) for i in range(dp_size)])

    def call(body, name, outs, *args, scratch=(), limit=40, **static):
        static["Q"] = Q
        return kernel_call(
            functools.partial(body, **static), name, outs, idx, *args, scratch=scratch, limit=limit
        )

    w_self = jnp.stack([self_query, self_key, self_value, self_out])
    w_cross = jnp.stack([cross_query, cross_key, cross_value, cross_out])
    w_self_p = over_mp(w_self, 1)
    x_full = lax.all_gather(decoder_in[0], "mp", axis=0, tiled=True)
    w_cross_p = over_mp(w_cross, 1)
    up_p = over_mp(ffn_up, 1)
    down_p = over_mp(ffn_down, 1)

    def rows_of_chip(v):
        other = over_mp(v, 2)
        own = jnp.where(y == 0, jnp.concatenate([v, other]), jnp.concatenate([other, v]))
        return own, over_mp(own, 1)

    enc_own, enc_oth = rows_of_chip(encoder_states[0])
    g_own, g_oth = rows_of_chip(out_grad[0])

    turned = jnp.concatenate([offset_buckets[:1], offset_buckets[1:][::-1]])
    one_hot = (turned[:, None] == jnp.arange(buckets)[None, :]).astype(f32)
    table_p = over_mp(bias_table, 1)
    table_both = jnp.concatenate([bias_table, table_p, jnp.zeros((buckets, 8 - 2 * heads), f32)], axis=1)
    by_place = jnp.dot(table_both.T, one_hot.T, precision=highest)
    bias, cross_mask = call(
        bias_body,
        "bias",
        [shape((2 * heads, 2 * Q, L), f32), shape((2 * Q, L), f32)],
        by_place,
        dec_segments.reshape(L, 1),
        dec_segments,
        enc_segments,
    )

    grp_rows, grp_all = shape((2, 2 * Q, W)), shape((2, L, W))
    square = shape((2 * heads, 2 * Q, L))
    half = shape((2 * Q, D))
    half_f = shape((2 * Q, D), f32)
    line = shape((8, D), f32)

    part1, h1, q1, k1, v1, p1, o1 = call(
        self_forward,
        "self_forward",
        [half, shape((L, D)), grp_rows, grp_all, grp_all, square, grp_rows],
        x_full,
        norm_gains,
        w_self,
        w_self_p,
        bias,
    )
    recv1 = over_mp(part1, 2)
    k2, v2 = call(encoder_keys, "encoder_keys", [grp_all, grp_all], enc_own, enc_oth, w_cross, w_cross_p)
    part2, x1, h2, q2, p2, o2 = call(
        cross_forward,
        "cross_forward",
        [half, half_f, half, grp_rows, square, grp_rows],
        x_full,
        part1,
        recv1,
        norm_gains,
        w_cross,
        w_cross_p,
        k2,
        v2,
        cross_mask,
    )
    recv2 = over_mp(part2, 2)
    part3, x2, a_own, du_own, send3 = call(
        ffn_both,
        "ffn_both",
        [half, half_f, shape((2 * Q, F)), shape((2 * Q, F)), shape((3, 2 * Q, D))],
        x1,
        part2,
        recv2,
        norm_gains,
        ffn_up,
        up_p,
        ffn_down,
        down_p,
        g_own,
    )
    recv3 = over_mp(part3, 2)
    recv_ffn = over_mp(send3, 1)
    quarter, quarter_f = shape((Q, D)), shape((Q, D), f32)
    y_keep, y_send = call(
        ffn_out,
        "ffn_out",
        [quarter_f, quarter],
        a_own,
        send3,
        ffn_down,
        down_p,
        scratch=[pltpu.VMEM((2 * Q, D), f32)],
    )
    y_recv = over_mp(y_send, 2)
    (output,) = call(output_body, "output", [quarter], x2, y_keep, y_recv)

    def grad_kernel(body, name, cols, *args, extra=(), scratch=(), **static):
        if split:
            keep = shape((dp_size // 2, D // dp_size, cols))
            outs = [keep, keep, *extra]
            scratch = [pltpu.VMEM((D, cols), f32), *scratch]
        else:
            outs = [shape((D, cols), f32), *extra]
        res = call(body, name, outs, *args, scratch=scratch, split=split, **static)
        return (res[:2], res[2:]) if split else (res[:1], res[1:])

    def reduce_rows(parts, count):
        cols = parts[0].shape[-1]
        if not split:
            total = lax.psum_scatter(parts[0], "dp", scatter_dimension=0, tiled=True)
            return jnp.split(total, count, axis=1)
        keep, send = parts
        n = D // dp_size
        recv = over_dp(send, 1)
        own, *sends = kernel_call(
            pair_sum, "pair_sum", [shape((n, cols), f32)] + [shape((n, cols))] * 3, idx, keep, recv
        )
        recvs = [over_dp(v, 2 * (i + 1)) for i, v in enumerate(sends)]
        return kernel_call(
            last_sum, "last_sum", [shape((n, cols // count), f32)] * count, idx, own, *recvs
        )

    down_parts, _ = grad_kernel(ffn_weights, "down_weights", F, g_own, g_oth, a_own, recv_ffn, left=None, right=1)
    up_parts, _ = grad_kernel(ffn_weights, "up_weights", F, send3, recv_ffn, du_own, recv_ffn, left=0, right=2)
    (grad_down,) = reduce_rows(down_parts, 1)
    (grad_up,) = reduce_rows(up_parts, 1)

    own_cols = shape((2 * Q, W))
    all_f, all_low = shape((L, W), f32), shape((L, W))
    packed = shape((12 * Q, W))
    part4, dx2, send4, do2, ds2, dq2, dq2_p, gain3 = call(
        cross_back,
        "cross_back",
        [half, half_f, shape((2, 2 * Q, D)), grp_rows, square, own_cols, own_cols, line],
        g_own,
        part3,
        recv3,
        x2,
        norm_gains,
        w_cross,
        w_cross_p,
        k2,
        v2,
        p2,
        h2,
    )
    recv4 = over_mp(part4, 2)
    recv_h = over_mp(send4, 1)
    dk2, dv2, send_k = call(keys_body, "cross_keys", [all_f, all_f, packed], ds2, p2, q2, do2, dq2_p, o2)
    recv_k = over_mp(send_k, 1)
    enc_keep, enc_send, dk2_full, dv2_full = call(
        encoder_grad, "encoder_grad", [half_f, half, all_low, all_low], dk2, dv2, recv_k, w_cross
    )
    enc_recv = over_mp(enc_send, 1)
    cross_parts, _ = grad_kernel(
        cross_weights, "cross_weights", 4 * W, send4, recv_h, enc_own, enc_oth, dq2, dk2_full, dv2_full, o2, recv_k
    )
    grad_cq, grad_ck, grad_cv, grad_co = reduce_rows(cross_parts, 4)
    enc_mine, enc_theirs = call(halve_body, "encoder_halve", [quarter_f, quarter], enc_keep, enc_recv)
    enc_last = over_mp(enc_theirs, 2)
    (grad_encoder,) = call(add_body, "encoder_add", [quarter], enc_mine, enc_last)

    dx1, gs, dq1, dk1, dv1, send_s, gain2, dist = call(
        self_back,
        "self_back",
        [half_f, half, own_cols, all_f, all_f, packed, line, shape((8, L), f32)],
        dx2,
        part4,
        recv4,
        x1,
        norm_gains,
        w_self,
        w_self_p,
        k1,
        v1,
        p1,
        q1,
        o1,
        scratch=[pltpu.VMEM((2 * heads, 2 * Q, L), bf16), pltpu.VMEM((2, 2 * Q, W), bf16)],
    )
    recv_s = over_mp(send_s, 1)
    gs_oth = over_mp(gs, 1)
    self_parts, (dq1_full, dk1_full, dv1_full, gain1) = grad_kernel(
        self_weights,
        "self_weights",
        4 * W,
        h1,
        gs,
        gs_oth,
        o1,
        dq1,
        dk1,
        dv1,
        recv_s,
        w_self,
        norm_gains,
        extra=[all_low, all_low, all_low, line],
        scratch=[pltpu.VMEM((L, 3 * W), bf16)],
    )
    grad_sq, grad_sk, grad_sv, grad_so = reduce_rows(self_parts, 4)
    in_keep, in_send = call(input_grad, "input_grad", [half_f, half], dq1_full, dk1_full, dv1_full, w_self)
    in_recv = over_mp(in_send, 1)
    in_mine, in_theirs = call(halve_body, "input_halve", [quarter_f, quarter], in_keep, in_recv)
    in_last = over_mp(in_theirs, 2)
    (grad_decoder,) = call(decoder_grad, "decoder_grad", [quarter], in_mine, in_last, x_full, dx1, norm_gains)

    per_head = jnp.dot(dist, one_hot, precision=highest)
    table = jnp.zeros((4 * heads, buckets), f32)
    table = lax.dynamic_update_slice(table, per_head[:heads], (mp * heads, jnp.int32(0)))
    table = lax.dynamic_update_slice(table, per_head[heads : 2 * heads], ((mp + 1 - 2 * core) * heads, jnp.int32(0)))
    small = jnp.concatenate([gain1[0], gain2[0], gain3[0], table.reshape(-1)]).reshape(-1, 128)
    small = small + over_mp(small, 1)
    small = small + over_mp(small, 2)
    flip = 1
    while flip < dp_size:
        small = small + over_dp(small, flip)
        flip *= 2
    small = small.reshape(-1)
    gain_total = small[: 3 * D].reshape(3, D)
    table_total = small[3 * D :].reshape(4 * heads, buckets).T

    def row(v):
        return v.reshape((1,) + v.shape)

    return (
        row(output),
        row(grad_decoder),
        row(grad_encoder),
        grad_sq,
        grad_sk,
        grad_sv,
        grad_so,
        grad_cq,
        grad_ck,
        grad_cv,
        grad_co,
        grad_up,
        grad_down,
        gain_total,
        table_total,
    )


def solution(mesh):
    rows = P("dp", "mp", None)
    cols = P(None, "mp")
    grads = P("dp", "mp")
    in_specs = (rows, rows, P("dp", None), P("dp", None), P(), P(), cols) + (cols,) * 10 + (rows,)
    out_specs = (rows, rows, rows) + (grads,) * 10 + (P(), P())
    body = functools.partial(local, dp_size=mesh.shape["dp"])
    return jax.shard_map(body, mesh=mesh, in_specs=in_specs, out_specs=out_specs, check_vma=False)
```

```python
import functools

import jax
import jax.numpy as jnp
from jax import lax
from jax.experimental import pallas as pl
from jax.experimental.pallas import tpu as pltpu
from jax.sharding import PartitionSpec as P

HEAD_DIM = 64
epsilon = 1e-06
key_scale = 0.125
masked_score = -1e30
highest = lax.Precision.HIGHEST
bf16 = jnp.bfloat16
f32 = jnp.float32


def dot(a, b):
    return lax.dot_general(a, b, (((1,), (0,)), ((), ())), preferred_element_type=f32)


def dot_nt(a, b):
    return lax.dot_general(a, b, (((1,), (1,)), ((), ())), preferred_element_type=f32)


def dot_tn(a, b):
    return lax.dot_general(a, b, (((0,), (0,)), ((), ())), preferred_element_type=f32)


def norm_parts(rows):
    inv = lax.rsqrt(jnp.mean(rows * rows, axis=-1, keepdims=True) + epsilon)
    return rows * inv, inv


def norm_back(rows, gain, grad):
    unit, inv = norm_parts(rows)
    grad_unit = grad * gain
    grad_rows = inv * (grad_unit - unit * jnp.mean(grad_unit * unit, axis=-1, keepdims=True))
    return grad_rows, jnp.sum(grad * unit, axis=0, keepdims=True)


def at(index, size):
    return pl.ds(pl.multiple_of(index * size, size), size)


def shape(dims, dtype=bf16):
    return jax.ShapeDtypeStruct(dims, dtype)


class Whole:
    def __init__(self, array):
        self.arrays = [array]
        self.scratch = [(array.shape, array.dtype)]
        self.copies = 1

    def plan(self, idx, refs, scr, Q):
        return [(refs[0], scr[0])]

    def view(self, lazy, scr):
        return Late(scr[0], lazy)


class Quarters:
    def __init__(self, pieces, n, first=0):
        self.arrays = list(pieces)
        self.first = first
        d = pieces[0].shape[1]
        self.scratch = [((4 * n, d), pieces[0].dtype)]
        self.copies = 4

    def plan(self, idx, refs, scr, Q):
        y, c = idx[0], idx[1]
        places = (2 * y + c, 2 * (1 - y) + c, 2 * y + 1 - c, 2 * (1 - y) + 1 - c)
        return [(r.at[pl.ds(self.first, Q)], scr[0].at[at(p, Q)]) for r, p in zip(refs, places)]

    def view(self, lazy, scr):
        return Late(scr[0], lazy)


class Joined:
    def __init__(self, own, other, picks, count):
        self.arrays = [own, other]
        self.picks = picks
        self.rows = own.shape[0] // count
        self.scratch = [((2 * self.rows, own.shape[1]), own.dtype) for _ in picks]
        self.copies = 2 * len(picks)

    def plan(self, idx, refs, scr, Q):
        n = self.rows
        out = []
        for s, i in zip(scr, self.picks):
            for half, r in enumerate(refs):
                out.append((r.at[pl.ds(i * n, n)], s.at[pl.ds(half * n, n)]))
        return out

    def view(self, lazy, scr):
        return [Late(s, lazy[2 * i : 2 * i + 2]) for i, s in enumerate(scr)]


class Part:
    def __init__(self, array, first, rows):
        self.arrays = [array]
        self.first, self.rows = first, rows
        self.scratch = [((rows,) + array.shape[1:], array.dtype)]
        self.copies = 1

    def plan(self, idx, refs, scr, Q):
        return [(refs[0].at[pl.ds(self.first, self.rows)], scr[0])]

    def view(self, lazy, scr):
        return Late(scr[0], lazy)


class Late:
    def __init__(self, ref, copies):
        self.ref, self.copies = ref, list(copies)
        self.shape, self.dtype = ref.shape, ref.dtype

    def __getitem__(self, index):
        while self.copies:
            self.copies.pop().wait()
        return self.ref[index]


class Result:
    def __init__(self, ref, copy):
        self.ref, self.copy, self.started = ref, copy, False
        self.shape, self.dtype = ref.shape, ref.dtype

    def __getitem__(self, index):
        return self.ref[index]

    def __setitem__(self, index, value):
        self.ref[index] = value

    def flush(self):
        if not self.started:
            self.copy.start()
            self.started = True


def kernel_call(body, name, outs, *args, scratch=(), Q=128, flops=0):
    specs = [a if not hasattr(a, "dtype") else Whole(a) for a in args]
    arrays = [v for s in specs for v in s.arrays]
    in_scr = [x for s in specs for x in s.scratch]
    n_copies = sum(s.copies for s in specs)

    def whole(*refs):
        refs = list(refs)
        mp, dp = lax.axis_index("mp"), lax.axis_index("dp")
        idx_ref = (mp >> 1, mp & 1, dp & 1, dp >> 1)
        ins = [refs.pop(0) for _ in arrays]
        out_refs = [refs.pop(0) for _ in outs]
        scrs = [refs.pop(0) for _ in in_scr]
        out_scr = [refs.pop(0) for _ in outs]
        in_sem, out_sem = refs.pop(0), refs.pop(0)
        views, sem = [], 0
        for s in specs:
            mine = [ins.pop(0) for _ in s.arrays]
            scr = [scrs.pop(0) for _ in s.scratch]
            copies = []
            for src, dst in s.plan(idx_ref, mine, scr, Q):
                copy = pltpu.make_async_copy(src, dst, in_sem.at[sem])
                copy.start()
                sem += 1
                copies.append(copy)
            views.append((s, copies, scr))
        lates = [s.view(copies, scr) for s, copies, scr in views]
        results = [
            Result(s, pltpu.make_async_copy(s, o, out_sem.at[i]))
            for i, (s, o) in enumerate(zip(out_scr, out_refs))
        ]
        body(idx_ref, *lates, *results, *refs)
        for late in lates:
            for v in late if isinstance(late, list) else [late]:
                while v.copies:
                    v.copies.pop().wait()
        for r in results:
            r.flush()
        for r in results:
            r.copy.wait()

    moved = sum(v.size * v.dtype.itemsize for v in arrays)
    moved += sum(v.size * v.dtype.itemsize for v in outs)
    return pl.pallas_call(
        whole,
        out_shape=outs,
        in_specs=[pl.BlockSpec(memory_space=pl.ANY)] * len(arrays),
        out_specs=[pl.BlockSpec(memory_space=pl.ANY)] * len(outs),
        scratch_shapes=[pltpu.VMEM(d, t) for d, t in in_scr]
        + [pltpu.VMEM(o.shape, o.dtype) for o in outs]
        + [pltpu.SemaphoreType.DMA((n_copies,)), pltpu.SemaphoreType.DMA((len(outs),))]
        + list(scratch),
        compiler_params=pltpu.CompilerParams(vmem_limit_bytes=58 * 1024 * 1024),
        cost_estimate=pl.CostEstimate(flops=flops, bytes_accessed=moved, transcendentals=0),
        name=name,
    )(*arrays)


def pair_masks(dtype):
    lane = lax.broadcasted_iota(jnp.int32, (1, 2 * HEAD_DIM), 1) // HEAD_DIM
    return [(lane == h).astype(f32).astype(dtype) for h in range(2)]


def bucket_rows(bucket_ref, count):
    L = bucket_ref.shape[1]
    return (lax.broadcasted_iota(jnp.int32, (count, L), 0) == bucket_ref[...]).astype(f32)


def backwards(L):
    row = lax.broadcasted_iota(jnp.int32, (L, L), 0)
    col = lax.broadcasted_iota(jnp.int32, (L, L), 1)
    return ((row + col == L) | ((row == 0) & (col == 0))).astype(f32)


def exact_dot(a, b, dims):
    return lax.dot_general(a, b, (dims, ((), ())), precision=highest, preferred_element_type=f32)


def bias_body(idx, to_ref, tp_ref, bucket_ref, segr_ref, enc_ref, bias_ref, cross_ref, *, Q):
    core = idx[1]
    L = 4 * Q
    heads, buckets = to_ref.shape
    hot = exact_dot(bucket_rows(bucket_ref, buckets), backwards(L), ((1,), (0,)))
    lines = [exact_dot(t[...], hot, ((1,), (0,))) for t in (to_ref, tp_ref)]
    seg = segr_ref[...]
    columns = jnp.broadcast_to(seg.astype(f32), (Q, L)).T
    for b in range(2):
        rows = pl.ds(b * Q, Q)
        low = columns[2 * b * Q : (2 * b + 1) * Q, 0:1]
        high = columns[(2 * b + 1) * Q : (2 * b + 2) * Q, 0:1]
        segc = jnp.where(core == 0, low, high).astype(jnp.int32)
        cross_ref[rows, :] = jnp.where(segc == enc_ref[...], 0.0, masked_score)
        place = (2 * b + core) * Q + lax.broadcasted_iota(jnp.int32, (Q, L), 0)
        col = lax.broadcasted_iota(jnp.int32, (Q, L), 1)
        allowed = (segc == seg) & (col <= place)
        for grp in range(2):
            turned = pltpu.roll(lines[grp], (2 * b + core) * Q, 1)
            for h in range(heads):
                line = jnp.broadcast_to(turned[h : h + 1, :], (Q, L))
                line = pltpu.roll(line, 0, 1, stride=1, stride_axis=0)
                bias_ref[grp * heads + h, rows, :] = jnp.where(allowed, line, masked_score)


def soft_mix(q_ref, k_ref, v_ref, extra, p_ref, o_ref, rows, nk):
    low, wide = pair_masks(bf16), pair_masks(f32)
    keys = pl.ds(0, nk)
    for pair in range(p_ref.shape[0] // 2):
        lanes = pl.ds(pair * 2 * HEAD_DIM, 2 * HEAD_DIM)
        q, k, v = q_ref[rows, lanes], k_ref[keys, lanes], v_ref[keys, lanes]
        mixed = None
        for i in range(2):
            h = 2 * pair + i
            s = dot_nt(q * low[i], k) * key_scale + extra(h)
            top = jnp.max(s, axis=-1, keepdims=True)
            e = jnp.exp(s - top)
            p = (e * (1.0 / jnp.sum(e, axis=-1, keepdims=True))).astype(bf16)
            p_ref[h, rows, keys] = p
            term = dot(p, v) * wide[i]
            mixed = term if mixed is None else mixed + term
        o_ref[rows, lanes] = mixed.astype(bf16)


def self_forward(idx, x_ref, g_ref, w, bias_ref, part_ref, h_ref, q_ref, k_ref, v_ref, p_ref, o_ref, *, Q):
    core = idx[1]
    gain = g_ref[0:1, :]
    for t in range(4):
        rows = pl.ds(t * Q, Q)
        unit, _ = norm_parts(x_ref[rows, :].astype(f32))
        h_ref[rows, :] = (unit * gain).astype(bf16)
    h_ref.flush()
    k_ref[...] = dot_nt(h_ref[...], w[1][...]).astype(bf16)
    k_ref.flush()
    v_ref[...] = dot_nt(h_ref[...], w[2][...]).astype(bf16)
    v_ref.flush()
    for b in range(2):
        hb = h_ref[at(2 * b + core, Q), :]
        q_ref[pl.ds(b * Q, Q), :] = dot_nt(hb, w[0][...]).astype(bf16)
    q_ref.flush()
    for i in range(p_ref.shape[0]):
        p_ref[i, pl.ds(0, Q), pl.ds(2 * Q, 2 * Q)] = jnp.zeros((Q, 2 * Q), bf16)
    for b in range(2):
        nk = 2 * Q * (b + 1)
        rows = pl.ds(b * Q, Q)
        soft_mix(q_ref, k_ref, v_ref, lambda h: bias_ref[h, rows, pl.ds(0, nk)], p_ref, o_ref, rows, nk)
    p_ref.flush()
    o_ref.flush()
    part_ref[...] = dot(o_ref[...], w[3][...]).astype(bf16)


def encoder_keys(idx, e_ref, w, k_ref, v_ref, *, Q):
    k_ref[...] = dot_nt(e_ref[...], w[0][...]).astype(bf16)
    v_ref[...] = dot_nt(e_ref[...], w[1][...]).astype(bf16)


def cross_forward(idx, x_ref, part_ref, recv_ref, g_ref, w, k_ref, v_ref, mask_ref, out_ref, x1_ref, h_ref, q_ref, p_ref, o_ref, *, Q):
    core = idx[1]
    for b in range(2):
        rows = pl.ds(b * Q, Q)
        x1 = x_ref[at(2 * b + core, Q), :].astype(f32) + (
            part_ref[rows, :].astype(f32) + recv_ref[rows, :].astype(f32)
        )
        x1_ref[rows, :] = x1
        unit, _ = norm_parts(x1)
        h_ref[rows, :] = (unit * g_ref[1:2, :]).astype(bf16)
    x1_ref.flush()
    h_ref.flush()
    q_ref[...] = dot_nt(h_ref[...], w[0][...]).astype(bf16)
    q_ref.flush()
    for b in range(2):
        rows = pl.ds(b * Q, Q)
        soft_mix(q_ref, k_ref, v_ref, lambda h: mask_ref[rows, :], p_ref, o_ref, rows, 4 * Q)
    p_ref.flush()
    o_ref.flush()
    out_ref[...] = dot(o_ref[...], w[1][...]).astype(bf16)


gelu_c = 0.7978845608028654
gelu_k = 0.044715


def act_grads(idx, g_ref, w, out_ref, *, Q):
    n = w[0].shape[0] // 2
    core = idx[1]
    for half in range(2):
        for b in range(2):
            out_ref[half, pl.ds(b * Q, Q), :] = dot(
                g_ref[at(2 * b + core, Q), :], w[0][pl.ds(half * n, n), :]
            ).astype(bf16)


def ffn_both(idx, x1_ref, part_ref, recv_ref, g_ref, up, ga_ref, out_ref, x2_ref, a_ref, du_ref, send_ref, *, Q):
    for b in range(2):
        rows = pl.ds(b * Q, Q)
        x2 = x1_ref[rows, :] + (part_ref[rows, :].astype(f32) + recv_ref[rows, :].astype(f32))
        x2_ref[rows, :] = x2
        unit, _ = norm_parts(x2)
        send_ref[0, rows, :] = (unit * g_ref[2:3, :]).astype(bf16)
    x2_ref.flush()
    n = up[0].shape[0] // 2
    for grp in range(2):
        u = dot(send_ref[0], up[0][pl.ds(grp * n, n), :])
        t = jnp.tanh(gelu_c * (u + gelu_k * (u * u * u)))
        half = 0.5 * (1.0 + t)
        a = (u * half).astype(bf16)
        slope = half + 0.5 * u * (1.0 - t * t) * (gelu_c * (1.0 + 3.0 * gelu_k * (u * u)))
        du = (ga_ref[grp].astype(f32) * slope).astype(bf16)
        if grp == 0:
            a_ref[...] = a
            du_ref[...] = du
            a_ref.flush()
            du_ref.flush()
        else:
            send_ref[1] = a
            send_ref[2] = du
            send_ref.flush()
    out_ref[...] = (
        dot_nt(du_ref[...], up[0][pl.ds(0, n), :]) + dot_nt(send_ref[2], up[0][pl.ds(n, n), :])
    ).astype(bf16)


def ffn_out(idx, a_ref, b_ref, down, x2_ref, keep_ref, out_ref, sum_ref, *, Q):
    y = idx[0]
    n = down[0].shape[0] // 2
    sum_ref[...] = dot_nt(a_ref[...], down[0][pl.ds(0, n), :]) + dot_nt(b_ref[0], down[0][pl.ds(n, n), :])
    out_ref[...] = sum_ref[at(1 - y, Q), :].astype(bf16)
    out_ref.flush()
    keep_ref[...] = sum_ref[at(y, Q), :] + x2_ref[at(y, Q), :]


def attend_back(k_ref, v_ref, do_ref, p_ref, ds_ref, dq_ref, rows, nk):
    low, wide = pair_masks(bf16), pair_masks(f32)
    keys = pl.ds(0, nk)
    for pair in range(ds_ref.shape[0] // 2):
        lanes = pl.ds(pair * 2 * HEAD_DIM, 2 * HEAD_DIM)
        go, k, v = do_ref[rows, lanes], k_ref[keys, lanes], v_ref[keys, lanes]
        total = None
        for i in range(2):
            h = 2 * pair + i
            p = p_ref[h, rows, keys].astype(f32)
            gp = dot_nt(go * low[i], v)
            ds = (p * (gp - jnp.sum(p * gp, axis=-1, keepdims=True))).astype(bf16)
            ds_ref[h, rows, keys] = ds
            term = dot(ds, k) * wide[i]
            total = term if total is None else total + term
        dq_ref[rows, lanes] = (total * key_scale).astype(bf16)


def cross_back(idx, gr_ref, part_ref, recv_ref, x2_ref, g_ref, w, k_ref, v_ref, p_ref, h2_ref, out_ref, dx_ref, sendh_ref, do_ref, ds_ref, dq_ref, gain_ref, *, Q):
    core = idx[1]
    total = None
    for b in range(2):
        rows = pl.ds(b * Q, Q)
        dh = part_ref[rows, :].astype(f32) + recv_ref[rows, :].astype(f32)
        grad_rows, grad_gain = norm_back(x2_ref[rows, :], g_ref[2:3, :], dh)
        dx = gr_ref[at(2 * b + core, Q), :].astype(f32) + grad_rows
        dx_ref[rows, :] = dx
        total = grad_gain if total is None else total + grad_gain
        sendh_ref[0, rows, :] = dx.astype(bf16)
    dx_ref.flush()
    do_ref[...] = dot_nt(sendh_ref[0], w[1][...]).astype(bf16)
    do_ref.flush()
    for b in range(2):
        attend_back(k_ref, v_ref, do_ref, p_ref, ds_ref, dq_ref, pl.ds(b * Q, Q), 4 * Q)
    ds_ref.flush()
    dq_ref.flush()
    out_ref[...] = dot(dq_ref[...], w[0][...]).astype(bf16)
    out_ref.flush()
    sendh_ref[1] = h2_ref[...]
    gain_ref[...] = jnp.broadcast_to(total * 0.5, gain_ref.shape)


def key_grads(ds_ref, p_ref, q, go, dkt_ref, dvt_ref):
    qt = q.astype(f32).T.astype(bf16)
    gt = go.astype(f32).T.astype(bf16)
    for h in range(ds_ref.shape[0]):
        rows = pl.ds(h * HEAD_DIM, HEAD_DIM)
        take = slice(h * HEAD_DIM, (h + 1) * HEAD_DIM)
        dkt_ref[rows, :] = dot(qt[take], ds_ref[h]) * key_scale
        dvt_ref[rows, :] = dot(gt[take], p_ref[h])


def pack_keys(dkt_ref, dvt_ref, dq_ref, o_ref, dk_ref, dv_ref, send_ref, Q):
    W = dk_ref.shape[1]
    dk, dv = dkt_ref[...].T, dvt_ref[...].T
    send_ref[pl.ds(0, 4 * Q), 0:W] = dk[:, W:].astype(bf16)
    send_ref[pl.ds(0, 4 * Q), W:] = dv[:, W:].astype(bf16)
    send_ref[pl.ds(4 * Q, 2 * Q), 0:W] = dq_ref[:, W:]
    send_ref[pl.ds(4 * Q, 2 * Q), W:] = o_ref[:, W:]
    send_ref.flush()
    dk_ref[...] = dk[:, :W]
    dv_ref[...] = dv[:, :W]


def keys_body(idx, ds_ref, p_ref, q_ref, do_ref, dq_ref, o_ref, dk_ref, dv_ref, send_ref, dkt_ref, dvt_ref, *, Q):
    key_grads(ds_ref, p_ref, q_ref[...], do_ref[...], dkt_ref, dvt_ref)
    pack_keys(dkt_ref, dvt_ref, dq_ref, o_ref, dk_ref, dv_ref, send_ref, Q)


def self_back(idx, dx_ref, part_ref, recv_ref, x1_ref, g_ref, w, k_ref, v_ref, p_ref, q_ref, o_ref, gain3_ref, dx1_ref, gs_ref, dq_ref, dk_ref, dv_ref, send_ref, gain_ref, ds_ref, do_ref, dkt_ref, dvt_ref, sum_ref, *, Q):
    total = None
    for b in range(2):
        rows = pl.ds(b * Q, Q)
        dh = part_ref[rows, :].astype(f32) + recv_ref[rows, :].astype(f32)
        grad_rows, grad_gain = norm_back(x1_ref[rows, :], g_ref[1:2, :], dh)
        dx = dx_ref[rows, :] + grad_rows
        sum_ref[rows, :] = dx
        total = grad_gain if total is None else total + grad_gain
        gs_ref[rows, :] = dx.astype(bf16)
    gs_ref.flush()
    dx1_ref[...] = sum_ref[at(idx[0], Q), :]
    dx1_ref.flush()
    for i in range(ds_ref.shape[0]):
        ds_ref[i, pl.ds(0, Q), pl.ds(2 * Q, 2 * Q)] = jnp.zeros((Q, 2 * Q), bf16)
    do_ref[...] = dot_nt(gs_ref[...], w[0][...]).astype(bf16)
    for b in range(2):
        attend_back(k_ref, v_ref, do_ref, p_ref, ds_ref, dq_ref, pl.ds(b * Q, Q), 2 * Q * (b + 1))
    ds_ref.flush()
    dq_ref.flush()
    key_grads(ds_ref, p_ref, q_ref[...], do_ref[...], dkt_ref, dvt_ref)
    pack_keys(dkt_ref, dvt_ref, dq_ref, o_ref, dk_ref, dv_ref, send_ref, Q)
    gain_ref[0:1, :] = total * 0.5
    gain_ref[1:, :] = gain3_ref[1:, :]


def small_sums(idx, ds_ref, bucket_ref, gain1_ref, gain23_ref, out_ref, *, Q, buckets):
    y, core = idx[0], idx[1]
    L = 4 * Q
    heads = ds_ref.shape[0]
    lines = []
    for h in range(heads):
        line = ds_ref[h, pl.ds(0, Q), :].astype(f32) + pltpu.roll(
            ds_ref[h, pl.ds(Q, Q), :].astype(f32), L - 2 * Q, 1
        )
        n = Q // 2
        while n >= 1:
            line = line[:n] + pltpu.roll(line[n : 2 * n], L - n, 1)
            n //= 2
        lines.append(line)
    lines.append(jnp.zeros((8 - heads, L), f32))
    lines = pltpu.roll(jnp.concatenate(lines, axis=0), (4 - core) * Q, 1)
    lines = exact_dot(lines, backwards(L), ((1,), (0,)))
    sums = exact_dot(lines, bucket_rows(bucket_ref, buckets), ((1,), (1,)))
    out_ref[...] = jnp.zeros(out_ref.shape, f32)
    out_ref[0:1, :] = gain1_ref[0:1, :]
    out_ref[1:3, :] = gain23_ref[0:2, :]
    row = lax.broadcasted_iota(jnp.int32, (out_ref.shape[0], buckets), 0)
    table = out_ref[:, 0:buckets]
    for grp in range(2):
        first = (2 * y + (core if grp == 0 else 1 - core)) * (heads // 2)
        for h in range(heads // 2):
            k = grp * (heads // 2) + h
            table = jnp.where(row == first + h + 3, jnp.broadcast_to(sums[k : k + 1, :], row.shape), table)
    out_ref[:, 0:buckets] = table


def self_weights(idx, h_ref, gs_ref, gsr_ref, o_ref, dq_ref, dk_ref, dv_ref, recv_ref, *rest, Q, split):
    core = idx[1]
    if split:
        keep_ref, send_ref, d_ref, sum_ref = rest
    else:
        sum_ref, d_ref = rest
    W = dk_ref.shape[1]
    for b in range(2):
        rows = pl.ds(b * Q, Q)
        d_ref[at(2 * b + core, Q), 0:W] = dq_ref[rows, 0:W]
        d_ref[at(2 * b + 1 - core, Q), 0:W] = recv_ref[pl.ds((4 + b) * Q, Q), 0:W]
    keys = pl.ds(0, 4 * Q)
    d_ref[:, W : 2 * W] = (dk_ref[...] + recv_ref[keys, 0:W].astype(f32)).astype(bf16)
    d_ref[:, 2 * W : 3 * W] = (dv_ref[...] + recv_ref[keys, W:].astype(f32)).astype(bf16)
    d_ref.flush()
    sum_ref[:, 0 : 3 * W] = dot_tn(h_ref[...], d_ref[...])
    sum_ref[:, 3 * W : 4 * W] = dot_tn(gs_ref[...], o_ref[:, 0:W]) + dot_tn(
        gsr_ref[...], recv_ref[pl.ds(4 * Q, 2 * Q), W:]
    )
    if split:
        split_rows(idx, sum_ref, keep_ref, send_ref)


def split_rows(idx, sum_ref, keep_ref, send_ref):
    x, z = idx[2], idx[3]
    n = keep_ref.shape[1]
    for i in range(keep_ref.shape[0]):
        place = 2 * lax.bitwise_xor(z, i)
        send_ref[i] = sum_ref[at(place + 1 - x, n), :].astype(send_ref.dtype)
    send_ref.flush()
    for i in range(keep_ref.shape[0]):
        place = 2 * lax.bitwise_xor(z, i)
        keep_ref[i] = sum_ref[at(place + x, n), :].astype(keep_ref.dtype)


def cross_weights(idx, sendh_ref, recvh_ref, e_ref, dq_ref, d_ref, o_ref, recv_ref, *rest, Q, split):
    if split:
        keep_ref, send_ref, sum_ref = rest
    else:
        (sum_ref,) = rest
    W = dq_ref.shape[1] // 2
    low = pl.ds(4 * Q, 2 * Q)
    sum_ref[:, 0:W] = dot_tn(sendh_ref[1], dq_ref[:, 0:W]) + dot_tn(recvh_ref[1], recv_ref[low, 0:W])
    sum_ref[:, W : 3 * W] = dot_tn(e_ref[...], d_ref[...])
    sum_ref[:, 3 * W : 4 * W] = dot_tn(sendh_ref[0], o_ref[:, 0:W]) + dot_tn(recvh_ref[0], recv_ref[low, W:])
    if split:
        split_rows(idx, sum_ref, keep_ref, send_ref)


def down_weights(idx, g_ref, a_ref, r_ref, *rest, Q, split):
    core = idx[1]
    if split:
        keep_ref, send_ref, sum_ref, all_ref = rest
    else:
        sum_ref, all_ref = rest
    for b in range(2):
        all_ref[at(2 * b + core, Q), :] = a_ref[pl.ds(b * Q, Q), :]
        all_ref[at(2 * b + 1 - core, Q), :] = r_ref[0, pl.ds(b * Q, Q), :]
    sum_ref[...] = dot_tn(g_ref[...], all_ref[...])
    if split:
        split_rows(idx, sum_ref, keep_ref, send_ref)


def up_weights(idx, h_ref, d_ref, hr_ref, dr_ref, *rest, Q, split):
    if split:
        keep_ref, send_ref, sum_ref = rest
    else:
        (sum_ref,) = rest
    sum_ref[...] = dot_tn(h_ref[0], d_ref[...]) + dot_tn(hr_ref[0], dr_ref[0])
    if split:
        split_rows(idx, sum_ref, keep_ref, send_ref)


def shares(idx):
    y, core = idx[0], idx[1]
    return (2 * y + core, 2 * (1 - y) + core), (2 * y + 1 - core, 2 * (1 - y) + 1 - core)


def encoder_grad(idx, dk_ref, dv_ref, recv_ref, wk_ref, wv_ref, keep_ref, send_ref, d_ref, *, Q):
    W = dk_ref.shape[1]
    keys = pl.ds(0, 4 * Q)
    d_ref[:, 0:W] = (dk_ref[...] + recv_ref[keys, 0:W].astype(f32)).astype(bf16)
    d_ref[:, W:] = (dv_ref[...] + recv_ref[keys, W:].astype(f32)).astype(bf16)
    d_ref.flush()
    keep, send = shares(idx)
    for out, places in ((send_ref, send), (keep_ref, keep)):
        for i, place in enumerate(places):
            take = d_ref[at(place, Q), :]
            out[i] = (dot(take[:, :W], wk_ref[...]) + dot(take[:, W:], wv_ref[...])).astype(out.dtype)
        out.flush()


def input_grad(idx, d_ref, w_ref, h_ref, g_ref, keep_ref, send_ref, gain_ref, *, Q):
    keep, send = shares(idx)
    total = None
    for out, places in ((send_ref, send), (keep_ref, keep)):
        for i, place in enumerate(places):
            rows = at(place, Q)
            grad = dot(d_ref[rows, :], w_ref[...])
            out[i] = grad.astype(out.dtype)
            term = jnp.sum(grad * h_ref[rows, :].astype(f32), axis=0, keepdims=True)
            total = term if total is None else total + term
        out.flush()
    gain_ref[...] = jnp.broadcast_to(total / g_ref[0:1, :], gain_ref.shape)


def after(value, *others):
    return lax.optimization_barrier((value, others))[0]


def local(
    decoder_in,
    encoder_states,
    dec_segments,
    enc_segments,
    offset_buckets,
    norm_gains,
    bias_table,
    self_query,
    self_key,
    self_value,
    self_out,
    cross_query,
    cross_key,
    cross_value,
    cross_out,
    ffn_up,
    ffn_down,
    out_grad,
    dp_size,
):
    Q, D = decoder_in.shape[1:]
    L = 4 * Q
    W = self_query.shape[1]
    F = ffn_up.shape[1]
    heads = bias_table.shape[1]
    buckets = bias_table.shape[0]
    split = dp_size == 8
    mp = lax.axis_index("mp")
    y = mp // 2

    def over_mp(v, flip):
        return lax.ppermute(v, "mp", [(i, i ^ flip) for i in range(4)])

    def over_dp(v, flip):
        return lax.ppermute(v, "dp", [(i, i ^ flip) for i in range(dp_size)])

    def call(body, name, outs, *args, scratch=(), **static):
        static["Q"] = Q
        return kernel_call(functools.partial(body, **static), name, outs, *args, scratch=scratch, Q=Q)

    def quarters(v):
        across = over_mp(v, 2)
        return v, across, over_mp(v, 1), over_mp(across, 1)

    x4 = quarters(decoder_in[0])
    w_self = jnp.concatenate([self_query.T, self_key.T, self_value.T, self_out.T])
    w_self_p = over_mp(w_self, 1)
    table_p = over_mp(bias_table.T, 1)
    eg4 = quarters(jnp.concatenate([encoder_states[0], out_grad[0]]))
    w_cross = jnp.concatenate([cross_query.T, cross_key.T, cross_value.T, cross_out.T])
    w_cross_p = over_mp(w_cross, 1)
    up_p = over_mp(ffn_up, 1)
    down_p = over_mp(ffn_down, 1)

    def x_rows():
        return Quarters(x4, Q)

    def e_rows():
        return Quarters(eg4, Q)

    def g_rows():
        return Quarters(eg4, Q, Q)

    def self_w(*picks):
        return Joined(w_self, w_self_p, picks, 4)

    def cross_w(*picks):
        return Joined(w_cross, w_cross_p, picks, 4)

    up = Joined(ffn_up, up_p, (0,), 1)
    down = Joined(ffn_down, down_p, (0,), 1)

    bucket_line = offset_buckets.reshape(1, L)
    bias, cross_mask = call(
        bias_body,
        "bias",
        [shape((2 * heads, 2 * Q, L), f32), shape((2 * Q, L), f32)],
        bias_table.T,
        table_p,
        bucket_line,
        dec_segments,
        enc_segments,
    )

    both_rows, both_all = shape((2 * Q, 2 * W)), shape((L, 2 * W))
    square = shape((2 * heads, 2 * Q, L))
    half = shape((2 * Q, D))
    half_f = shape((2 * Q, D), f32)
    line = shape((8, D), f32)

    part1, h1, q1, k1, v1, p1, o1 = call(
        self_forward,
        "self_forward",
        [half, shape((L, D)), both_rows, both_all, both_all, square, both_rows],
        x_rows(),
        norm_gains,
        self_w(0, 1, 2, 3),
        bias,
    )
    recv1 = over_mp(part1, 2)
    k2, v2 = call(encoder_keys, "encoder_keys", [both_all, both_all], e_rows(), cross_w(1, 2))
    part2, x1, h2, q2, p2, o2 = call(
        cross_forward,
        "cross_forward",
        [half, half_f, half, both_rows, square, both_rows],
        x_rows(),
        part1,
        recv1,
        norm_gains,
        cross_w(0, 3),
        k2,
        v2,
        cross_mask,
    )
    recv2 = over_mp(part2, 2)
    (grad_act,) = call(act_grads, "act_grads", [shape((2, 2 * Q, F))], g_rows(), down)
    part3, x2, a_own, du_own, send3 = call(
        ffn_both,
        "ffn_both",
        [half, half_f, shape((2 * Q, F)), shape((2 * Q, F)), shape((3, 2 * Q, D))],
        x1,
        part2,
        recv2,
        norm_gains,
        up,
        grad_act,
    )
    recv3 = over_mp(part3, 2)
    recv_ffn = over_mp(send3, 1)
    quarter, quarter_f = shape((Q, D)), shape((Q, D), f32)

    def grad_kernel(body, name, cols, *args, extra=(), scratch=(), **static):
        if split:
            keep = shape((dp_size // 2, D // dp_size, cols))
            outs = [keep, keep, *extra]
            scratch = [pltpu.VMEM((D, cols), f32), *scratch]
        else:
            outs = [shape((D, cols), f32), *extra]
        res = call(body, name, outs, *args, scratch=scratch, split=split, **static)
        return (res[:2], res[2:]) if split else (res[:1], res[1:])

    def reduce_x(parts):
        if not split:
            return parts
        keep, send = parts
        recv = over_dp(send, 1)
        return [(keep[i].astype(f32) + recv[i].astype(f32)) for i in range(dp_size // 2)]

    def reduce_z(sums, count):
        if not split:
            total = lax.psum_scatter(sums[0], "dp", scatter_dimension=0, tiled=True)
        else:
            total = sums[0]
            for i in range(1, dp_size // 2):
                total = total + over_dp(sums[i].astype(bf16), 2 * i).astype(f32)
        width = total.shape[1] // count
        return [total[:, i * width : (i + 1) * width] for i in range(count)]

    down_parts, _ = grad_kernel(
        down_weights, "down_weights", F, g_rows(), a_own, Part(recv_ffn, 1, 1), scratch=[pltpu.VMEM((L, F), bf16)]
    )
    up_parts, _ = grad_kernel(
        up_weights, "up_weights", F, Part(send3, 0, 1), du_own, Part(recv_ffn, 0, 1), Part(recv_ffn, 2, 1)
    )
    y_keep, y_send = call(
        ffn_out,
        "ffn_out",
        [quarter_f, quarter],
        a_own,
        Part(send3, 1, 1),
        down,
        x2,
        scratch=[pltpu.VMEM((2 * Q, D), f32)],
    )
    output = (y_keep + over_mp(y_send, 2).astype(f32)).astype(bf16)

    own_f = shape((L, W), f32)
    packed = shape((6 * Q, 2 * W))
    turned_f = pltpu.VMEM((2 * W, L), f32)
    recv3 = after(recv3, down_parts, up_parts)
    part4, dx2, send4, do2, ds2, dq2, gain3 = call(
        cross_back,
        "cross_back",
        [half, half_f, shape((2, 2 * Q, D)), both_rows, square, both_rows, line],
        g_rows(),
        part3,
        recv3,
        x2,
        norm_gains,
        cross_w(0, 3),
        k2,
        v2,
        p2,
        h2,
    )
    recv4 = over_mp(part4, 2)
    recv_h = over_mp(send4, 1)
    dk2, dv2, send_k = call(
        keys_body, "cross_keys", [own_f, own_f, packed], ds2, p2, q2, do2, dq2, o2, scratch=[turned_f, turned_f]
    )
    recv_k = over_mp(send_k, 1)
    pair_f, pair = shape((2, Q, D), f32), shape((2, Q, D))
    enc_keep, enc_send, d2 = call(
        encoder_grad,
        "encoder_grad",
        [pair_f, pair, both_all],
        dk2,
        dv2,
        recv_k,
        Part(w_cross, W, W),
        Part(w_cross, 2 * W, W),
    )
    cross_parts, _ = grad_kernel(
        cross_weights, "cross_weights", 4 * W, send4, recv_h, e_rows(), dq2, d2, o2, recv_k
    )

    def finish_rows(keep, send):
        recv = over_mp(send, 1).astype(f32)
        across = over_mp((keep[1] + recv[1]).astype(bf16), 2)
        return keep[0] + recv[0] + across.astype(f32)

    grad_encoder = finish_rows(enc_keep, enc_send).astype(bf16)

    recv4 = after(recv4, cross_parts)
    dx1, gs, dq1, dk1, dv1, send_s, gain23, ds1 = call(
        self_back,
        "self_back",
        [quarter_f, half, both_rows, own_f, own_f, packed, line, square],
        dx2,
        part4,
        recv4,
        x1,
        norm_gains,
        self_w(3),
        k1,
        v1,
        p1,
        q1,
        o1,
        gain3,
        scratch=[pltpu.VMEM((2 * Q, 2 * W), bf16), turned_f, turned_f, pltpu.VMEM((2 * Q, D), f32)],
    )
    recv_s = over_mp(send_s, 1)
    gs_oth = over_mp(gs, 1)
    self_parts, (d1,) = grad_kernel(
        self_weights, "self_weights", 4 * W, h1, gs, gs_oth, o1, dq1, dk1, dv1, recv_s, extra=[shape((L, 3 * W))]
    )
    in_keep, in_send, gain1 = call(
        input_grad, "input_grad", [pair_f, pair, line], d1, Part(w_self, 0, 3 * W), h1, norm_gains
    )
    grad_rows, _ = norm_back(decoder_in[0].astype(f32), norm_gains[0:1], finish_rows(in_keep, in_send))
    grad_decoder = (dx1 + grad_rows).astype(bf16)

    (small,) = call(
        small_sums, "small_sums", [shape((16, D), f32)], ds1, bucket_line, gain1, gain23, buckets=buckets
    )
    small = small + over_mp(small, 1)
    small = small + over_mp(small, 2)
    flip = dp_size // 2
    while flip:
        small = small + over_dp(small, flip)
        flip //= 2
    gain_total = small[:3]
    table_total = small[3 : 3 + 4 * heads, :buckets].T

    (grad_down,) = reduce_z(reduce_x(down_parts), 1)
    (grad_up,) = reduce_z(reduce_x(up_parts), 1)
    grad_cq, grad_ck, grad_cv, grad_co = reduce_z(reduce_x(cross_parts), 4)
    grad_sq, grad_sk, grad_sv, grad_so = reduce_z(reduce_x(self_parts), 4)

    def row(v):
        return v.reshape((1,) + v.shape)

    return (
        row(output),
        row(grad_decoder),
        row(grad_encoder),
        grad_sq,
        grad_sk,
        grad_sv,
        grad_so,
        grad_cq,
        grad_ck,
        grad_cv,
        grad_co,
        grad_up,
        grad_down,
        gain_total,
        table_total,
    )


def solution(mesh):
    rows = P("dp", "mp", None)
    cols = P(None, "mp")
    grads = P("dp", "mp")
    in_specs = (rows, rows, P("dp", None), P("dp", None), P(), P(), cols) + (cols,) * 10 + (rows,)
    out_specs = (rows, rows, rows) + (grads,) * 10 + (P(), P())
    body = functools.partial(local, dp_size=mesh.shape["dp"])
    return jax.shard_map(body, mesh=mesh, in_specs=in_specs, out_specs=out_specs, check_vma=False)
```

```python
import functools

import jax
import jax.numpy as jnp
from jax import lax
from jax.experimental import pallas as pl
from jax.experimental.pallas import tpu as pltpu
from jax.sharding import PartitionSpec as P

HEAD_DIM = 64
epsilon = 1e-06
key_scale = 0.125
masked_score = -1e30
highest = lax.Precision.HIGHEST
bf16 = jnp.bfloat16
f32 = jnp.float32


def dot(a, b):
    return lax.dot_general(a, b, (((1,), (0,)), ((), ())), preferred_element_type=f32)


def dot_nt(a, b):
    return lax.dot_general(a, b, (((1,), (1,)), ((), ())), preferred_element_type=f32)


def dot_tn(a, b):
    return lax.dot_general(a, b, (((0,), (0,)), ((), ())), preferred_element_type=f32)


def norm_parts(rows):
    inv = lax.rsqrt(jnp.mean(rows * rows, axis=-1, keepdims=True) + epsilon)
    return rows * inv, inv


def norm_back(rows, gain, grad):
    unit, inv = norm_parts(rows)
    grad_unit = grad * gain
    grad_rows = inv * (grad_unit - unit * jnp.mean(grad_unit * unit, axis=-1, keepdims=True))
    return grad_rows, jnp.sum(grad * unit, axis=0, keepdims=True)


def at(index, size):
    return pl.ds(pl.multiple_of(index * size, size), size)


def shape(dims, dtype=bf16):
    return jax.ShapeDtypeStruct(dims, dtype)


class Whole:
    def __init__(self, array):
        self.arrays = [array]
        self.scratch = [(array.shape, array.dtype)]
        self.copies = 1

    def plan(self, idx, refs, scr, Q):
        return [(refs[0], scr[0])]

    def view(self, lazy, scr):
        return Late(scr[0], lazy)


class Quarters:
    def __init__(self, pieces, n, first=0):
        self.arrays = list(pieces)
        self.first = first
        d = pieces[0].shape[1]
        self.scratch = [((4 * n, d), pieces[0].dtype)]
        self.copies = 4

    def plan(self, idx, refs, scr, Q):
        y, c = idx[0], idx[1]
        places = (2 * y + c, 2 * (1 - y) + c, 2 * y + 1 - c, 2 * (1 - y) + 1 - c)
        return [(r.at[pl.ds(self.first, Q)], scr[0].at[at(p, Q)]) for r, p in zip(refs, places)]

    def view(self, lazy, scr):
        return Late(scr[0], lazy)


class Joined:
    def __init__(self, own, other, picks, count):
        self.arrays = [own, other]
        self.picks = picks
        self.rows = own.shape[0] // count
        self.scratch = [((2 * self.rows, own.shape[1]), own.dtype) for _ in picks]
        self.copies = 2 * len(picks)

    def plan(self, idx, refs, scr, Q):
        n = self.rows
        out = []
        for s, i in zip(scr, self.picks):
            for half, r in enumerate(refs):
                out.append((r.at[pl.ds(i * n, n)], s.at[pl.ds(half * n, n)]))
        return out

    def view(self, lazy, scr):
        return [Late(s, lazy[2 * i : 2 * i + 2]) for i, s in enumerate(scr)]


class Part:
    def __init__(self, array, first, rows):
        self.arrays = [array]
        self.first, self.rows = first, rows
        self.scratch = [((rows,) + array.shape[1:], array.dtype)]
        self.copies = 1

    def plan(self, idx, refs, scr, Q):
        return [(refs[0].at[pl.ds(self.first, self.rows)], scr[0])]

    def view(self, lazy, scr):
        return Late(scr[0], lazy)


class Late:
    def __init__(self, ref, copies):
        self.ref, self.copies = ref, list(copies)
        self.shape, self.dtype = ref.shape, ref.dtype

    def __getitem__(self, index):
        while self.copies:
            self.copies.pop().wait()
        return self.ref[index]


class Result:
    def __init__(self, ref, copy):
        self.ref, self.copy, self.started = ref, copy, False
        self.shape, self.dtype = ref.shape, ref.dtype

    def __getitem__(self, index):
        return self.ref[index]

    def __setitem__(self, index, value):
        self.ref[index] = value

    def flush(self):
        if not self.started:
            self.copy.start()
            self.started = True


def kernel_call(body, name, outs, *args, scratch=(), Q=128, flops=0):
    specs = [a if not hasattr(a, "dtype") else Whole(a) for a in args]
    arrays = [v for s in specs for v in s.arrays]
    in_scr = [x for s in specs for x in s.scratch]
    n_copies = sum(s.copies for s in specs)

    def whole(*refs):
        refs = list(refs)
        mp, dp = lax.axis_index("mp"), lax.axis_index("dp")
        idx_ref = (mp >> 1, mp & 1, dp & 1, dp >> 1)
        ins = [refs.pop(0) for _ in arrays]
        out_refs = [refs.pop(0) for _ in outs]
        scrs = [refs.pop(0) for _ in in_scr]
        out_scr = [refs.pop(0) for _ in outs]
        in_sem, out_sem = refs.pop(0), refs.pop(0)
        views, sem = [], 0
        for s in specs:
            mine = [ins.pop(0) for _ in s.arrays]
            scr = [scrs.pop(0) for _ in s.scratch]
            copies = []
            for src, dst in s.plan(idx_ref, mine, scr, Q):
                copy = pltpu.make_async_copy(src, dst, in_sem.at[sem])
                copy.start()
                sem += 1
                copies.append(copy)
            views.append((s, copies, scr))
        lates = [s.view(copies, scr) for s, copies, scr in views]
        results = [
            Result(s, pltpu.make_async_copy(s, o, out_sem.at[i]))
            for i, (s, o) in enumerate(zip(out_scr, out_refs))
        ]
        body(idx_ref, *lates, *results, *refs)
        for late in lates:
            for v in late if isinstance(late, list) else [late]:
                while v.copies:
                    v.copies.pop().wait()
        for r in results:
            r.flush()
        for r in results:
            r.copy.wait()

    moved = sum(v.size * v.dtype.itemsize for v in arrays)
    moved += sum(v.size * v.dtype.itemsize for v in outs)
    return pl.pallas_call(
        whole,
        out_shape=outs,
        in_specs=[pl.BlockSpec(memory_space=pl.ANY)] * len(arrays),
        out_specs=[pl.BlockSpec(memory_space=pl.ANY)] * len(outs),
        scratch_shapes=[pltpu.VMEM(d, t) for d, t in in_scr]
        + [pltpu.VMEM(o.shape, o.dtype) for o in outs]
        + [pltpu.SemaphoreType.DMA((n_copies,)), pltpu.SemaphoreType.DMA((len(outs),))]
        + list(scratch),
        compiler_params=pltpu.CompilerParams(vmem_limit_bytes=58 * 1024 * 1024),
        cost_estimate=pl.CostEstimate(flops=flops, bytes_accessed=moved, transcendentals=0),
        name=name,
    )(*arrays)


def pair_masks(dtype):
    lane = lax.broadcasted_iota(jnp.int32, (1, 2 * HEAD_DIM), 1) // HEAD_DIM
    return [(lane == h).astype(f32).astype(dtype) for h in range(2)]


def bucket_rows(bucket_ref, count):
    L = bucket_ref.shape[1]
    return (lax.broadcasted_iota(jnp.int32, (count, L), 0) == bucket_ref[...]).astype(f32)


def backwards(L):
    row = lax.broadcasted_iota(jnp.int32, (L, L), 0)
    col = lax.broadcasted_iota(jnp.int32, (L, L), 1)
    return ((row + col == L) | ((row == 0) & (col == 0))).astype(f32)


def exact_dot(a, b, dims):
    return lax.dot_general(a, b, (dims, ((), ())), precision=highest, preferred_element_type=f32)


def bias_body(idx, to_ref, tp_ref, bucket_ref, segr_ref, enc_ref, bias_ref, cross_ref, *, Q):
    core = idx[1]
    L = 4 * Q
    heads, buckets = to_ref.shape
    hot = exact_dot(bucket_rows(bucket_ref, buckets), backwards(L), ((1,), (0,)))
    lines = [exact_dot(t[...], hot, ((1,), (0,))) for t in (to_ref, tp_ref)]
    seg = segr_ref[...]
    columns = jnp.broadcast_to(seg.astype(f32), (Q, L)).T
    for b in range(2):
        rows = pl.ds(b * Q, Q)
        low = columns[2 * b * Q : (2 * b + 1) * Q, 0:1]
        high = columns[(2 * b + 1) * Q : (2 * b + 2) * Q, 0:1]
        segc = jnp.where(core == 0, low, high).astype(jnp.int32)
        cross_ref[rows, :] = jnp.where(segc == enc_ref[...], 0.0, masked_score)
        place = (2 * b + core) * Q + lax.broadcasted_iota(jnp.int32, (Q, L), 0)
        col = lax.broadcasted_iota(jnp.int32, (Q, L), 1)
        allowed = (segc == seg) & (col <= place)
        for grp in range(2):
            turned = pltpu.roll(lines[grp], (2 * b + core) * Q, 1)
            for h in range(heads):
                line = jnp.broadcast_to(turned[h : h + 1, :], (Q, L))
                line = pltpu.roll(line, 0, 1, stride=1, stride_axis=0)
                bias_ref[grp * heads + h, rows, :] = jnp.where(allowed, line, masked_score)


def soft_mix(q_ref, k_ref, v_ref, extra, p_ref, o_ref, rows, nk):
    low, wide = pair_masks(bf16), pair_masks(f32)
    keys = pl.ds(0, nk)
    for pair in range(p_ref.shape[0] // 2):
        lanes = pl.ds(pair * 2 * HEAD_DIM, 2 * HEAD_DIM)
        q, k, v = q_ref[rows, lanes], k_ref[keys, lanes], v_ref[keys, lanes]
        mixed = None
        for i in range(2):
            h = 2 * pair + i
            s = dot_nt(q * low[i], k) * key_scale + extra(h)
            top = jnp.max(s, axis=-1, keepdims=True)
            e = jnp.exp(s - top)
            p = (e * (1.0 / jnp.sum(e, axis=-1, keepdims=True))).astype(bf16)
            p_ref[h, rows, keys] = p
            term = dot(p, v) * wide[i]
            mixed = term if mixed is None else mixed + term
        o_ref[rows, lanes] = mixed.astype(bf16)


def self_forward(idx, x_ref, g_ref, w, bias_ref, part_ref, h_ref, q_ref, k_ref, v_ref, p_ref, o_ref, *, Q):
    core = idx[1]
    gain = g_ref[0:1, :]
    for t in range(4):
        rows = pl.ds(t * Q, Q)
        unit, _ = norm_parts(x_ref[rows, :].astype(f32))
        h_ref[rows, :] = (unit * gain).astype(bf16)
    h_ref.flush()
    k_ref[...] = dot_nt(h_ref[...], w[1][...]).astype(bf16)
    k_ref.flush()
    v_ref[...] = dot_nt(h_ref[...], w[2][...]).astype(bf16)
    v_ref.flush()
    for b in range(2):
        hb = h_ref[at(2 * b + core, Q), :]
        q_ref[pl.ds(b * Q, Q), :] = dot_nt(hb, w[0][...]).astype(bf16)
    q_ref.flush()
    for i in range(p_ref.shape[0]):
        p_ref[i, pl.ds(0, Q), pl.ds(2 * Q, 2 * Q)] = jnp.zeros((Q, 2 * Q), bf16)
    for b in range(2):
        nk = 2 * Q * (b + 1)
        rows = pl.ds(b * Q, Q)
        soft_mix(q_ref, k_ref, v_ref, lambda h: bias_ref[h, rows, pl.ds(0, nk)], p_ref, o_ref, rows, nk)
    p_ref.flush()
    o_ref.flush()
    part_ref[...] = dot(o_ref[...], w[3][...]).astype(bf16)


def encoder_keys(idx, e_ref, w, k_ref, v_ref, *, Q):
    k_ref[...] = dot_nt(e_ref[...], w[0][...]).astype(bf16)
    v_ref[...] = dot_nt(e_ref[...], w[1][...]).astype(bf16)


def cross_forward(idx, x_ref, part_ref, recv_ref, g_ref, w, k_ref, v_ref, mask_ref, out_ref, x1_ref, h_ref, q_ref, p_ref, o_ref, *, Q):
    core = idx[1]
    for b in range(2):
        rows = pl.ds(b * Q, Q)
        x1 = x_ref[at(2 * b + core, Q), :].astype(f32) + (
            part_ref[rows, :].astype(f32) + recv_ref[rows, :].astype(f32)
        )
        x1_ref[rows, :] = x1
        unit, _ = norm_parts(x1)
        h_ref[rows, :] = (unit * g_ref[1:2, :]).astype(bf16)
    x1_ref.flush()
    h_ref.flush()
    q_ref[...] = dot_nt(h_ref[...], w[0][...]).astype(bf16)
    q_ref.flush()
    for b in range(2):
        rows = pl.ds(b * Q, Q)
        soft_mix(q_ref, k_ref, v_ref, lambda h: mask_ref[rows, :], p_ref, o_ref, rows, 4 * Q)
    p_ref.flush()
    o_ref.flush()
    out_ref[...] = dot(o_ref[...], w[1][...]).astype(bf16)


gelu_c = 0.7978845608028654
gelu_k = 0.044715


def act_grads(idx, g_ref, w, out_ref, *, Q):
    n = w[0].shape[0] // 2
    core = idx[1]
    for half in range(2):
        for b in range(2):
            out_ref[half, pl.ds(b * Q, Q), :] = dot(
                g_ref[at(2 * b + core, Q), :], w[0][pl.ds(half * n, n), :]
            ).astype(bf16)


def ffn_both(idx, x1_ref, part_ref, recv_ref, g_ref, up, ga_ref, out_ref, x2_ref, a_ref, du_ref, send_ref, *, Q):
    for b in range(2):
        rows = pl.ds(b * Q, Q)
        x2 = x1_ref[rows, :] + (part_ref[rows, :].astype(f32) + recv_ref[rows, :].astype(f32))
        x2_ref[rows, :] = x2
        unit, _ = norm_parts(x2)
        send_ref[0, rows, :] = (unit * g_ref[2:3, :]).astype(bf16)
    x2_ref.flush()
    n = up[0].shape[0] // 2
    for grp in range(2):
        u = dot(send_ref[0], up[0][pl.ds(grp * n, n), :])
        t = jnp.tanh(gelu_c * (u + gelu_k * (u * u * u)))
        half = 0.5 * (1.0 + t)
        a = (u * half).astype(bf16)
        slope = half + 0.5 * u * (1.0 - t * t) * (gelu_c * (1.0 + 3.0 * gelu_k * (u * u)))
        du = (ga_ref[grp].astype(f32) * slope).astype(bf16)
        if grp == 0:
            a_ref[...] = a
            du_ref[...] = du
            a_ref.flush()
            du_ref.flush()
        else:
            send_ref[1] = a
            send_ref[2] = du
            send_ref.flush()
    out_ref[...] = (
        dot_nt(du_ref[...], up[0][pl.ds(0, n), :]) + dot_nt(send_ref[2], up[0][pl.ds(n, n), :])
    ).astype(bf16)


def attend_back(k_ref, v_ref, do_ref, p_ref, ds_ref, dq_ref, rows, nk):
    low, wide = pair_masks(bf16), pair_masks(f32)
    keys = pl.ds(0, nk)
    for pair in range(ds_ref.shape[0] // 2):
        lanes = pl.ds(pair * 2 * HEAD_DIM, 2 * HEAD_DIM)
        go, k, v = do_ref[rows, lanes], k_ref[keys, lanes], v_ref[keys, lanes]
        total = None
        for i in range(2):
            h = 2 * pair + i
            p = p_ref[h, rows, keys].astype(f32)
            gp = dot_nt(go * low[i], v)
            ds = (p * (gp - jnp.sum(p * gp, axis=-1, keepdims=True))).astype(bf16)
            ds_ref[h, rows, keys] = ds
            term = dot(ds, k) * wide[i]
            total = term if total is None else total + term
        dq_ref[rows, lanes] = (total * key_scale).astype(bf16)


def cross_back(idx, gr_ref, part_ref, recv_ref, x2_ref, g_ref, w, k_ref, v_ref, p_ref, h2_ref, out_ref, dx_ref, sendh_ref, do_ref, ds_ref, dq_ref, gain_ref, *, Q):
    core = idx[1]
    total = None
    for b in range(2):
        rows = pl.ds(b * Q, Q)
        dh = part_ref[rows, :].astype(f32) + recv_ref[rows, :].astype(f32)
        grad_rows, grad_gain = norm_back(x2_ref[rows, :], g_ref[2:3, :], dh)
        dx = gr_ref[at(2 * b + core, Q), :].astype(f32) + grad_rows
        dx_ref[rows, :] = dx
        total = grad_gain if total is None else total + grad_gain
        sendh_ref[0, rows, :] = dx.astype(bf16)
    dx_ref.flush()
    do_ref[...] = dot_nt(sendh_ref[0], w[1][...]).astype(bf16)
    do_ref.flush()
    for b in range(2):
        attend_back(k_ref, v_ref, do_ref, p_ref, ds_ref, dq_ref, pl.ds(b * Q, Q), 4 * Q)
    ds_ref.flush()
    dq_ref.flush()
    out_ref[...] = dot(dq_ref[...], w[0][...]).astype(bf16)
    out_ref.flush()
    sendh_ref[1] = h2_ref[...]
    gain_ref[...] = jnp.broadcast_to(total * 0.5, gain_ref.shape)


def key_grads(ds_ref, p_ref, q, go, dkt_ref, dvt_ref):
    qt = q.astype(f32).T.astype(bf16)
    gt = go.astype(f32).T.astype(bf16)
    for h in range(ds_ref.shape[0]):
        rows = pl.ds(h * HEAD_DIM, HEAD_DIM)
        take = slice(h * HEAD_DIM, (h + 1) * HEAD_DIM)
        dkt_ref[rows, :] = dot(qt[take], ds_ref[h]) * key_scale
        dvt_ref[rows, :] = dot(gt[take], p_ref[h])


def pack_keys(dkt_ref, dvt_ref, dq_ref, o_ref, dk_ref, dv_ref, send_ref, Q):
    W = dk_ref.shape[1]
    dk, dv = dkt_ref[...].T, dvt_ref[...].T
    send_ref[pl.ds(0, 4 * Q), 0:W] = dk[:, W:].astype(bf16)
    send_ref[pl.ds(0, 4 * Q), W:] = dv[:, W:].astype(bf16)
    send_ref[pl.ds(4 * Q, 2 * Q), 0:W] = dq_ref[:, W:]
    send_ref[pl.ds(4 * Q, 2 * Q), W:] = o_ref[:, W:]
    send_ref.flush()
    dk_ref[...] = dk[:, :W]
    dv_ref[...] = dv[:, :W]


def keys_body(idx, ds_ref, p_ref, q_ref, do_ref, dq_ref, o_ref, dk_ref, dv_ref, send_ref, dkt_ref, dvt_ref, *, Q):
    key_grads(ds_ref, p_ref, q_ref[...], do_ref[...], dkt_ref, dvt_ref)
    pack_keys(dkt_ref, dvt_ref, dq_ref, o_ref, dk_ref, dv_ref, send_ref, Q)


def self_back(idx, dx_ref, part_ref, recv_ref, x1_ref, g_ref, w, k_ref, v_ref, p_ref, q_ref, o_ref, gain3_ref, dx1_ref, gs_ref, dq_ref, dk_ref, dv_ref, send_ref, gain_ref, ds_ref, do_ref, dkt_ref, dvt_ref, sum_ref, *, Q):
    total = None
    for b in range(2):
        rows = pl.ds(b * Q, Q)
        dh = part_ref[rows, :].astype(f32) + recv_ref[rows, :].astype(f32)
        grad_rows, grad_gain = norm_back(x1_ref[rows, :], g_ref[1:2, :], dh)
        dx = dx_ref[rows, :] + grad_rows
        sum_ref[rows, :] = dx
        total = grad_gain if total is None else total + grad_gain
        gs_ref[rows, :] = dx.astype(bf16)
    gs_ref.flush()
    dx1_ref[...] = sum_ref[at(idx[0], Q), :]
    dx1_ref.flush()
    for i in range(ds_ref.shape[0]):
        ds_ref[i, pl.ds(0, Q), pl.ds(2 * Q, 2 * Q)] = jnp.zeros((Q, 2 * Q), bf16)
    do_ref[...] = dot_nt(gs_ref[...], w[0][...]).astype(bf16)
    for b in range(2):
        attend_back(k_ref, v_ref, do_ref, p_ref, ds_ref, dq_ref, pl.ds(b * Q, Q), 2 * Q * (b + 1))
    ds_ref.flush()
    dq_ref.flush()
    key_grads(ds_ref, p_ref, q_ref[...], do_ref[...], dkt_ref, dvt_ref)
    pack_keys(dkt_ref, dvt_ref, dq_ref, o_ref, dk_ref, dv_ref, send_ref, Q)
    gain_ref[0:1, :] = total * 0.5
    gain_ref[1:, :] = gain3_ref[1:, :]


def table_sums(idx, ds_ref, bucket_ref, Q, buckets, wide):
    y, core = idx[0], idx[1]
    L = 4 * Q
    heads = ds_ref.shape[0]
    lines = []
    for h in range(heads):
        line = ds_ref[h, pl.ds(0, Q), :].astype(f32) + pltpu.roll(
            ds_ref[h, pl.ds(Q, Q), :].astype(f32), L - 2 * Q, 1
        )
        n = Q // 2
        while n >= 1:
            line = line[:n] + pltpu.roll(line[n : 2 * n], L - n, 1)
            n //= 2
        lines.append(line)
    lines.append(jnp.zeros((8 - heads, L), f32))
    lines = pltpu.roll(jnp.concatenate(lines, axis=0), (4 - core) * Q, 1)
    lines = exact_dot(lines, backwards(L), ((1,), (0,)))
    sums = exact_dot(lines, bucket_rows(bucket_ref, buckets), ((1,), (1,)))
    lane = lax.broadcasted_iota(jnp.int32, (buckets, wide), 1)
    spread = (lax.broadcasted_iota(jnp.int32, (buckets, wide), 0) == lane % buckets).astype(f32)
    sums = exact_dot(sums, spread, ((1,), (0,)))
    row = lax.broadcasted_iota(jnp.int32, (8, wide), 0)
    other = (row >= heads // 2).astype(jnp.int32)
    owner = (2 * y + core) * (1 - other) + (2 * y + 1 - core) * other
    head = owner * (heads // 2) + row - other * (heads // 2)
    mine = (row < heads) & (lax.broadcasted_iota(jnp.int32, (8, wide), 1) // buckets == head)
    return jnp.sum(jnp.where(mine, sums, 0.0), axis=0, keepdims=True)


def shares(idx):
    y, core = idx[0], idx[1]
    return (2 * y + core, 2 * (1 - y) + core), (2 * y + 1 - core, 2 * (1 - y) + 1 - core)


def self_weights(idx, h_ref, gs_ref, gsr_ref, o_ref, dq_ref, dk_ref, dv_ref, recv_ref, w_ref, g_ref, ds_ref, bucket_ref, gain23_ref, *rest, Q, split, buckets, wide):
    core = idx[1]
    if split:
        keep_ref, send_ref, in_keep_ref, in_send_ref, small_ref, sum_ref, d_ref = rest
    else:
        sum_ref, in_keep_ref, in_send_ref, small_ref, d_ref = rest
    W = dk_ref.shape[1]
    for b in range(2):
        rows = pl.ds(b * Q, Q)
        d_ref[at(2 * b + core, Q), 0:W] = dq_ref[rows, 0:W]
        d_ref[at(2 * b + 1 - core, Q), 0:W] = recv_ref[pl.ds((4 + b) * Q, Q), 0:W]
    keys = pl.ds(0, 4 * Q)
    d_ref[:, W : 2 * W] = (dk_ref[...] + recv_ref[keys, 0:W].astype(f32)).astype(bf16)
    d_ref[:, 2 * W : 3 * W] = (dv_ref[...] + recv_ref[keys, W:].astype(f32)).astype(bf16)
    total = None
    for out, places in zip((in_keep_ref, in_send_ref), shares(idx)):
        for i, place in enumerate(places):
            rows = at(place, Q)
            grad = dot(d_ref[rows, :], w_ref[...])
            out[i] = grad.astype(out.dtype)
            term = jnp.sum(grad * h_ref[rows, :].astype(f32), axis=0, keepdims=True)
            total = term if total is None else total + term
        out.flush()
    small_ref[...] = jnp.zeros(small_ref.shape, f32)
    small_ref[0:1, :] = total / g_ref[0:1, :]
    small_ref[1:3, :] = gain23_ref[0:2, :]
    small_ref[3:4, 0:wide] = table_sums(idx, ds_ref, bucket_ref, Q, buckets, wide)
    small_ref.flush()
    sum_ref[:, 0 : 3 * W] = dot_tn(h_ref[...], d_ref[...])
    sum_ref[:, 3 * W : 4 * W] = dot_tn(gs_ref[...], o_ref[:, 0:W]) + dot_tn(
        gsr_ref[...], recv_ref[pl.ds(4 * Q, 2 * Q), W:]
    )
    if split:
        last = pl.ds(keep_ref.shape[0] * keep_ref.shape[1], 16)
        small = small_ref[...]
        high = small.astype(bf16)
        send_ref[last, :] = jnp.concatenate([high.astype(f32), small - high.astype(f32)]).astype(bf16)
        split_rows(idx, sum_ref, keep_ref, send_ref)


def split_rows(idx, sum_ref, keep_ref, send_ref):
    x, z_here = idx[2], idx[3]
    n = keep_ref.shape[1]
    places = [lax.bitwise_xor(z_here, i) for i in (0, 2, 1, 3)]
    for i, z in enumerate(places):
        block = sum_ref[at(2 * z + 1 - x, n), :].astype(send_ref.dtype)
        if len(send_ref.shape) == 3:
            send_ref[i] = block
        else:
            send_ref[pl.ds(i * n, n), :] = block
    send_ref.flush()
    for i, z in enumerate(places):
        keep_ref[i] = sum_ref[at(2 * z + x, n), :].astype(keep_ref.dtype)


def cross_weights(idx, sendh_ref, recvh_ref, e_ref, dq_ref, dk_ref, dv_ref, o_ref, recv_ref, wk_ref, wv_ref, a_ref, b_ref, down, x2_ref, *rest, Q, split):
    y = idx[0]
    outs, (d_ref, rows_ref) = list(rest[:-2]), rest[-2:]
    if split:
        keep_ref, send_ref, ekeep_ref, esend_ref, okeep_ref, osend_ref, sum_ref = outs
    else:
        sum_ref, ekeep_ref, esend_ref, okeep_ref, osend_ref = outs
    W = dk_ref.shape[1]
    low, keys = pl.ds(4 * Q, 2 * Q), pl.ds(0, 4 * Q)
    d_ref[:, 0:W] = (dk_ref[...] + recv_ref[keys, 0:W].astype(f32)).astype(bf16)
    d_ref[:, W:] = (dv_ref[...] + recv_ref[keys, W:].astype(f32)).astype(bf16)
    sum_ref[:, W : 3 * W] = dot_tn(e_ref[...], d_ref[...])
    sum_ref[:, 0:W] = dot_tn(sendh_ref[1], dq_ref[:, 0:W]) + dot_tn(recvh_ref[1], recv_ref[low, 0:W])
    sum_ref[:, 3 * W : 4 * W] = dot_tn(sendh_ref[0], o_ref[:, 0:W]) + dot_tn(recvh_ref[0], recv_ref[low, W:])
    if split:
        split_rows(idx, sum_ref, keep_ref, send_ref)
        keep_ref.flush()
    keep, send = shares(idx)
    for out, places in ((esend_ref, send), (ekeep_ref, keep)):
        for i, place in enumerate(places):
            take = d_ref[at(place, Q), :]
            out[i] = (dot(take[:, :W], wk_ref[...]) + dot(take[:, W:], wv_ref[...])).astype(out.dtype)
        out.flush()
    n = down[0].shape[0] // 2
    rows_ref[...] = dot_nt(a_ref[...], down[0][pl.ds(0, n), :]) + dot_nt(b_ref[0], down[0][pl.ds(n, n), :])
    osend_ref[...] = rows_ref[at(1 - y, Q), :].astype(bf16)
    osend_ref.flush()
    okeep_ref[...] = rows_ref[at(y, Q), :] + x2_ref[at(y, Q), :]


def ffn_weights(idx, g_ref, a_ref, h_ref, d_ref, hr_ref, ar_ref, dr_ref, *rest, Q, split):
    core = idx[1]
    F = a_ref.shape[1]
    if split:
        keep_ref, send_ref, sum_ref, all_ref = rest
    else:
        sum_ref, all_ref = rest
    for b in range(2):
        all_ref[at(2 * b + core, Q), :] = a_ref[pl.ds(b * Q, Q), :]
        all_ref[at(2 * b + 1 - core, Q), :] = ar_ref[0, pl.ds(b * Q, Q), :]
    sum_ref[:, F:] = dot_tn(g_ref[...], all_ref[...])
    sum_ref[:, 0:F] = dot_tn(h_ref[0], d_ref[...]) + dot_tn(hr_ref[0], dr_ref[0])
    if split:
        split_rows(idx, sum_ref, keep_ref, send_ref)


def together(*values):
    return lax.optimization_barrier(values)


def local(
    decoder_in,
    encoder_states,
    dec_segments,
    enc_segments,
    offset_buckets,
    norm_gains,
    bias_table,
    self_query,
    self_key,
    self_value,
    self_out,
    cross_query,
    cross_key,
    cross_value,
    cross_out,
    ffn_up,
    ffn_down,
    out_grad,
    dp_size,
):
    Q, D = decoder_in.shape[1:]
    L = 4 * Q
    W = self_query.shape[1]
    F = ffn_up.shape[1]
    heads = bias_table.shape[1]
    buckets = bias_table.shape[0]
    split = dp_size == 8
    mp = lax.axis_index("mp")
    y = mp // 2

    def over_mp(v, flip):
        return lax.ppermute(v, "mp", [(i, i ^ flip) for i in range(4)])

    def over_dp(v, flip):
        return lax.ppermute(v, "dp", [(i, i ^ flip) for i in range(dp_size)])

    def call(body, name, outs, *args, scratch=(), **static):
        static["Q"] = Q
        return kernel_call(functools.partial(body, **static), name, outs, *args, scratch=scratch, Q=Q)

    x_here = decoder_in[0]
    x_core = over_mp(x_here, 1)
    x_across = over_mp(x_here, 2)
    table_p = over_mp(bias_table.T, 1)
    wq, table_p = together(self_query.T, table_p)
    w_self = jnp.concatenate([wq, self_key.T, self_value.T, self_out.T])
    w_self_p = over_mp(w_self, 1)
    bucket_line = offset_buckets.reshape(1, L)
    bias, cross_mask = call(
        bias_body,
        "bias",
        [shape((2 * heads, 2 * Q, L), f32), shape((2 * Q, L), f32)],
        bias_table.T,
        table_p,
        bucket_line,
        dec_segments,
        enc_segments,
    )
    x_across, bias = together(x_across, bias)
    x4 = (x_here, x_across, x_core, over_mp(x_across, 1))

    def x_rows():
        return Quarters(x4, Q)

    eg_here = jnp.concatenate([encoder_states[0], out_grad[0]])
    eg_across = over_mp(eg_here, 2)
    w_cross = jnp.concatenate([cross_query.T, cross_key.T, cross_value.T, cross_out.T])

    def e_rows():
        return Quarters(eg4, Q)

    def g_rows():
        return Quarters(eg4, Q, Q)

    def self_w(*picks):
        return Joined(w_self, w_self_p, picks, 4)

    def cross_w(*picks):
        return Joined(w_cross, w_cross_p, picks, 4)

    both_rows, both_all = shape((2 * Q, 2 * W)), shape((L, 2 * W))
    square = shape((2 * heads, 2 * Q, L))
    half = shape((2 * Q, D))
    half_f = shape((2 * Q, D), f32)
    line = shape((8, D), f32)

    part1, h1, q1, k1, v1, p1, o1 = call(
        self_forward,
        "self_forward",
        [half, shape((L, D)), both_rows, both_all, both_all, square, both_rows],
        x_rows(),
        norm_gains,
        self_w(0, 1, 2, 3),
        bias,
    )
    recv1 = over_mp(part1, 2)
    w_cross_p = over_mp(w_cross, 1)
    eg_across, q1 = together(eg_across, q1)
    eg4 = (eg_here, eg_across, over_mp(eg_here, 1), over_mp(eg_across, 1))
    up = Joined(ffn_up, over_mp(ffn_up, 1), (0,), 1)
    down_p = over_mp(ffn_down, 1)
    k2, v2 = call(encoder_keys, "encoder_keys", [both_all, both_all], e_rows(), cross_w(1, 2))
    part2, x1, h2, q2, p2, o2 = call(
        cross_forward,
        "cross_forward",
        [half, half_f, half, both_rows, square, both_rows],
        x_rows(),
        part1,
        recv1,
        norm_gains,
        cross_w(0, 3),
        k2,
        v2,
        cross_mask,
    )
    recv2 = over_mp(part2, 2)
    down_p, h2 = together(down_p, h2)
    down = Joined(ffn_down, down_p, (0,), 1)
    (grad_act,) = call(act_grads, "act_grads", [shape((2, 2 * Q, F))], g_rows(), down)
    part3, x2, a_own, du_own, send3 = call(
        ffn_both,
        "ffn_both",
        [half, half_f, shape((2 * Q, F)), shape((2 * Q, F)), shape((3, 2 * Q, D))],
        x1,
        part2,
        recv2,
        norm_gains,
        up,
        grad_act,
    )
    recv3 = over_mp(part3, 2)
    recv_ffn = over_mp(send3, 1)
    quarter, quarter_f = shape((Q, D)), shape((Q, D), f32)

    def grad_kernel(body, name, cols, *args, extra=(), scratch=(), send_rows=0, **static):
        if split:
            keep = shape((dp_size // 2, D // dp_size, cols))
            outs = [keep, shape((send_rows, cols)) if send_rows else keep, *extra]
            scratch = [pltpu.VMEM((D, cols), f32), *scratch]
        else:
            outs = [shape((D, cols), f32), *extra]
        res = call(body, name, outs, *args, scratch=scratch, split=split, **static)
        return (res[:2], res[2:]) if split else (res[:1], res[1:])

    def over_x(parts):
        return (parts[0], over_dp(parts[1], 1)) if split else parts

    def first_half(pair):
        return (pair[0][2:].astype(f32) + pair[1][2:].astype(f32)).astype(bf16)

    def second_half(pair, recv):
        return (pair[0][1].astype(f32) + pair[1][1].astype(f32) + recv[1].astype(f32)).astype(bf16)

    def finish(pair, recv, last):
        return pair[0][0].astype(f32) + pair[1][0].astype(f32) + recv[0].astype(f32) + last.astype(f32)

    def scatter(parts):
        return lax.psum_scatter(parts[0], "dp", scatter_dimension=0, tiled=True)

    def columns(total, count):
        width = total.shape[1] // count
        return [total[:, i * width : (i + 1) * width] for i in range(count)]

    ffn_parts, _ = grad_kernel(
        ffn_weights,
        "ffn_weights",
        2 * F,
        g_rows(),
        a_own,
        Part(send3, 0, 1),
        du_own,
        Part(recv_ffn, 0, 1),
        Part(recv_ffn, 1, 1),
        Part(recv_ffn, 2, 1),
        scratch=[pltpu.VMEM((L, F), bf16)],
    )
    own_f = shape((L, W), f32)
    packed = shape((6 * Q, 2 * W))
    turned_f = pltpu.VMEM((2 * W, L), f32)
    if split:
        recv3, ffn_keep = together(recv3, ffn_parts[0])
        ffn_parts = (ffn_keep, ffn_parts[1])
    part4, dx2, send4, do2, ds2, dq2, gain3 = call(
        cross_back,
        "cross_back",
        [half, half_f, shape((2, 2 * Q, D)), both_rows, square, both_rows, line],
        g_rows(),
        part3,
        recv3,
        x2,
        norm_gains,
        cross_w(0, 3),
        k2,
        v2,
        p2,
        h2,
    )
    recv4 = over_mp(part4, 2)
    if split:
        do2, ffn_send = together(do2, ffn_parts[1])
        ffn_parts = (ffn_parts[0], ffn_send)
    recv_h = over_mp(send4, 1)
    dk2, dv2, send_k = call(
        keys_body, "cross_keys", [own_f, own_f, packed], ds2, p2, q2, do2, dq2, o2, scratch=[turned_f, turned_f]
    )
    recv_k = over_mp(send_k, 1)
    pair_f, pair = shape((2, Q, D), f32), shape((2, Q, D))
    recv4, dk2 = together(recv4, dk2)
    dx1, gs, dq1, dk1, dv1, send_s, gain23, ds1 = call(
        self_back,
        "self_back",
        [quarter_f, half, both_rows, own_f, own_f, packed, line, square],
        dx2,
        part4,
        recv4,
        x1,
        norm_gains,
        self_w(3),
        k1,
        v1,
        p1,
        q1,
        o1,
        gain3,
        scratch=[pltpu.VMEM((2 * Q, 2 * W), bf16), turned_f, turned_f, pltpu.VMEM((2 * Q, D), f32)],
    )
    recv_s = over_mp(send_s, 1)
    gs_oth = over_mp(gs, 1)
    n = D // dp_size
    if split:
        ffn_pair = over_x(ffn_parts)
    self_parts, (in_keep, in_send, small) = grad_kernel(
        self_weights,
        "self_weights",
        4 * W,
        h1,
        gs,
        gs_oth,
        o1,
        dq1,
        dk1,
        dv1,
        recv_s,
        Part(w_self, 0, 3 * W),
        norm_gains,
        ds1,
        bucket_line,
        gain23,
        buckets=buckets,
        wide=4 * heads * buckets,
        extra=[pair_f, pair, shape((8, D), f32)],
        scratch=[pltpu.VMEM((L, 3 * W), bf16)],
        send_rows=D // 2 + 16,
    )
    if split:
        recv_k, in_keep, ffn_half = together(recv_k, in_keep, first_half(ffn_pair))
        ffn_recv = over_dp(ffn_half, 2)
    cross_parts, (enc_keep, enc_send, out_keep, out_send) = grad_kernel(
        cross_weights,
        "cross_weights",
        4 * W,
        send4,
        recv_h,
        e_rows(),
        dq2,
        dk2,
        dv2,
        o2,
        recv_k,
        Part(w_cross, W, W),
        Part(w_cross, 2 * W, W),
        a_own,
        Part(send3, 1, 1),
        down,
        x2,
        extra=[pair_f, pair, quarter_f, quarter],
        scratch=[pltpu.VMEM((L, 2 * W), bf16), pltpu.VMEM((2 * Q, D), f32)],
    )

    def halves(v):
        high = v.astype(bf16)
        return [high, (v - high.astype(f32)).astype(bf16)]

    def passed_on(keep, recv):
        return (keep[1] + recv[1].astype(f32)).astype(bf16)

    def add_tail(v, tail):
        return v + (tail[:8].astype(f32) + tail[8:].astype(f32))

    if split:
        self_recv = over_dp(self_parts[1], 1)
        in_send, enc_send, cross_send, self_recv, ffn_recv = together(
            in_send, enc_send, cross_parts[1], self_recv, ffn_recv
        )
        cross_parts = (cross_parts[0], cross_send)
    in_recv, enc_recv = over_mp(in_send, 1), over_mp(enc_send, 1)
    across = jnp.concatenate([passed_on(in_keep, in_recv), passed_on(enc_keep, enc_recv), out_send])
    across = over_mp(across, 2)
    if split:
        keep, recv = self_parts[0], self_recv
        m = D // 2
        small = add_tail(small, recv[m:])
        half = (keep[2:].reshape(2 * n, 4 * W).astype(f32) + recv[2 * n : m].astype(f32)).astype(bf16)
        half_recv = over_dp(jnp.concatenate([half, *halves(small)]), 2)
        cross_pair = over_x(cross_parts)
        half_recv, cross_recv = together(half_recv, cross_pair[1])
        cross_pair = (cross_pair[0], cross_recv)
        small = add_tail(small, half_recv[2 * n :])
        ffn_last = over_dp(second_half(ffn_pair, ffn_recv), 4)
        quarter_sum = keep[1].astype(f32) + recv[n : 2 * n].astype(f32) + half_recv[n : 2 * n].astype(f32)
        last = over_dp(jnp.concatenate([quarter_sum.astype(bf16), *halves(small)]), 4)
        last, ffn_last = together(last, ffn_last)
        small = add_tail(small, last[n:])
        self_total = (
            keep[0].astype(f32) + recv[:n].astype(f32) + half_recv[:n].astype(f32) + last[:n].astype(f32)
        )
        ffn_total = finish(ffn_pair, ffn_recv, ffn_last)
        cross_recv = over_dp(first_half(cross_pair), 2)
        cross_total = finish(cross_pair, cross_recv, over_dp(second_half(cross_pair, cross_recv), 4))
    else:
        small = lax.psum(small, "dp")
        ffn_total, cross_total, self_total = map(scatter, (ffn_parts, cross_parts, self_parts))
    grad_up, grad_down = ffn_total[:, :F], ffn_total[:, F:]

    def sum_rows(keep, recv, last):
        return keep[0] + recv[0].astype(f32) + last.astype(f32)

    grad_rows, _ = norm_back(decoder_in[0].astype(f32), norm_gains[0:1], sum_rows(in_keep, in_recv, across[:Q]))
    grad_decoder = (dx1 + grad_rows).astype(bf16)
    grad_encoder = sum_rows(enc_keep, enc_recv, across[Q : 2 * Q]).astype(bf16)
    output = (out_keep + across[2 * Q :].astype(f32)).astype(bf16)

    small = small + over_mp(small, 1)
    small = small + over_mp(small, 2)
    gain_total = small[:3]
    table_total = small[3, : 4 * heads * buckets].reshape(4 * heads, buckets).T
    grad_cq, grad_ck, grad_cv, grad_co = columns(cross_total, 4)
    grad_sq, grad_sk, grad_sv, grad_so = columns(self_total, 4)

    def row(v):
        return v.reshape((1,) + v.shape)

    return (
        row(output),
        row(grad_decoder),
        row(grad_encoder),
        grad_sq,
        grad_sk,
        grad_sv,
        grad_so,
        grad_cq,
        grad_ck,
        grad_cv,
        grad_co,
        grad_up,
        grad_down,
        gain_total,
        table_total,
    )


def solution(mesh):
    rows = P("dp", "mp", None)
    cols = P(None, "mp")
    grads = P("dp", "mp")
    in_specs = (rows, rows, P("dp", None), P("dp", None), P(), P(), cols) + (cols,) * 10 + (rows,)
    out_specs = (rows, rows, rows) + (grads,) * 10 + (P(), P())
    body = functools.partial(local, dp_size=mesh.shape["dp"])
    return jax.shard_map(body, mesh=mesh, in_specs=in_specs, out_specs=out_specs, check_vma=False)
```

```python
import functools

import jax
import jax.numpy as jnp
from jax import lax
from jax.experimental import pallas as pl
from jax.experimental.pallas import tpu as pltpu
from jax.sharding import PartitionSpec as P

HEAD_DIM = 64
epsilon = 1e-06
key_scale = 0.125
masked_score = -1e30
highest = lax.Precision.HIGHEST
bf16 = jnp.bfloat16
f32 = jnp.float32


def dot(a, b):
    return lax.dot_general(a, b, (((1,), (0,)), ((), ())), preferred_element_type=f32)


def dot_nt(a, b):
    return lax.dot_general(a, b, (((1,), (1,)), ((), ())), preferred_element_type=f32)


def dot_tn(a, b):
    return lax.dot_general(a, b, (((0,), (0,)), ((), ())), preferred_element_type=f32)


def norm_parts(rows):
    inv = lax.rsqrt(jnp.mean(rows * rows, axis=-1, keepdims=True) + epsilon)
    return rows * inv, inv


def norm_back(rows, gain, grad):
    unit, inv = norm_parts(rows)
    grad_unit = grad * gain
    grad_rows = inv * (grad_unit - unit * jnp.mean(grad_unit * unit, axis=-1, keepdims=True))
    return grad_rows, jnp.sum(grad * unit, axis=0, keepdims=True)


def at(index, size):
    return pl.ds(pl.multiple_of(index * size, size), size)


def shape(dims, dtype=bf16):
    return jax.ShapeDtypeStruct(dims, dtype)


class Whole:
    def __init__(self, array):
        self.arrays = [array]
        self.scratch = [(array.shape, array.dtype)]
        self.copies = 1

    def plan(self, idx, refs, scr, Q):
        return [(refs[0], scr[0])]

    def view(self, lazy, scr):
        return Late(scr[0], lazy)


class Quarters:
    def __init__(self, pieces, n, first=0):
        self.arrays = list(pieces)
        self.first = first
        d = pieces[0].shape[1]
        self.scratch = [((4 * n, d), pieces[0].dtype)]
        self.copies = 4

    def plan(self, idx, refs, scr, Q):
        y, c = idx[0], idx[1]
        places = (2 * y + c, 2 * (1 - y) + c, 2 * y + 1 - c, 2 * (1 - y) + 1 - c)
        return [(r.at[pl.ds(self.first, Q)], scr[0].at[at(p, Q)]) for r, p in zip(refs, places)]

    def view(self, lazy, scr):
        return Late(scr[0], lazy)


class Joined:
    def __init__(self, own, other, picks, count):
        self.arrays = [own, other]
        self.picks = picks
        self.rows = own.shape[0] // count
        self.scratch = [((2 * self.rows, own.shape[1]), own.dtype) for _ in picks]
        self.copies = 2 * len(picks)

    def plan(self, idx, refs, scr, Q):
        n = self.rows
        out = []
        for s, i in zip(scr, self.picks):
            for half, r in enumerate(refs):
                out.append((r.at[pl.ds(i * n, n)], s.at[pl.ds(half * n, n)]))
        return out

    def view(self, lazy, scr):
        return [Late(s, lazy[2 * i : 2 * i + 2]) for i, s in enumerate(scr)]


class Part:
    def __init__(self, array, first, rows):
        self.arrays = [array]
        self.first, self.rows = first, rows
        self.scratch = [((rows,) + array.shape[1:], array.dtype)]
        self.copies = 1

    def plan(self, idx, refs, scr, Q):
        return [(refs[0].at[pl.ds(self.first, self.rows)], scr[0])]

    def view(self, lazy, scr):
        return Late(scr[0], lazy)


class Late:
    def __init__(self, ref, copies):
        self.ref, self.copies = ref, list(copies)
        self.shape, self.dtype = ref.shape, ref.dtype

    def __getitem__(self, index):
        while self.copies:
            self.copies.pop().wait()
        return self.ref[index]


class Result:
    def __init__(self, ref, copy):
        self.ref, self.copy, self.started = ref, copy, False
        self.shape, self.dtype = ref.shape, ref.dtype

    def __getitem__(self, index):
        return self.ref[index]

    def __setitem__(self, index, value):
        self.ref[index] = value

    def flush(self):
        if not self.started:
            self.copy.start()
            self.started = True


def kernel_call(body, name, outs, *args, scratch=(), Q=128, flops=0):
    specs = [a if not hasattr(a, "dtype") else Whole(a) for a in args]
    arrays = [v for s in specs for v in s.arrays]
    in_scr = [x for s in specs for x in s.scratch]
    n_copies = sum(s.copies for s in specs)

    def whole(*refs):
        refs = list(refs)
        mp, dp = lax.axis_index("mp"), lax.axis_index("dp")
        idx_ref = (mp >> 1, mp & 1, dp & 1, dp >> 1)
        ins = [refs.pop(0) for _ in arrays]
        out_refs = [refs.pop(0) for _ in outs]
        scrs = [refs.pop(0) for _ in in_scr]
        out_scr = [refs.pop(0) for _ in outs]
        in_sem, out_sem = refs.pop(0), refs.pop(0)
        views, sem = [], 0
        for s in specs:
            mine = [ins.pop(0) for _ in s.arrays]
            scr = [scrs.pop(0) for _ in s.scratch]
            copies = []
            for src, dst in s.plan(idx_ref, mine, scr, Q):
                copy = pltpu.make_async_copy(src, dst, in_sem.at[sem])
                copy.start()
                sem += 1
                copies.append(copy)
            views.append((s, copies, scr))
        lates = [s.view(copies, scr) for s, copies, scr in views]
        results = [
            Result(s, pltpu.make_async_copy(s, o, out_sem.at[i]))
            for i, (s, o) in enumerate(zip(out_scr, out_refs))
        ]
        body(idx_ref, *lates, *results, *refs)
        for late in lates:
            for v in late if isinstance(late, list) else [late]:
                while v.copies:
                    v.copies.pop().wait()
        for r in results:
            r.flush()
        for r in results:
            r.copy.wait()

    moved = sum(v.size * v.dtype.itemsize for v in arrays)
    moved += sum(v.size * v.dtype.itemsize for v in outs)
    return pl.pallas_call(
        whole,
        out_shape=outs,
        in_specs=[pl.BlockSpec(memory_space=pl.ANY)] * len(arrays),
        out_specs=[pl.BlockSpec(memory_space=pl.ANY)] * len(outs),
        scratch_shapes=[pltpu.VMEM(d, t) for d, t in in_scr]
        + [pltpu.VMEM(o.shape, o.dtype) for o in outs]
        + [pltpu.SemaphoreType.DMA((n_copies,)), pltpu.SemaphoreType.DMA((len(outs),))]
        + list(scratch),
        compiler_params=pltpu.CompilerParams(vmem_limit_bytes=58 * 1024 * 1024),
        cost_estimate=pl.CostEstimate(flops=flops, bytes_accessed=moved, transcendentals=0),
        name=name,
    )(*arrays)


def pair_masks(dtype):
    lane = lax.broadcasted_iota(jnp.int32, (1, 2 * HEAD_DIM), 1) // HEAD_DIM
    return [(lane == h).astype(f32).astype(dtype) for h in range(2)]


def bucket_rows(bucket_ref, count):
    L = bucket_ref.shape[1]
    return (lax.broadcasted_iota(jnp.int32, (count, L), 0) == bucket_ref[...]).astype(f32)


def backwards(L):
    row = lax.broadcasted_iota(jnp.int32, (L, L), 0)
    col = lax.broadcasted_iota(jnp.int32, (L, L), 1)
    return ((row + col == L) | ((row == 0) & (col == 0))).astype(f32)


def exact_dot(a, b, dims):
    return lax.dot_general(a, b, (dims, ((), ())), precision=highest, preferred_element_type=f32)


def bias_body(idx, to_ref, tp_ref, bucket_ref, segr_ref, enc_ref, bias_ref, cross_ref, *, Q):
    core = idx[1]
    L = 4 * Q
    heads, buckets = to_ref.shape
    hot = exact_dot(bucket_rows(bucket_ref, buckets), backwards(L), ((1,), (0,)))
    lines = [exact_dot(t[...], hot, ((1,), (0,))) for t in (to_ref, tp_ref)]
    seg = segr_ref[...]
    columns = jnp.broadcast_to(seg.astype(f32), (Q, L)).T
    for b in range(2):
        rows = pl.ds(b * Q, Q)
        low = columns[2 * b * Q : (2 * b + 1) * Q, 0:1]
        high = columns[(2 * b + 1) * Q : (2 * b + 2) * Q, 0:1]
        segc = jnp.where(core == 0, low, high).astype(jnp.int32)
        cross_ref[rows, :] = jnp.where(segc == enc_ref[...], 0.0, masked_score)
        place = (2 * b + core) * Q + lax.broadcasted_iota(jnp.int32, (Q, L), 0)
        col = lax.broadcasted_iota(jnp.int32, (Q, L), 1)
        allowed = (segc == seg) & (col <= place)
        for grp in range(2):
            turned = pltpu.roll(lines[grp], (2 * b + core) * Q, 1)
            for h in range(heads):
                line = jnp.broadcast_to(turned[h : h + 1, :], (Q, L))
                line = pltpu.roll(line, 0, 1, stride=1, stride_axis=0)
                bias_ref[grp * heads + h, rows, :] = jnp.where(allowed, line, masked_score)


def soft_mix(q_ref, k_ref, v_ref, extra, p_ref, o_ref, rows, nk):
    low, wide = pair_masks(bf16), pair_masks(f32)
    keys = pl.ds(0, nk)
    for pair in range(p_ref.shape[0] // 2):
        lanes = pl.ds(pair * 2 * HEAD_DIM, 2 * HEAD_DIM)
        q, k, v = q_ref[rows, lanes], k_ref[keys, lanes], v_ref[keys, lanes]
        mixed = None
        for i in range(2):
            h = 2 * pair + i
            s = dot_nt(q * low[i], k) * key_scale + extra(h)
            top = jnp.max(s, axis=-1, keepdims=True)
            e = jnp.exp(s - top)
            p = (e * (1.0 / jnp.sum(e, axis=-1, keepdims=True))).astype(bf16)
            p_ref[h, rows, keys] = p
            term = dot(p, v) * wide[i]
            mixed = term if mixed is None else mixed + term
        o_ref[rows, lanes] = mixed.astype(bf16)


def self_forward(idx, x_ref, g_ref, w, bias_ref, part_ref, h_ref, q_ref, k_ref, v_ref, p_ref, o_ref, *, Q):
    core = idx[1]
    gain = g_ref[0:1, :]
    for t in range(4):
        rows = pl.ds(t * Q, Q)
        unit, _ = norm_parts(x_ref[rows, :].astype(f32))
        h_ref[rows, :] = (unit * gain).astype(bf16)
    h_ref.flush()
    k_ref[...] = dot_nt(h_ref[...], w[1][...]).astype(bf16)
    k_ref.flush()
    v_ref[...] = dot_nt(h_ref[...], w[2][...]).astype(bf16)
    v_ref.flush()
    for b in range(2):
        hb = h_ref[at(2 * b + core, Q), :]
        q_ref[pl.ds(b * Q, Q), :] = dot_nt(hb, w[0][...]).astype(bf16)
    q_ref.flush()
    for i in range(p_ref.shape[0]):
        p_ref[i, pl.ds(0, Q), pl.ds(2 * Q, 2 * Q)] = jnp.zeros((Q, 2 * Q), bf16)
    for b in range(2):
        nk = 2 * Q * (b + 1)
        rows = pl.ds(b * Q, Q)
        soft_mix(q_ref, k_ref, v_ref, lambda h: bias_ref[h, rows, pl.ds(0, nk)], p_ref, o_ref, rows, nk)
    p_ref.flush()
    o_ref.flush()
    part_ref[...] = dot(o_ref[...], w[3][...]).astype(bf16)


def encoder_keys(idx, e_ref, w, k_ref, v_ref, *, Q):
    k_ref[...] = dot_nt(e_ref[...], w[0][...]).astype(bf16)
    v_ref[...] = dot_nt(e_ref[...], w[1][...]).astype(bf16)


def cross_forward(idx, x_ref, part_ref, recv_ref, g_ref, w, k_ref, v_ref, mask_ref, out_ref, x1_ref, h_ref, q_ref, p_ref, o_ref, *, Q):
    core = idx[1]
    for b in range(2):
        rows = pl.ds(b * Q, Q)
        x1 = x_ref[at(2 * b + core, Q), :].astype(f32) + (
            part_ref[rows, :].astype(f32) + recv_ref[rows, :].astype(f32)
        )
        x1_ref[rows, :] = x1
        unit, _ = norm_parts(x1)
        h_ref[rows, :] = (unit * g_ref[1:2, :]).astype(bf16)
    x1_ref.flush()
    h_ref.flush()
    q_ref[...] = dot_nt(h_ref[...], w[0][...]).astype(bf16)
    q_ref.flush()
    for b in range(2):
        rows = pl.ds(b * Q, Q)
        soft_mix(q_ref, k_ref, v_ref, lambda h: mask_ref[rows, :], p_ref, o_ref, rows, 4 * Q)
    p_ref.flush()
    o_ref.flush()
    out_ref[...] = dot(o_ref[...], w[1][...]).astype(bf16)


gelu_c = 0.7978845608028654
gelu_k = 0.044715


def act_grads(idx, g_ref, w, out_ref, *, Q):
    n = w[0].shape[0] // 2
    core = idx[1]
    for half in range(2):
        for b in range(2):
            out_ref[half, pl.ds(b * Q, Q), :] = dot(
                g_ref[at(2 * b + core, Q), :], w[0][pl.ds(half * n, n), :]
            ).astype(bf16)


def ffn_both(idx, x1_ref, part_ref, recv_ref, g_ref, up, ga_ref, out_ref, x2_ref, a_ref, du_ref, send_ref, *, Q):
    for b in range(2):
        rows = pl.ds(b * Q, Q)
        x2 = x1_ref[rows, :] + (part_ref[rows, :].astype(f32) + recv_ref[rows, :].astype(f32))
        x2_ref[rows, :] = x2
        unit, _ = norm_parts(x2)
        send_ref[0, rows, :] = (unit * g_ref[2:3, :]).astype(bf16)
    x2_ref.flush()
    n = up[0].shape[0] // 2
    for grp in range(2):
        u = dot(send_ref[0], up[0][pl.ds(grp * n, n), :])
        t = jnp.tanh(gelu_c * (u + gelu_k * (u * u * u)))
        half = 0.5 * (1.0 + t)
        a = (u * half).astype(bf16)
        slope = half + 0.5 * u * (1.0 - t * t) * (gelu_c * (1.0 + 3.0 * gelu_k * (u * u)))
        du = (ga_ref[grp].astype(f32) * slope).astype(bf16)
        if grp == 0:
            a_ref[...] = a
            du_ref[...] = du
            a_ref.flush()
            du_ref.flush()
        else:
            send_ref[1] = a
            send_ref[2] = du
            send_ref.flush()
    out_ref[...] = (
        dot_nt(du_ref[...], up[0][pl.ds(0, n), :]) + dot_nt(send_ref[2], up[0][pl.ds(n, n), :])
    ).astype(bf16)


def attend_back(k_ref, v_ref, do_ref, p_ref, ds_ref, dq_ref, rows, nk):
    low, wide = pair_masks(bf16), pair_masks(f32)
    keys = pl.ds(0, nk)
    for pair in range(ds_ref.shape[0] // 2):
        lanes = pl.ds(pair * 2 * HEAD_DIM, 2 * HEAD_DIM)
        go, k, v = do_ref[rows, lanes], k_ref[keys, lanes], v_ref[keys, lanes]
        total = None
        for i in range(2):
            h = 2 * pair + i
            p = p_ref[h, rows, keys].astype(f32)
            gp = dot_nt(go * low[i], v)
            ds = (p * (gp - jnp.sum(p * gp, axis=-1, keepdims=True))).astype(bf16)
            ds_ref[h, rows, keys] = ds
            term = dot(ds, k) * wide[i]
            total = term if total is None else total + term
        dq_ref[rows, lanes] = (total * key_scale).astype(bf16)


def cross_back(idx, gr_ref, part_ref, recv_ref, x2_ref, g_ref, w, k_ref, v_ref, p_ref, h2_ref, out_ref, dx_ref, sendh_ref, do_ref, ds_ref, dq_ref, gain_ref, *, Q):
    core = idx[1]
    total = None
    for b in range(2):
        rows = pl.ds(b * Q, Q)
        dh = part_ref[rows, :].astype(f32) + recv_ref[rows, :].astype(f32)
        grad_rows, grad_gain = norm_back(x2_ref[rows, :], g_ref[2:3, :], dh)
        dx = gr_ref[at(2 * b + core, Q), :].astype(f32) + grad_rows
        dx_ref[rows, :] = dx
        total = grad_gain if total is None else total + grad_gain
        sendh_ref[0, rows, :] = dx.astype(bf16)
    dx_ref.flush()
    do_ref[...] = dot_nt(sendh_ref[0], w[1][...]).astype(bf16)
    do_ref.flush()
    for b in range(2):
        attend_back(k_ref, v_ref, do_ref, p_ref, ds_ref, dq_ref, pl.ds(b * Q, Q), 4 * Q)
    ds_ref.flush()
    dq_ref.flush()
    out_ref[...] = dot(dq_ref[...], w[0][...]).astype(bf16)
    out_ref.flush()
    sendh_ref[1] = h2_ref[...]
    gain_ref[...] = jnp.broadcast_to(total * 0.5, gain_ref.shape)


def key_grads(ds_ref, p_ref, q, go, dkt_ref, dvt_ref):
    qt = q.astype(f32).T.astype(bf16)
    gt = go.astype(f32).T.astype(bf16)
    for h in range(ds_ref.shape[0]):
        rows = pl.ds(h * HEAD_DIM, HEAD_DIM)
        take = slice(h * HEAD_DIM, (h + 1) * HEAD_DIM)
        dkt_ref[rows, :] = dot(qt[take], ds_ref[h]) * key_scale
        dvt_ref[rows, :] = dot(gt[take], p_ref[h])


def pack_keys(dkt_ref, dvt_ref, dq_ref, o_ref, dk_ref, dv_ref, send_ref, Q):
    W = dk_ref.shape[1]
    dk, dv = dkt_ref[...].T, dvt_ref[...].T
    send_ref[pl.ds(0, 4 * Q), 0:W] = dk[:, W:].astype(bf16)
    send_ref[pl.ds(0, 4 * Q), W:] = dv[:, W:].astype(bf16)
    send_ref[pl.ds(4 * Q, 2 * Q), 0:W] = dq_ref[:, W:]
    send_ref[pl.ds(4 * Q, 2 * Q), W:] = o_ref[:, W:]
    send_ref.flush()
    dk_ref[...] = dk[:, :W]
    dv_ref[...] = dv[:, :W]


def keys_body(idx, ds_ref, p_ref, q_ref, do_ref, dq_ref, o_ref, dk_ref, dv_ref, send_ref, dkt_ref, dvt_ref, *, Q):
    key_grads(ds_ref, p_ref, q_ref[...], do_ref[...], dkt_ref, dvt_ref)
    pack_keys(dkt_ref, dvt_ref, dq_ref, o_ref, dk_ref, dv_ref, send_ref, Q)


def self_back(idx, dx_ref, part_ref, recv_ref, x1_ref, g_ref, w, k_ref, v_ref, p_ref, q_ref, o_ref, gain3_ref, dx1_ref, gs_ref, dq_ref, dk_ref, dv_ref, send_ref, gain_ref, ds_ref, do_ref, dkt_ref, dvt_ref, sum_ref, *, Q):
    total = None
    for b in range(2):
        rows = pl.ds(b * Q, Q)
        dh = part_ref[rows, :].astype(f32) + recv_ref[rows, :].astype(f32)
        grad_rows, grad_gain = norm_back(x1_ref[rows, :], g_ref[1:2, :], dh)
        dx = dx_ref[rows, :] + grad_rows
        sum_ref[rows, :] = dx
        total = grad_gain if total is None else total + grad_gain
        gs_ref[rows, :] = dx.astype(bf16)
    gs_ref.flush()
    dx1_ref[...] = sum_ref[at(idx[0], Q), :]
    dx1_ref.flush()
    for i in range(ds_ref.shape[0]):
        ds_ref[i, pl.ds(0, Q), pl.ds(2 * Q, 2 * Q)] = jnp.zeros((Q, 2 * Q), bf16)
    do_ref[...] = dot_nt(gs_ref[...], w[0][...]).astype(bf16)
    for b in range(2):
        attend_back(k_ref, v_ref, do_ref, p_ref, ds_ref, dq_ref, pl.ds(b * Q, Q), 2 * Q * (b + 1))
    ds_ref.flush()
    dq_ref.flush()
    key_grads(ds_ref, p_ref, q_ref[...], do_ref[...], dkt_ref, dvt_ref)
    pack_keys(dkt_ref, dvt_ref, dq_ref, o_ref, dk_ref, dv_ref, send_ref, Q)
    gain_ref[0:1, :] = total * 0.5
    gain_ref[1:, :] = gain3_ref[1:, :]


def table_sums(idx, ds_ref, bucket_ref, Q, buckets, wide):
    y, core = idx[0], idx[1]
    L = 4 * Q
    heads = ds_ref.shape[0]
    lines = []
    for h in range(heads):
        line = ds_ref[h, pl.ds(0, Q), :].astype(f32) + pltpu.roll(
            ds_ref[h, pl.ds(Q, Q), :].astype(f32), L - 2 * Q, 1
        )
        n = Q // 2
        while n >= 1:
            line = line[:n] + pltpu.roll(line[n : 2 * n], L - n, 1)
            n //= 2
        lines.append(line)
    lines.append(jnp.zeros((8 - heads, L), f32))
    lines = pltpu.roll(jnp.concatenate(lines, axis=0), (4 - core) * Q, 1)
    lines = exact_dot(lines, backwards(L), ((1,), (0,)))
    sums = exact_dot(lines, bucket_rows(bucket_ref, buckets), ((1,), (1,)))
    lane = lax.broadcasted_iota(jnp.int32, (buckets, wide), 1)
    spread = (lax.broadcasted_iota(jnp.int32, (buckets, wide), 0) == lane % buckets).astype(f32)
    sums = exact_dot(sums, spread, ((1,), (0,)))
    row = lax.broadcasted_iota(jnp.int32, (8, wide), 0)
    other = (row >= heads // 2).astype(jnp.int32)
    owner = (2 * y + core) * (1 - other) + (2 * y + 1 - core) * other
    head = owner * (heads // 2) + row - other * (heads // 2)
    mine = (row < heads) & (lax.broadcasted_iota(jnp.int32, (8, wide), 1) // buckets == head)
    return jnp.sum(jnp.where(mine, sums, 0.0), axis=0, keepdims=True)


def shares(idx):
    y, core = idx[0], idx[1]
    return (2 * y + core, 2 * (1 - y) + core), (2 * y + 1 - core, 2 * (1 - y) + 1 - core)


def self_weights(idx, h_ref, gs_ref, gsr_ref, o_ref, dq_ref, dk_ref, dv_ref, recv_ref, w_ref, g_ref, ds_ref, bucket_ref, gain23_ref, *rest, Q, split, buckets, wide):
    core = idx[1]
    if split:
        keep_ref, send_ref, in_keep_ref, in_send_ref, small_ref, sum_ref, d_ref = rest
    else:
        sum_ref, in_keep_ref, in_send_ref, small_ref, d_ref = rest
    W = dk_ref.shape[1]
    for b in range(2):
        rows = pl.ds(b * Q, Q)
        d_ref[at(2 * b + core, Q), 0:W] = dq_ref[rows, 0:W]
        d_ref[at(2 * b + 1 - core, Q), 0:W] = recv_ref[pl.ds((4 + b) * Q, Q), 0:W]
    keys = pl.ds(0, 4 * Q)
    d_ref[:, W : 2 * W] = (dk_ref[...] + recv_ref[keys, 0:W].astype(f32)).astype(bf16)
    d_ref[:, 2 * W : 3 * W] = (dv_ref[...] + recv_ref[keys, W:].astype(f32)).astype(bf16)
    total = None
    for out, places in zip((in_keep_ref, in_send_ref), shares(idx)):
        for i, place in enumerate(places):
            rows = at(place, Q)
            grad = dot(d_ref[rows, :], w_ref[...])
            out[i] = grad.astype(out.dtype)
            term = jnp.sum(grad * h_ref[rows, :].astype(f32), axis=0, keepdims=True)
            total = term if total is None else total + term
        out.flush()
    small_ref[...] = jnp.zeros(small_ref.shape, f32)
    small_ref[0:1, :] = total / g_ref[0:1, :]
    small_ref[1:3, :] = gain23_ref[0:2, :]
    small_ref[3:4, 0:wide] = table_sums(idx, ds_ref, bucket_ref, Q, buckets, wide)
    small_ref.flush()
    sum_ref[:, 0 : 3 * W] = dot_tn(h_ref[...], d_ref[...])
    sum_ref[:, 3 * W : 4 * W] = dot_tn(gs_ref[...], o_ref[:, 0:W]) + dot_tn(
        gsr_ref[...], recv_ref[pl.ds(4 * Q, 2 * Q), W:]
    )
    if split:
        last = pl.ds(keep_ref.shape[0] * keep_ref.shape[1], 16)
        small = small_ref[...]
        high = small.astype(bf16)
        send_ref[last, :] = jnp.concatenate([high.astype(f32), small - high.astype(f32)]).astype(bf16)
        split_rows(idx, sum_ref, keep_ref, send_ref)


def split_rows(idx, sum_ref, keep_ref, send_ref):
    x, z_here = idx[2], idx[3]
    n = keep_ref.shape[1]
    places = [lax.bitwise_xor(z_here, i) for i in (0, 2, 1, 3)]
    for i, z in enumerate(places):
        block = sum_ref[at(2 * z + 1 - x, n), :].astype(send_ref.dtype)
        if len(send_ref.shape) == 3:
            send_ref[i] = block
        else:
            send_ref[pl.ds(i * n, n), :] = block
    send_ref.flush()
    for i, z in enumerate(places):
        keep_ref[i] = sum_ref[at(2 * z + x, n), :].astype(keep_ref.dtype)


def cross_weights(idx, sendh_ref, recvh_ref, e_ref, dq_ref, dk_ref, dv_ref, o_ref, recv_ref, wk_ref, wv_ref, a_ref, b_ref, down, x2_ref, *rest, Q, split):
    y = idx[0]
    outs, (d_ref, rows_ref) = list(rest[:-2]), rest[-2:]
    if split:
        keep_ref, send_ref, ekeep_ref, esend_ref, okeep_ref, osend_ref, sum_ref = outs
    else:
        sum_ref, ekeep_ref, esend_ref, okeep_ref, osend_ref = outs
    W = dk_ref.shape[1]
    low, keys = pl.ds(4 * Q, 2 * Q), pl.ds(0, 4 * Q)
    d_ref[:, 0:W] = (dk_ref[...] + recv_ref[keys, 0:W].astype(f32)).astype(bf16)
    d_ref[:, W:] = (dv_ref[...] + recv_ref[keys, W:].astype(f32)).astype(bf16)
    sum_ref[:, W : 3 * W] = dot_tn(e_ref[...], d_ref[...])
    sum_ref[:, 0:W] = dot_tn(sendh_ref[1], dq_ref[:, 0:W]) + dot_tn(recvh_ref[1], recv_ref[low, 0:W])
    sum_ref[:, 3 * W : 4 * W] = dot_tn(sendh_ref[0], o_ref[:, 0:W]) + dot_tn(recvh_ref[0], recv_ref[low, W:])
    if split:
        split_rows(idx, sum_ref, keep_ref, send_ref)
        keep_ref.flush()
    keep, send = shares(idx)
    for out, places in ((esend_ref, send), (ekeep_ref, keep)):
        for i, place in enumerate(places):
            take = d_ref[at(place, Q), :]
            out[i] = (dot(take[:, :W], wk_ref[...]) + dot(take[:, W:], wv_ref[...])).astype(out.dtype)
        out.flush()
    n = down[0].shape[0] // 2
    rows_ref[...] = dot_nt(a_ref[...], down[0][pl.ds(0, n), :]) + dot_nt(b_ref[0], down[0][pl.ds(n, n), :])
    osend_ref[...] = rows_ref[at(1 - y, Q), :].astype(bf16)
    osend_ref.flush()
    okeep_ref[...] = rows_ref[at(y, Q), :] + x2_ref[at(y, Q), :]


def ffn_weights(idx, g_ref, a_ref, h_ref, d_ref, hr_ref, ar_ref, dr_ref, *rest, Q, split):
    core = idx[1]
    F = a_ref.shape[1]
    if split:
        keep_ref, send_ref, sum_ref, all_ref = rest
    else:
        sum_ref, all_ref = rest
    for b in range(2):
        all_ref[at(2 * b + core, Q), :] = a_ref[pl.ds(b * Q, Q), :]
        all_ref[at(2 * b + 1 - core, Q), :] = ar_ref[0, pl.ds(b * Q, Q), :]
    sum_ref[:, F:] = dot_tn(g_ref[...], all_ref[...])
    sum_ref[:, 0:F] = dot_tn(h_ref[0], d_ref[...]) + dot_tn(hr_ref[0], dr_ref[0])
    if split:
        split_rows(idx, sum_ref, keep_ref, send_ref)


def together(*values):
    return lax.optimization_barrier(values)


def local(
    decoder_in,
    encoder_states,
    dec_segments,
    enc_segments,
    offset_buckets,
    norm_gains,
    bias_table,
    self_query,
    self_key,
    self_value,
    self_out,
    cross_query,
    cross_key,
    cross_value,
    cross_out,
    ffn_up,
    ffn_down,
    out_grad,
    dp_size,
):
    Q, D = decoder_in.shape[1:]
    L = 4 * Q
    W = self_query.shape[1]
    F = ffn_up.shape[1]
    heads = bias_table.shape[1]
    buckets = bias_table.shape[0]
    split = dp_size == 8
    mp = lax.axis_index("mp")
    y = mp // 2

    def over_mp(v, flip):
        return lax.ppermute(v, "mp", [(i, i ^ flip) for i in range(4)])

    def over_dp(v, flip):
        return lax.ppermute(v, "dp", [(i, i ^ flip) for i in range(dp_size)])

    def call(body, name, outs, *args, scratch=(), **static):
        static["Q"] = Q
        return kernel_call(functools.partial(body, **static), name, outs, *args, scratch=scratch, Q=Q)

    x_here = decoder_in[0]
    x_core = over_mp(x_here, 1)
    x_across = over_mp(x_here, 2)
    table_p = over_mp(bias_table.T, 1)
    wq, table_p = together(self_query.T, table_p)
    w_self = jnp.concatenate([wq, self_key.T, self_value.T, self_out.T])
    w_self_p = over_mp(w_self, 1)
    bucket_line = offset_buckets.reshape(1, L)
    bias, cross_mask = call(
        bias_body,
        "bias",
        [shape((2 * heads, 2 * Q, L), f32), shape((2 * Q, L), f32)],
        bias_table.T,
        table_p,
        bucket_line,
        dec_segments,
        enc_segments,
    )
    x_across, bias = together(x_across, bias)
    x4 = (x_here, x_across, x_core, over_mp(x_across, 1))

    def x_rows():
        return Quarters(x4, Q)

    eg_here = jnp.concatenate([encoder_states[0], out_grad[0]])
    eg_across = over_mp(eg_here, 2)
    w_cross = jnp.concatenate([cross_query.T, cross_key.T, cross_value.T, cross_out.T])

    def e_rows():
        return Quarters(eg4, Q)

    def g_rows():
        return Quarters(eg4, Q, Q)

    def self_w(*picks):
        return Joined(w_self, w_self_p, picks, 4)

    def cross_w(*picks):
        return Joined(w_cross, w_cross_p, picks, 4)

    both_rows, both_all = shape((2 * Q, 2 * W)), shape((L, 2 * W))
    square = shape((2 * heads, 2 * Q, L))
    half = shape((2 * Q, D))
    half_f = shape((2 * Q, D), f32)
    line = shape((8, D), f32)

    part1, h1, q1, k1, v1, p1, o1 = call(
        self_forward,
        "self_forward",
        [half, shape((L, D)), both_rows, both_all, both_all, square, both_rows],
        x_rows(),
        norm_gains,
        self_w(0, 1, 2, 3),
        bias,
    )
    recv1 = over_mp(part1, 2)
    w_cross_p = over_mp(w_cross, 1)
    eg_across, q1 = together(eg_across, q1)
    eg4 = (eg_here, eg_across, over_mp(eg_here, 1), over_mp(eg_across, 1))
    up = Joined(ffn_up, over_mp(ffn_up, 1), (0,), 1)
    down_p = over_mp(ffn_down, 1)
    k2, v2 = call(encoder_keys, "encoder_keys", [both_all, both_all], e_rows(), cross_w(1, 2))
    part2, x1, h2, q2, p2, o2 = call(
        cross_forward,
        "cross_forward",
        [half, half_f, half, both_rows, square, both_rows],
        x_rows(),
        part1,
        recv1,
        norm_gains,
        cross_w(0, 3),
        k2,
        v2,
        cross_mask,
    )
    recv2 = over_mp(part2, 2)
    down_p, h2 = together(down_p, h2)
    down = Joined(ffn_down, down_p, (0,), 1)
    (grad_act,) = call(act_grads, "act_grads", [shape((2, 2 * Q, F))], g_rows(), down)
    part3, x2, a_own, du_own, send3 = call(
        ffn_both,
        "ffn_both",
        [half, half_f, shape((2 * Q, F)), shape((2 * Q, F)), shape((3, 2 * Q, D))],
        x1,
        part2,
        recv2,
        norm_gains,
        up,
        grad_act,
    )
    recv3 = over_mp(part3, 2)
    recv_ffn = over_mp(send3, 1)
    quarter, quarter_f = shape((Q, D)), shape((Q, D), f32)

    def grad_kernel(body, name, cols, *args, extra=(), scratch=(), send_rows=0, **static):
        if split:
            keep = shape((dp_size // 2, D // dp_size, cols))
            outs = [keep, shape((send_rows, cols)) if send_rows else keep, *extra]
            scratch = [pltpu.VMEM((D, cols), f32), *scratch]
        else:
            outs = [shape((D, cols), f32), *extra]
        res = call(body, name, outs, *args, scratch=scratch, split=split, **static)
        return (res[:2], res[2:]) if split else (res[:1], res[1:])

    def over_x(parts):
        return (parts[0], over_dp(parts[1], 1)) if split else parts

    def first_half(pair):
        return (pair[0][2:].astype(f32) + pair[1][2:].astype(f32)).astype(bf16)

    def second_half(pair, recv):
        return (pair[0][1].astype(f32) + pair[1][1].astype(f32) + recv[1].astype(f32)).astype(bf16)

    def finish(pair, recv, last):
        return pair[0][0].astype(f32) + pair[1][0].astype(f32) + recv[0].astype(f32) + last.astype(f32)

    def scatter(parts):
        return lax.psum_scatter(parts[0], "dp", scatter_dimension=0, tiled=True)

    def columns(total, count):
        width = total.shape[1] // count
        return [total[:, i * width : (i + 1) * width] for i in range(count)]

    ffn_parts, _ = grad_kernel(
        ffn_weights,
        "ffn_weights",
        2 * F,
        g_rows(),
        a_own,
        Part(send3, 0, 1),
        du_own,
        Part(recv_ffn, 0, 1),
        Part(recv_ffn, 1, 1),
        Part(recv_ffn, 2, 1),
        scratch=[pltpu.VMEM((L, F), bf16)],
    )
    own_f = shape((L, W), f32)
    packed = shape((6 * Q, 2 * W))
    turned_f = pltpu.VMEM((2 * W, L), f32)
    if split:
        recv3, ffn_keep = together(recv3, ffn_parts[0])
        ffn_parts = (ffn_keep, ffn_parts[1])
    part4, dx2, send4, do2, ds2, dq2, gain3 = call(
        cross_back,
        "cross_back",
        [half, half_f, shape((2, 2 * Q, D)), both_rows, square, both_rows, line],
        g_rows(),
        part3,
        recv3,
        x2,
        norm_gains,
        cross_w(0, 3),
        k2,
        v2,
        p2,
        h2,
    )
    recv4 = over_mp(part4, 2)
    if split:
        do2, ffn_send = together(do2, ffn_parts[1])
        ffn_parts = (ffn_parts[0], ffn_send)
    recv_h = over_mp(send4, 1)
    dk2, dv2, send_k = call(
        keys_body, "cross_keys", [own_f, own_f, packed], ds2, p2, q2, do2, dq2, o2, scratch=[turned_f, turned_f]
    )
    pair_f, pair = shape((2, Q, D), f32), shape((2, Q, D))
    recv4, dk2 = together(recv4, dk2)
    dx1, gs, dq1, dk1, dv1, send_s, gain23, ds1 = call(
        self_back,
        "self_back",
        [quarter_f, half, both_rows, own_f, own_f, packed, line, square],
        dx2,
        part4,
        recv4,
        x1,
        norm_gains,
        self_w(3),
        k1,
        v1,
        p1,
        q1,
        o1,
        gain3,
        scratch=[pltpu.VMEM((2 * Q, 2 * W), bf16), turned_f, turned_f, pltpu.VMEM((2 * Q, D), f32)],
    )
    recv_s = over_mp(send_s, 1)
    gs_oth = over_mp(gs, 1)
    n = D // dp_size
    send_k, ds1 = together(send_k, ds1)
    recv_k = over_mp(send_k, 1)
    cross_parts, (enc_keep, enc_send, out_keep, out_send) = grad_kernel(
        cross_weights,
        "cross_weights",
        4 * W,
        send4,
        recv_h,
        e_rows(),
        dq2,
        dk2,
        dv2,
        o2,
        recv_k,
        Part(w_cross, W, W),
        Part(w_cross, 2 * W, W),
        a_own,
        Part(send3, 1, 1),
        down,
        x2,
        extra=[pair_f, pair, quarter_f, quarter],
        scratch=[pltpu.VMEM((L, 2 * W), bf16), pltpu.VMEM((2 * Q, D), f32)],
    )
    if split:
        ffn_pair, cross_pair = over_x(ffn_parts), over_x(cross_parts)
        recv_s, cross_keep, ffn_half = together(recv_s, cross_pair[0], first_half(ffn_pair))
        cross_pair = (cross_keep, cross_pair[1])
        ffn_recv = over_dp(ffn_half, 2)
    self_parts, (in_keep, in_send, small) = grad_kernel(
        self_weights,
        "self_weights",
        4 * W,
        h1,
        gs,
        gs_oth,
        o1,
        dq1,
        dk1,
        dv1,
        recv_s,
        Part(w_self, 0, 3 * W),
        norm_gains,
        ds1,
        bucket_line,
        gain23,
        buckets=buckets,
        wide=4 * heads * buckets,
        extra=[pair_f, pair, shape((8, D), f32)],
        scratch=[pltpu.VMEM((L, 3 * W), bf16)],
        send_rows=D // 2 + 16,
    )
    def halves(v):
        high = v.astype(bf16)
        return [high, (v - high.astype(f32)).astype(bf16)]

    def passed_on(keep, recv):
        return (keep[1] + recv[1].astype(f32)).astype(bf16)

    def add_tail(v, tail):
        return v + (tail[:8].astype(f32) + tail[8:].astype(f32))

    if split:
        self_recv = over_dp(self_parts[1], 1)
        in_send, enc_send, ffn_recv = together(in_send, enc_send, ffn_recv)
    in_recv, enc_recv = over_mp(in_send, 1), over_mp(enc_send, 1)
    across = jnp.concatenate([passed_on(in_keep, in_recv), passed_on(enc_keep, enc_recv), out_send])
    across = over_mp(across, 2)
    if split:
        self_recv, in_recv, enc_recv = together(self_recv, in_recv, enc_recv)
        keep, recv = self_parts[0], self_recv
        m = D // 2
        small = add_tail(small, recv[m:])
        tail = halves(small)
        self_total = keep[0].astype(f32) + recv[:n].astype(f32)
        for i in range(1, dp_size // 2):
            block = (keep[i].astype(f32) + recv[i * n : (i + 1) * n].astype(f32)).astype(bf16)
            last = over_dp(jnp.concatenate([block, *tail]), (0, 4, 2, 6)[i])
            self_total = self_total + last[:n].astype(f32)
            small = add_tail(small, last[n:])
        ffn_last = over_dp(second_half(ffn_pair, ffn_recv), 4)
        ffn_total = finish(ffn_pair, ffn_recv, ffn_last)
        cross_recv = over_dp(first_half(cross_pair), 2)
        cross_last = over_dp(second_half(cross_pair, cross_recv), 4)
        small, across, cross_last = together(small, across, cross_last)
        cross_total = finish(cross_pair, cross_recv, cross_last)
    else:
        small = lax.psum(small, "dp")
        ffn_total, cross_total, self_total = map(scatter, (ffn_parts, cross_parts, self_parts))
    grad_up, grad_down = ffn_total[:, :F], ffn_total[:, F:]

    def sum_rows(keep, recv, last):
        return keep[0] + recv[0].astype(f32) + last.astype(f32)

    grad_rows, _ = norm_back(decoder_in[0].astype(f32), norm_gains[0:1], sum_rows(in_keep, in_recv, across[:Q]))
    grad_decoder = (dx1 + grad_rows).astype(bf16)
    grad_encoder = sum_rows(enc_keep, enc_recv, across[Q : 2 * Q]).astype(bf16)
    output = (out_keep + across[2 * Q :].astype(f32)).astype(bf16)

    small = small + over_mp(small, 1)
    small = small + over_mp(small, 2)
    gain_total = small[:3]
    table_total = small[3, : 4 * heads * buckets].reshape(4 * heads, buckets).T
    grad_cq, grad_ck, grad_cv, grad_co = columns(cross_total, 4)
    grad_sq, grad_sk, grad_sv, grad_so = columns(self_total, 4)

    def row(v):
        return v.reshape((1,) + v.shape)

    return (
        row(output),
        row(grad_decoder),
        row(grad_encoder),
        grad_sq,
        grad_sk,
        grad_sv,
        grad_so,
        grad_cq,
        grad_ck,
        grad_cv,
        grad_co,
        grad_up,
        grad_down,
        gain_total,
        table_total,
    )


def solution(mesh):
    rows = P("dp", "mp", None)
    cols = P(None, "mp")
    grads = P("dp", "mp")
    in_specs = (rows, rows, P("dp", None), P("dp", None), P(), P(), cols) + (cols,) * 10 + (rows,)
    out_specs = (rows, rows, rows) + (grads,) * 10 + (P(), P())
    body = functools.partial(local, dp_size=mesh.shape["dp"])
    return jax.shard_map(body, mesh=mesh, in_specs=in_specs, out_specs=out_specs, check_vma=False)
```

```python
import functools

import jax
import jax.numpy as jnp
from jax import lax
from jax.experimental import pallas as pl
from jax.experimental.pallas import tpu as pltpu
from jax.sharding import PartitionSpec as P

HEAD_DIM = 64
epsilon = 1e-06
key_scale = 0.125
masked_score = -1e30
highest = lax.Precision.HIGHEST
bf16 = jnp.bfloat16
f32 = jnp.float32


def dot(a, b):
    return lax.dot_general(a, b, (((1,), (0,)), ((), ())), preferred_element_type=f32)


def dot_nt(a, b):
    return lax.dot_general(a, b, (((1,), (1,)), ((), ())), preferred_element_type=f32)


def dot_tn(a, b):
    return lax.dot_general(a, b, (((0,), (0,)), ((), ())), preferred_element_type=f32)


def norm_parts(rows):
    inv = lax.rsqrt(jnp.mean(rows * rows, axis=-1, keepdims=True) + epsilon)
    return rows * inv, inv


def norm_back(rows, gain, grad):
    unit, inv = norm_parts(rows)
    grad_unit = grad * gain
    grad_rows = inv * (grad_unit - unit * jnp.mean(grad_unit * unit, axis=-1, keepdims=True))
    return grad_rows, jnp.sum(grad * unit, axis=0, keepdims=True)


def at(index, size):
    return pl.ds(pl.multiple_of(index * size, size), size)


def shape(dims, dtype=bf16):
    return jax.ShapeDtypeStruct(dims, dtype)


class Whole:
    def __init__(self, array):
        self.arrays = [array]
        self.scratch = [(array.shape, array.dtype)]
        self.copies = 1

    def plan(self, idx, refs, scr, Q):
        return [(refs[0], scr[0])]

    def view(self, lazy, scr):
        return Late(scr[0], lazy)


class Quarters:
    def __init__(self, pieces, n, first=0):
        self.arrays = list(pieces)
        self.first = first
        d = pieces[0].shape[1]
        self.scratch = [((4 * n, d), pieces[0].dtype)]
        self.copies = 4

    def plan(self, idx, refs, scr, Q):
        y, c = idx[0], idx[1]
        places = (2 * y + c, 2 * (1 - y) + c, 2 * y + 1 - c, 2 * (1 - y) + 1 - c)
        return [(r.at[pl.ds(self.first, Q)], scr[0].at[at(p, Q)]) for r, p in zip(refs, places)]

    def view(self, lazy, scr):
        return Late(scr[0], lazy)


class Joined:
    def __init__(self, own, other, picks, count):
        self.arrays = [own, other]
        self.picks = picks
        self.rows = own.shape[0] // count
        self.scratch = [((2 * self.rows, own.shape[1]), own.dtype) for _ in picks]
        self.copies = 2 * len(picks)

    def plan(self, idx, refs, scr, Q):
        n = self.rows
        out = []
        for s, i in zip(scr, self.picks):
            for half, r in enumerate(refs):
                out.append((r.at[pl.ds(i * n, n)], s.at[pl.ds(half * n, n)]))
        return out

    def view(self, lazy, scr):
        return [Late(s, lazy[2 * i : 2 * i + 2]) for i, s in enumerate(scr)]


class Part:
    def __init__(self, array, first, rows):
        self.arrays = [array]
        self.first, self.rows = first, rows
        self.scratch = [((rows,) + array.shape[1:], array.dtype)]
        self.copies = 1

    def plan(self, idx, refs, scr, Q):
        return [(refs[0].at[pl.ds(self.first, self.rows)], scr[0])]

    def view(self, lazy, scr):
        return Late(scr[0], lazy)


class Late:
    def __init__(self, ref, copies):
        self.ref, self.copies = ref, list(copies)
        self.shape, self.dtype = ref.shape, ref.dtype

    def __getitem__(self, index):
        while self.copies:
            self.copies.pop().wait()
        return self.ref[index]


class Result:
    def __init__(self, ref, copy):
        self.ref, self.copy, self.started = ref, copy, False
        self.shape, self.dtype = ref.shape, ref.dtype

    def __getitem__(self, index):
        return self.ref[index]

    def __setitem__(self, index, value):
        self.ref[index] = value

    def flush(self):
        if not self.started:
            self.copy.start()
            self.started = True


def kernel_call(body, name, outs, *args, scratch=(), Q=128, flops=0):
    specs = [a if not hasattr(a, "dtype") else Whole(a) for a in args]
    arrays = [v for s in specs for v in s.arrays]
    in_scr = [x for s in specs for x in s.scratch]
    n_copies = sum(s.copies for s in specs)

    def whole(*refs):
        refs = list(refs)
        mp, dp = lax.axis_index("mp"), lax.axis_index("dp")
        idx_ref = (mp >> 1, mp & 1, dp & 1, dp >> 1)
        ins = [refs.pop(0) for _ in arrays]
        out_refs = [refs.pop(0) for _ in outs]
        scrs = [refs.pop(0) for _ in in_scr]
        out_scr = [refs.pop(0) for _ in outs]
        in_sem, out_sem = refs.pop(0), refs.pop(0)
        views, sem = [], 0
        for s in specs:
            mine = [ins.pop(0) for _ in s.arrays]
            scr = [scrs.pop(0) for _ in s.scratch]
            copies = []
            for src, dst in s.plan(idx_ref, mine, scr, Q):
                copy = pltpu.make_async_copy(src, dst, in_sem.at[sem])
                copy.start()
                sem += 1
                copies.append(copy)
            views.append((s, copies, scr))
        lates = [s.view(copies, scr) for s, copies, scr in views]
        results = [
            Result(s, pltpu.make_async_copy(s, o, out_sem.at[i]))
            for i, (s, o) in enumerate(zip(out_scr, out_refs))
        ]
        body(idx_ref, *lates, *results, *refs)
        for late in lates:
            for v in late if isinstance(late, list) else [late]:
                while v.copies:
                    v.copies.pop().wait()
        for r in results:
            r.flush()
        for r in results:
            r.copy.wait()

    moved = sum(v.size * v.dtype.itemsize for v in arrays)
    moved += sum(v.size * v.dtype.itemsize for v in outs)
    return pl.pallas_call(
        whole,
        out_shape=outs,
        in_specs=[pl.BlockSpec(memory_space=pl.ANY)] * len(arrays),
        out_specs=[pl.BlockSpec(memory_space=pl.ANY)] * len(outs),
        scratch_shapes=[pltpu.VMEM(d, t) for d, t in in_scr]
        + [pltpu.VMEM(o.shape, o.dtype) for o in outs]
        + [pltpu.SemaphoreType.DMA((n_copies,)), pltpu.SemaphoreType.DMA((len(outs),))]
        + list(scratch),
        compiler_params=pltpu.CompilerParams(vmem_limit_bytes=58 * 1024 * 1024),
        cost_estimate=pl.CostEstimate(flops=flops, bytes_accessed=moved, transcendentals=0),
        name=name,
    )(*arrays)


def pair_masks(dtype):
    lane = lax.broadcasted_iota(jnp.int32, (1, 2 * HEAD_DIM), 1) // HEAD_DIM
    return [(lane == h).astype(f32).astype(dtype) for h in range(2)]


def bucket_rows(bucket_ref, count):
    L = bucket_ref.shape[1]
    return (lax.broadcasted_iota(jnp.int32, (count, L), 0) == bucket_ref[...]).astype(f32)


def backwards(L):
    row = lax.broadcasted_iota(jnp.int32, (L, L), 0)
    col = lax.broadcasted_iota(jnp.int32, (L, L), 1)
    return ((row + col == L) | ((row == 0) & (col == 0))).astype(f32)


def exact_dot(a, b, dims):
    return lax.dot_general(a, b, (dims, ((), ())), precision=highest, preferred_element_type=f32)


def bias_body(idx, to_ref, tp_ref, bucket_ref, segr_ref, enc_ref, near_ref, bias_ref, cross_ref, *, Q):
    core = idx[1]
    L = 4 * Q
    heads, buckets = to_ref.shape
    hot = exact_dot(bucket_rows(bucket_ref, buckets), backwards(L), ((1,), (0,)))
    lines = [exact_dot(t[...], hot, ((1,), (0,))) for t in (to_ref, tp_ref)]
    seg = segr_ref[...]
    columns = jnp.broadcast_to(seg.astype(f32), (Q, L)).T
    for b in range(2):
        rows = pl.ds(b * Q, Q)
        low = columns[2 * b * Q : (2 * b + 1) * Q, 0:1]
        high = columns[(2 * b + 1) * Q : (2 * b + 2) * Q, 0:1]
        segc = jnp.where(core == 0, low, high).astype(jnp.int32)
        cross_ref[rows, :] = jnp.where(segc == enc_ref[...], 0.0, masked_score)
        place = (2 * b + core) * Q + lax.broadcasted_iota(jnp.int32, (Q, L), 0)
        col = lax.broadcasted_iota(jnp.int32, (Q, L), 1)
        allowed = (segc == seg) & (col <= place)
        out, m = (near_ref, 2 * Q) if b == 0 else (bias_ref, L)
        first = lax.broadcasted_iota(jnp.int32, (heads, m), 1) == 0
        for grp in range(2):
            turned = lines[grp] if b else jnp.where(first, lines[grp][:, :m], lines[grp][:, m:])
            turned = pltpu.roll(turned, core * Q + (2 * b * Q) % m, 1)
            for h in range(heads):
                line = jnp.broadcast_to(turned[h : h + 1, :], (Q, m))
                line = pltpu.roll(line, 0, 1, stride=1, stride_axis=0)
                out[grp * heads + h] = jnp.where(allowed[:, :m], line, masked_score)
        out.flush()


def soft_mix(q_ref, k_ref, v_ref, extra, p_ref, o_ref, rows, nk):
    low, wide = pair_masks(bf16), pair_masks(f32)
    keys = pl.ds(0, nk)
    for pair in range(p_ref.shape[0] // 2):
        lanes = pl.ds(pair * 2 * HEAD_DIM, 2 * HEAD_DIM)
        q, k, v = q_ref[rows, lanes], k_ref[keys, lanes], v_ref[keys, lanes]
        mixed = None
        for i in range(2):
            h = 2 * pair + i
            s = dot_nt(q * low[i], k) * key_scale + extra(h)
            top = jnp.max(s, axis=-1, keepdims=True)
            e = jnp.exp(s - top)
            p = (e * (1.0 / jnp.sum(e, axis=-1, keepdims=True))).astype(bf16)
            p_ref[h, rows, keys] = p
            term = dot(p, v) * wide[i]
            mixed = term if mixed is None else mixed + term
        o_ref[rows, lanes] = mixed.astype(bf16)


def self_forward(idx, x_ref, g_ref, w, near_ref, bias_ref, part_ref, h_ref, q_ref, k_ref, v_ref, p_ref, o_ref, *, Q):
    core = idx[1]
    gain = g_ref[0:1, :]
    for t in range(4):
        rows = pl.ds(t * Q, Q)
        unit, _ = norm_parts(x_ref[rows, :].astype(f32))
        h_ref[rows, :] = (unit * gain).astype(bf16)
    h_ref.flush()
    k_ref[...] = dot_nt(h_ref[...], w[1][...]).astype(bf16)
    k_ref.flush()
    v_ref[...] = dot_nt(h_ref[...], w[2][...]).astype(bf16)
    v_ref.flush()
    for b in range(2):
        hb = h_ref[at(2 * b + core, Q), :]
        q_ref[pl.ds(b * Q, Q), :] = dot_nt(hb, w[0][...]).astype(bf16)
    q_ref.flush()
    for i in range(p_ref.shape[0]):
        p_ref[i, pl.ds(0, Q), pl.ds(2 * Q, 2 * Q)] = jnp.zeros((Q, 2 * Q), bf16)
    for b in range(2):
        nk = 2 * Q * (b + 1)
        rows = pl.ds(b * Q, Q)
        soft_mix(q_ref, k_ref, v_ref, (lambda h: bias_ref[h]) if b else (lambda h: near_ref[h]), p_ref, o_ref, rows, nk)
    p_ref.flush()
    o_ref.flush()
    part_ref[...] = dot(o_ref[...], w[3][...]).astype(bf16)


def encoder_keys(idx, e_ref, w, k_ref, v_ref, *, Q):
    k_ref[...] = dot_nt(e_ref[...], w[0][...]).astype(bf16)
    v_ref[...] = dot_nt(e_ref[...], w[1][...]).astype(bf16)


def cross_forward(idx, x_ref, part_ref, recv_ref, g_ref, w, k_ref, v_ref, mask_ref, out_ref, x1_ref, h_ref, q_ref, p_ref, o_ref, *, Q):
    core = idx[1]
    for b in range(2):
        rows = pl.ds(b * Q, Q)
        x1 = x_ref[at(2 * b + core, Q), :].astype(f32) + (
            part_ref[rows, :].astype(f32) + recv_ref[rows, :].astype(f32)
        )
        x1_ref[rows, :] = x1
        unit, _ = norm_parts(x1)
        h_ref[rows, :] = (unit * g_ref[1:2, :]).astype(bf16)
    x1_ref.flush()
    h_ref.flush()
    q_ref[...] = dot_nt(h_ref[...], w[0][...]).astype(bf16)
    q_ref.flush()
    for b in range(2):
        rows = pl.ds(b * Q, Q)
        soft_mix(q_ref, k_ref, v_ref, lambda h: mask_ref[rows, :], p_ref, o_ref, rows, 4 * Q)
    p_ref.flush()
    o_ref.flush()
    out_ref[...] = dot(o_ref[...], w[1][...]).astype(bf16)


gelu_c = 0.7978845608028654
gelu_k = 0.044715


def act_grads(idx, g_ref, w, out_ref, *, Q):
    n = w[0].shape[0] // 2
    core = idx[1]
    for half in range(2):
        for b in range(2):
            out_ref[half, pl.ds(b * Q, Q), :] = dot(
                g_ref[at(2 * b + core, Q), :], w[0][pl.ds(half * n, n), :]
            ).astype(bf16)


def ffn_both(idx, x1_ref, part_ref, recv_ref, g_ref, up, ga_ref, out_ref, x2_ref, a_ref, du_ref, send_ref, *, Q):
    for b in range(2):
        rows = pl.ds(b * Q, Q)
        x2 = x1_ref[rows, :] + (part_ref[rows, :].astype(f32) + recv_ref[rows, :].astype(f32))
        x2_ref[rows, :] = x2
        unit, _ = norm_parts(x2)
        send_ref[0, rows, :] = (unit * g_ref[2:3, :]).astype(bf16)
    x2_ref.flush()
    n = up[0].shape[0] // 2
    for grp in range(2):
        u = dot(send_ref[0], up[0][pl.ds(grp * n, n), :])
        t = jnp.tanh(gelu_c * (u + gelu_k * (u * u * u)))
        half = 0.5 * (1.0 + t)
        a = (u * half).astype(bf16)
        slope = half + 0.5 * u * (1.0 - t * t) * (gelu_c * (1.0 + 3.0 * gelu_k * (u * u)))
        du = (ga_ref[grp].astype(f32) * slope).astype(bf16)
        if grp == 0:
            a_ref[...] = a
            du_ref[...] = du
            a_ref.flush()
            du_ref.flush()
        else:
            send_ref[1] = a
            send_ref[2] = du
            send_ref.flush()
    out_ref[...] = (
        dot_nt(du_ref[...], up[0][pl.ds(0, n), :]) + dot_nt(send_ref[2], up[0][pl.ds(n, n), :])
    ).astype(bf16)


def attend_back(k_ref, v_ref, do_ref, p_ref, ds_ref, dq_ref, rows, nk):
    low, wide = pair_masks(bf16), pair_masks(f32)
    keys = pl.ds(0, nk)
    for pair in range(ds_ref.shape[0] // 2):
        lanes = pl.ds(pair * 2 * HEAD_DIM, 2 * HEAD_DIM)
        go, k, v = do_ref[rows, lanes], k_ref[keys, lanes], v_ref[keys, lanes]
        total = None
        for i in range(2):
            h = 2 * pair + i
            p = p_ref[h, rows, keys].astype(f32)
            gp = dot_nt(go * low[i], v)
            ds = (p * (gp - jnp.sum(p * gp, axis=-1, keepdims=True))).astype(bf16)
            ds_ref[h, rows, keys] = ds
            term = dot(ds, k) * wide[i]
            total = term if total is None else total + term
        dq_ref[rows, lanes] = (total * key_scale).astype(bf16)


def cross_back(idx, gr_ref, part_ref, recv_ref, x2_ref, g_ref, w, k_ref, v_ref, p_ref, h2_ref, out_ref, dx_ref, sendh_ref, do_ref, ds_ref, dq_ref, gain_ref, *, Q):
    core = idx[1]
    total = None
    for b in range(2):
        rows = pl.ds(b * Q, Q)
        dh = part_ref[rows, :].astype(f32) + recv_ref[rows, :].astype(f32)
        grad_rows, grad_gain = norm_back(x2_ref[rows, :], g_ref[2:3, :], dh)
        dx = gr_ref[at(2 * b + core, Q), :].astype(f32) + grad_rows
        dx_ref[rows, :] = dx
        total = grad_gain if total is None else total + grad_gain
        sendh_ref[0, rows, :] = dx.astype(bf16)
    dx_ref.flush()
    do_ref[...] = dot_nt(sendh_ref[0], w[1][...]).astype(bf16)
    do_ref.flush()
    for b in range(2):
        attend_back(k_ref, v_ref, do_ref, p_ref, ds_ref, dq_ref, pl.ds(b * Q, Q), 4 * Q)
    ds_ref.flush()
    dq_ref.flush()
    out_ref[...] = dot(dq_ref[...], w[0][...]).astype(bf16)
    out_ref.flush()
    sendh_ref[1] = h2_ref[...]
    gain_ref[...] = jnp.broadcast_to(total * 0.5, gain_ref.shape)


def key_grads(ds_ref, p_ref, q, go, dkt_ref, dvt_ref):
    qt = q.astype(f32).T.astype(bf16)
    gt = go.astype(f32).T.astype(bf16)
    for h in range(ds_ref.shape[0]):
        rows = pl.ds(h * HEAD_DIM, HEAD_DIM)
        take = slice(h * HEAD_DIM, (h + 1) * HEAD_DIM)
        dkt_ref[rows, :] = dot(qt[take], ds_ref[h]) * key_scale
        dvt_ref[rows, :] = dot(gt[take], p_ref[h])


def pack_keys(dkt_ref, dvt_ref, dq_ref, o_ref, dk_ref, dv_ref, send_ref, Q):
    W = dk_ref.shape[1]
    dk, dv = dkt_ref[...].T, dvt_ref[...].T
    send_ref[pl.ds(0, 4 * Q), 0:W] = dk[:, W:].astype(bf16)
    send_ref[pl.ds(0, 4 * Q), W:] = dv[:, W:].astype(bf16)
    send_ref[pl.ds(4 * Q, 2 * Q), 0:W] = dq_ref[:, W:]
    send_ref[pl.ds(4 * Q, 2 * Q), W:] = o_ref[:, W:]
    send_ref.flush()
    dk_ref[...] = dk[:, :W]
    dv_ref[...] = dv[:, :W]


def keys_body(idx, ds_ref, p_ref, q_ref, do_ref, dq_ref, o_ref, dk_ref, dv_ref, send_ref, dkt_ref, dvt_ref, *, Q):
    key_grads(ds_ref, p_ref, q_ref[...], do_ref[...], dkt_ref, dvt_ref)
    pack_keys(dkt_ref, dvt_ref, dq_ref, o_ref, dk_ref, dv_ref, send_ref, Q)


def self_back(idx, dx_ref, part_ref, recv_ref, x1_ref, g_ref, w, k_ref, v_ref, p_ref, q_ref, o_ref, gain3_ref, dx1_ref, gs_ref, dq_ref, dk_ref, dv_ref, send_ref, gain_ref, ds_ref, do_ref, dkt_ref, dvt_ref, sum_ref, *, Q):
    total = None
    for b in range(2):
        rows = pl.ds(b * Q, Q)
        dh = part_ref[rows, :].astype(f32) + recv_ref[rows, :].astype(f32)
        grad_rows, grad_gain = norm_back(x1_ref[rows, :], g_ref[1:2, :], dh)
        dx = dx_ref[rows, :] + grad_rows
        sum_ref[rows, :] = dx
        total = grad_gain if total is None else total + grad_gain
        gs_ref[rows, :] = dx.astype(bf16)
    gs_ref.flush()
    dx1_ref[...] = sum_ref[at(idx[0], Q), :]
    dx1_ref.flush()
    for i in range(ds_ref.shape[0]):
        ds_ref[i, pl.ds(0, Q), pl.ds(2 * Q, 2 * Q)] = jnp.zeros((Q, 2 * Q), bf16)
    do_ref[...] = dot_nt(gs_ref[...], w[0][...]).astype(bf16)
    for b in range(2):
        attend_back(k_ref, v_ref, do_ref, p_ref, ds_ref, dq_ref, pl.ds(b * Q, Q), 2 * Q * (b + 1))
    ds_ref.flush()
    dq_ref.flush()
    key_grads(ds_ref, p_ref, q_ref[...], do_ref[...], dkt_ref, dvt_ref)
    pack_keys(dkt_ref, dvt_ref, dq_ref, o_ref, dk_ref, dv_ref, send_ref, Q)
    gain_ref[0:1, :] = total * 0.5
    gain_ref[1:, :] = gain3_ref[1:, :]


def table_sums(idx, ds_ref, bucket_ref, Q, buckets, wide):
    y, core = idx[0], idx[1]
    L = 4 * Q
    heads = ds_ref.shape[0]
    lines = []
    for h in range(heads):
        line = ds_ref[h, pl.ds(0, Q), :].astype(f32) + pltpu.roll(
            ds_ref[h, pl.ds(Q, Q), :].astype(f32), L - 2 * Q, 1
        )
        n = Q // 2
        while n >= 1:
            line = line[:n] + pltpu.roll(line[n : 2 * n], L - n, 1)
            n //= 2
        lines.append(line)
    lines.append(jnp.zeros((8 - heads, L), f32))
    lines = pltpu.roll(jnp.concatenate(lines, axis=0), (4 - core) * Q, 1)
    lines = exact_dot(lines, backwards(L), ((1,), (0,)))
    sums = exact_dot(lines, bucket_rows(bucket_ref, buckets), ((1,), (1,)))
    lane = lax.broadcasted_iota(jnp.int32, (buckets, wide), 1)
    spread = (lax.broadcasted_iota(jnp.int32, (buckets, wide), 0) == lane % buckets).astype(f32)
    sums = exact_dot(sums, spread, ((1,), (0,)))
    row = lax.broadcasted_iota(jnp.int32, (8, wide), 0)
    other = (row >= heads // 2).astype(jnp.int32)
    owner = (2 * y + core) * (1 - other) + (2 * y + 1 - core) * other
    head = owner * (heads // 2) + row - other * (heads // 2)
    mine = (row < heads) & (lax.broadcasted_iota(jnp.int32, (8, wide), 1) // buckets == head)
    return jnp.sum(jnp.where(mine, sums, 0.0), axis=0, keepdims=True)


def shares(idx):
    y, core = idx[0], idx[1]
    return (2 * y + core, 2 * (1 - y) + core), (2 * y + 1 - core, 2 * (1 - y) + 1 - core)


def self_weights(idx, h_ref, gs_ref, gsr_ref, o_ref, dq_ref, dk_ref, dv_ref, recv_ref, w_ref, g_ref, ds_ref, bucket_ref, gain23_ref, *rest, Q, split, buckets, wide):
    core = idx[1]
    if split:
        keep_ref, send_ref, in_keep_ref, in_send_ref, small_ref, sum_ref, d_ref = rest
    else:
        sum_ref, in_keep_ref, in_send_ref, small_ref, d_ref = rest
    W = dk_ref.shape[1]
    for b in range(2):
        rows = pl.ds(b * Q, Q)
        d_ref[at(2 * b + core, Q), 0:W] = dq_ref[rows, 0:W]
        d_ref[at(2 * b + 1 - core, Q), 0:W] = recv_ref[pl.ds((4 + b) * Q, Q), 0:W]
    keys = pl.ds(0, 4 * Q)
    d_ref[:, W : 2 * W] = (dk_ref[...] + recv_ref[keys, 0:W].astype(f32)).astype(bf16)
    d_ref[:, 2 * W : 3 * W] = (dv_ref[...] + recv_ref[keys, W:].astype(f32)).astype(bf16)
    total = None
    for out, places in zip((in_keep_ref, in_send_ref), shares(idx)):
        for i, place in enumerate(places):
            rows = at(place, Q)
            grad = dot(d_ref[rows, :], w_ref[...])
            out[i] = grad.astype(out.dtype)
            term = jnp.sum(grad * h_ref[rows, :].astype(f32), axis=0, keepdims=True)
            total = term if total is None else total + term
        out.flush()
    small_ref[...] = jnp.zeros(small_ref.shape, f32)
    small_ref[0:1, :] = total / g_ref[0:1, :]
    small_ref[1:3, :] = gain23_ref[0:2, :]
    small_ref[3:4, 0:wide] = table_sums(idx, ds_ref, bucket_ref, Q, buckets, wide)
    small_ref.flush()
    sum_ref[:, 0 : 3 * W] = dot_tn(h_ref[...], d_ref[...])
    sum_ref[:, 3 * W : 4 * W] = dot_tn(gs_ref[...], o_ref[:, 0:W]) + dot_tn(
        gsr_ref[...], recv_ref[pl.ds(4 * Q, 2 * Q), W:]
    )
    if split:
        last = pl.ds(keep_ref.shape[0] * keep_ref.shape[1], 16)
        small = small_ref[...]
        high = small.astype(bf16)
        send_ref[last, :] = jnp.concatenate([high.astype(f32), small - high.astype(f32)]).astype(bf16)
        split_rows(idx, sum_ref, keep_ref, send_ref)


def split_rows(idx, sum_ref, keep_ref, send_ref):
    x, z_here = idx[2], idx[3]
    n = keep_ref.shape[1]
    places = [lax.bitwise_xor(z_here, i) for i in (0, 2, 1, 3)]
    for i, z in enumerate(places):
        block = sum_ref[at(2 * z + 1 - x, n), :].astype(send_ref.dtype)
        if len(send_ref.shape) == 3:
            send_ref[i] = block
        else:
            send_ref[pl.ds(i * n, n), :] = block
    send_ref.flush()
    for i, z in enumerate(places):
        keep_ref[i] = sum_ref[at(2 * z + x, n), :].astype(keep_ref.dtype)


def cross_weights(idx, sendh_ref, recvh_ref, e_ref, dq_ref, dk_ref, dv_ref, o_ref, recv_ref, wk_ref, wv_ref, a_ref, b_ref, down, x2_ref, *rest, Q, split):
    y = idx[0]
    outs, (d_ref, rows_ref) = list(rest[:-2]), rest[-2:]
    if split:
        keep_ref, send_ref, ekeep_ref, esend_ref, okeep_ref, osend_ref, sum_ref = outs
    else:
        sum_ref, ekeep_ref, esend_ref, okeep_ref, osend_ref = outs
    W = dk_ref.shape[1]
    low, keys = pl.ds(4 * Q, 2 * Q), pl.ds(0, 4 * Q)
    d_ref[:, 0:W] = (dk_ref[...] + recv_ref[keys, 0:W].astype(f32)).astype(bf16)
    d_ref[:, W:] = (dv_ref[...] + recv_ref[keys, W:].astype(f32)).astype(bf16)
    sum_ref[:, W : 3 * W] = dot_tn(e_ref[...], d_ref[...])
    sum_ref[:, 0:W] = dot_tn(sendh_ref[1], dq_ref[:, 0:W]) + dot_tn(recvh_ref[1], recv_ref[low, 0:W])
    sum_ref[:, 3 * W : 4 * W] = dot_tn(sendh_ref[0], o_ref[:, 0:W]) + dot_tn(recvh_ref[0], recv_ref[low, W:])
    if split:
        split_rows(idx, sum_ref, keep_ref, send_ref)
        keep_ref.flush()
    keep, send = shares(idx)
    for out, places in ((esend_ref, send), (ekeep_ref, keep)):
        for i, place in enumerate(places):
            take = d_ref[at(place, Q), :]
            out[i] = (dot(take[:, :W], wk_ref[...]) + dot(take[:, W:], wv_ref[...])).astype(out.dtype)
        out.flush()
    n = down[0].shape[0] // 2
    rows_ref[...] = dot_nt(a_ref[...], down[0][pl.ds(0, n), :]) + dot_nt(b_ref[0], down[0][pl.ds(n, n), :])
    osend_ref[...] = rows_ref[at(1 - y, Q), :].astype(bf16)
    osend_ref.flush()
    okeep_ref[...] = rows_ref[at(y, Q), :] + x2_ref[at(y, Q), :]


def ffn_weights(idx, g_ref, a_ref, h_ref, d_ref, hr_ref, ar_ref, dr_ref, *rest, Q, split):
    core = idx[1]
    F = a_ref.shape[1]
    if split:
        keep_ref, send_ref, sum_ref, all_ref = rest
    else:
        sum_ref, all_ref = rest
    for b in range(2):
        all_ref[at(2 * b + core, Q), :] = a_ref[pl.ds(b * Q, Q), :]
        all_ref[at(2 * b + 1 - core, Q), :] = ar_ref[0, pl.ds(b * Q, Q), :]
    sum_ref[:, F:] = dot_tn(g_ref[...], all_ref[...])
    sum_ref[:, 0:F] = dot_tn(h_ref[0], d_ref[...]) + dot_tn(hr_ref[0], dr_ref[0])
    if split:
        split_rows(idx, sum_ref, keep_ref, send_ref)


def together(*values):
    return lax.optimization_barrier(values)


def local(
    decoder_in,
    encoder_states,
    dec_segments,
    enc_segments,
    offset_buckets,
    norm_gains,
    bias_table,
    self_query,
    self_key,
    self_value,
    self_out,
    cross_query,
    cross_key,
    cross_value,
    cross_out,
    ffn_up,
    ffn_down,
    out_grad,
    dp_size,
):
    Q, D = decoder_in.shape[1:]
    L = 4 * Q
    W = self_query.shape[1]
    F = ffn_up.shape[1]
    heads = bias_table.shape[1]
    buckets = bias_table.shape[0]
    split = dp_size == 8
    mp = lax.axis_index("mp")
    y = mp // 2

    def over_mp(v, flip):
        return lax.ppermute(v, "mp", [(i, i ^ flip) for i in range(4)])

    def over_dp(v, flip):
        return lax.ppermute(v, "dp", [(i, i ^ flip) for i in range(dp_size)])

    def call(body, name, outs, *args, scratch=(), **static):
        static["Q"] = Q
        return kernel_call(functools.partial(body, **static), name, outs, *args, scratch=scratch, Q=Q)

    x_here = decoder_in[0]
    x_core = over_mp(x_here, 1)
    x_across = over_mp(x_here, 2)
    table_p = over_mp(bias_table.T, 1)
    wq, table_p = together(self_query.T, table_p)
    w_self = jnp.concatenate([wq, self_key.T, self_value.T, self_out.T])
    w_self_p = over_mp(w_self, 1)
    bucket_line = offset_buckets.reshape(1, L)
    near_bias, bias, cross_mask = call(
        bias_body,
        "bias",
        [shape((2 * heads, Q, 2 * Q), f32), shape((2 * heads, Q, L), f32), shape((2 * Q, L), f32)],
        bias_table.T,
        table_p,
        bucket_line,
        dec_segments,
        enc_segments,
    )
    x_across, bias = together(x_across, bias)
    x4 = (x_here, x_across, x_core, over_mp(x_across, 1))

    def x_rows():
        return Quarters(x4, Q)

    eg_here = jnp.concatenate([encoder_states[0], out_grad[0]])
    eg_across = over_mp(eg_here, 2)
    w_cross = jnp.concatenate([cross_query.T, cross_key.T, cross_value.T, cross_out.T])

    def e_rows():
        return Quarters(eg4, Q)

    def g_rows():
        return Quarters(eg4, Q, Q)

    def self_w(*picks):
        return Joined(w_self, w_self_p, picks, 4)

    def cross_w(*picks):
        return Joined(w_cross, w_cross_p, picks, 4)

    both_rows, both_all = shape((2 * Q, 2 * W)), shape((L, 2 * W))
    square = shape((2 * heads, 2 * Q, L))
    half = shape((2 * Q, D))
    half_f = shape((2 * Q, D), f32)
    line = shape((8, D), f32)

    part1, h1, q1, k1, v1, p1, o1 = call(
        self_forward,
        "self_forward",
        [half, shape((L, D)), both_rows, both_all, both_all, square, both_rows],
        x_rows(),
        norm_gains,
        self_w(0, 1, 2, 3),
        near_bias,
        bias,
    )
    recv1 = over_mp(part1, 2)
    w_cross_p = over_mp(w_cross, 1)
    eg_across, q1 = together(eg_across, q1)
    eg4 = (eg_here, eg_across, over_mp(eg_here, 1), over_mp(eg_across, 1))
    up = Joined(ffn_up, over_mp(ffn_up, 1), (0,), 1)
    down_p = over_mp(ffn_down, 1)
    k2, v2 = call(encoder_keys, "encoder_keys", [both_all, both_all], e_rows(), cross_w(1, 2))
    part2, x1, h2, q2, p2, o2 = call(
        cross_forward,
        "cross_forward",
        [half, half_f, half, both_rows, square, both_rows],
        x_rows(),
        part1,
        recv1,
        norm_gains,
        cross_w(0, 3),
        k2,
        v2,
        cross_mask,
    )
    recv2 = over_mp(part2, 2)
    down_p, h2 = together(down_p, h2)
    down = Joined(ffn_down, down_p, (0,), 1)
    (grad_act,) = call(act_grads, "act_grads", [shape((2, 2 * Q, F))], g_rows(), down)
    part3, x2, a_own, du_own, send3 = call(
        ffn_both,
        "ffn_both",
        [half, half_f, shape((2 * Q, F)), shape((2 * Q, F)), shape((3, 2 * Q, D))],
        x1,
        part2,
        recv2,
        norm_gains,
        up,
        grad_act,
    )
    recv3 = over_mp(part3, 2)
    recv_ffn = over_mp(send3, 1)
    quarter, quarter_f = shape((Q, D)), shape((Q, D), f32)

    def grad_kernel(body, name, cols, *args, extra=(), scratch=(), send_rows=0, **static):
        if split:
            keep = shape((dp_size // 2, D // dp_size, cols))
            outs = [keep, shape((send_rows, cols)) if send_rows else keep, *extra]
            scratch = [pltpu.VMEM((D, cols), f32), *scratch]
        else:
            outs = [shape((D, cols), f32), *extra]
        res = call(body, name, outs, *args, scratch=scratch, split=split, **static)
        return (res[:2], res[2:]) if split else (res[:1], res[1:])

    def over_x(parts):
        return (parts[0], over_dp(parts[1], 1)) if split else parts

    def first_half(pair):
        return (pair[0][2:].astype(f32) + pair[1][2:].astype(f32)).astype(bf16)

    def second_half(pair, recv):
        return (pair[0][1].astype(f32) + pair[1][1].astype(f32) + recv[1].astype(f32)).astype(bf16)

    def finish(pair, recv, last):
        return pair[0][0].astype(f32) + pair[1][0].astype(f32) + recv[0].astype(f32) + last.astype(f32)

    def scatter(parts):
        return lax.psum_scatter(parts[0], "dp", scatter_dimension=0, tiled=True)

    def columns(total, count):
        width = total.shape[1] // count
        return [total[:, i * width : (i + 1) * width] for i in range(count)]

    ffn_parts, _ = grad_kernel(
        ffn_weights,
        "ffn_weights",
        2 * F,
        g_rows(),
        a_own,
        Part(send3, 0, 1),
        du_own,
        Part(recv_ffn, 0, 1),
        Part(recv_ffn, 1, 1),
        Part(recv_ffn, 2, 1),
        scratch=[pltpu.VMEM((L, F), bf16)],
    )
    own_f = shape((L, W), f32)
    packed = shape((6 * Q, 2 * W))
    turned_f = pltpu.VMEM((2 * W, L), f32)
    if split:
        recv3, ffn_keep = together(recv3, ffn_parts[0])
        ffn_parts = (ffn_keep, ffn_parts[1])
    part4, dx2, send4, do2, ds2, dq2, gain3 = call(
        cross_back,
        "cross_back",
        [half, half_f, shape((2, 2 * Q, D)), both_rows, square, both_rows, line],
        g_rows(),
        part3,
        recv3,
        x2,
        norm_gains,
        cross_w(0, 3),
        k2,
        v2,
        p2,
        h2,
    )
    recv4 = over_mp(part4, 2)
    if split:
        do2, ffn_send = together(do2, ffn_parts[1])
        ffn_parts = (ffn_parts[0], ffn_send)
    recv_h = over_mp(send4, 1)
    dk2, dv2, send_k = call(
        keys_body, "cross_keys", [own_f, own_f, packed], ds2, p2, q2, do2, dq2, o2, scratch=[turned_f, turned_f]
    )
    pair_f, pair = shape((2, Q, D), f32), shape((2, Q, D))
    recv4, dk2 = together(recv4, dk2)
    dx1, gs, dq1, dk1, dv1, send_s, gain23, ds1 = call(
        self_back,
        "self_back",
        [quarter_f, half, both_rows, own_f, own_f, packed, line, square],
        dx2,
        part4,
        recv4,
        x1,
        norm_gains,
        self_w(3),
        k1,
        v1,
        p1,
        q1,
        o1,
        gain3,
        scratch=[pltpu.VMEM((2 * Q, 2 * W), bf16), turned_f, turned_f, pltpu.VMEM((2 * Q, D), f32)],
    )
    recv_s = over_mp(send_s, 1)
    gs_oth = over_mp(gs, 1)
    n = D // dp_size
    send_k, ds1 = together(send_k, ds1)
    recv_k = over_mp(send_k, 1)
    cross_parts, (enc_keep, enc_send, out_keep, out_send) = grad_kernel(
        cross_weights,
        "cross_weights",
        4 * W,
        send4,
        recv_h,
        e_rows(),
        dq2,
        dk2,
        dv2,
        o2,
        recv_k,
        Part(w_cross, W, W),
        Part(w_cross, 2 * W, W),
        a_own,
        Part(send3, 1, 1),
        down,
        x2,
        extra=[pair_f, pair, quarter_f, quarter],
        scratch=[pltpu.VMEM((L, 2 * W), bf16), pltpu.VMEM((2 * Q, D), f32)],
    )
    if split:
        ffn_pair, cross_pair = over_x(ffn_parts), over_x(cross_parts)
        recv_s, cross_keep, ffn_half = together(recv_s, cross_pair[0], first_half(ffn_pair))
        cross_pair = (cross_keep, cross_pair[1])
        ffn_recv = over_dp(ffn_half, 2)
    self_parts, (in_keep, in_send, small) = grad_kernel(
        self_weights,
        "self_weights",
        4 * W,
        h1,
        gs,
        gs_oth,
        o1,
        dq1,
        dk1,
        dv1,
        recv_s,
        Part(w_self, 0, 3 * W),
        norm_gains,
        ds1,
        bucket_line,
        gain23,
        buckets=buckets,
        wide=4 * heads * buckets,
        extra=[pair_f, pair, shape((8, D), f32)],
        scratch=[pltpu.VMEM((L, 3 * W), bf16)],
        send_rows=D // 2 + 16,
    )
    def halves(v):
        high = v.astype(bf16)
        return [high, (v - high.astype(f32)).astype(bf16)]

    def passed_on(keep, recv):
        return (keep[1] + recv[1].astype(f32)).astype(bf16)

    def add_tail(v, tail):
        return v + (tail[:8].astype(f32) + tail[8:].astype(f32))

    if split:
        self_recv = over_dp(self_parts[1], 1)
        in_send, enc_send, ffn_recv = together(in_send, enc_send, ffn_recv)
    in_recv, enc_recv = over_mp(in_send, 1), over_mp(enc_send, 1)
    across = jnp.concatenate([passed_on(in_keep, in_recv), passed_on(enc_keep, enc_recv), out_send])
    across = over_mp(across, 2)
    if split:
        self_recv, in_recv, enc_recv = together(self_recv, in_recv, enc_recv)
        keep, recv = self_parts[0], self_recv
        m = D // 2
        small = add_tail(small, recv[m:])
        tail = halves(small)
        self_total = keep[0].astype(f32) + recv[:n].astype(f32)
        for i in range(1, dp_size // 2):
            block = (keep[i].astype(f32) + recv[i * n : (i + 1) * n].astype(f32)).astype(bf16)
            last = over_dp(jnp.concatenate([block, *tail]), (0, 4, 2, 6)[i])
            self_total = self_total + last[:n].astype(f32)
            small = add_tail(small, last[n:])
        ffn_last = over_dp(second_half(ffn_pair, ffn_recv), 4)
        ffn_total = finish(ffn_pair, ffn_recv, ffn_last)
        cross_recv = over_dp(first_half(cross_pair), 2)
        cross_last = over_dp(second_half(cross_pair, cross_recv), 4)
        small = small + over_mp(small, 1)
        small, across, cross_last = together(small, across, cross_last)
        cross_total = finish(cross_pair, cross_recv, cross_last)
    else:
        small = lax.psum(small, "dp")
        small = small + over_mp(small, 1)
        ffn_total, cross_total, self_total = map(scatter, (ffn_parts, cross_parts, self_parts))
    grad_up, grad_down = ffn_total[:, :F], ffn_total[:, F:]

    def sum_rows(keep, recv, last):
        return keep[0] + recv[0].astype(f32) + last.astype(f32)

    grad_rows, _ = norm_back(decoder_in[0].astype(f32), norm_gains[0:1], sum_rows(in_keep, in_recv, across[:Q]))
    grad_decoder = (dx1 + grad_rows).astype(bf16)
    grad_encoder = sum_rows(enc_keep, enc_recv, across[Q : 2 * Q]).astype(bf16)
    output = (out_keep + across[2 * Q :].astype(f32)).astype(bf16)

    small = small + over_mp(small, 2)
    gain_total = small[:3]
    table_total = small[3, : 4 * heads * buckets].reshape(4 * heads, buckets).T
    grad_cq, grad_ck, grad_cv, grad_co = columns(cross_total, 4)
    grad_sq, grad_sk, grad_sv, grad_so = columns(self_total, 4)

    def row(v):
        return v.reshape((1,) + v.shape)

    return (
        row(output),
        row(grad_decoder),
        row(grad_encoder),
        grad_sq,
        grad_sk,
        grad_sv,
        grad_so,
        grad_cq,
        grad_ck,
        grad_cv,
        grad_co,
        grad_up,
        grad_down,
        gain_total,
        table_total,
    )


def solution(mesh):
    rows = P("dp", "mp", None)
    cols = P(None, "mp")
    grads = P("dp", "mp")
    in_specs = (rows, rows, P("dp", None), P("dp", None), P(), P(), cols) + (cols,) * 10 + (rows,)
    out_specs = (rows, rows, rows) + (grads,) * 10 + (P(), P())
    body = functools.partial(local, dp_size=mesh.shape["dp"])
    return jax.shard_map(body, mesh=mesh, in_specs=in_specs, out_specs=out_specs, check_vma=False)
```

```python
import functools

import jax
import jax.numpy as jnp
from jax import lax
from jax.experimental import pallas as pl
from jax.experimental.pallas import tpu as pltpu
from jax.sharding import PartitionSpec as P

HEAD_DIM = 64
epsilon = 1e-06
key_scale = 0.125
masked_score = -1e30
highest = lax.Precision.HIGHEST
bf16 = jnp.bfloat16
f32 = jnp.float32


def dot(a, b):
    return lax.dot_general(a, b, (((1,), (0,)), ((), ())), preferred_element_type=f32)


def dot_nt(a, b):
    return lax.dot_general(a, b, (((1,), (1,)), ((), ())), preferred_element_type=f32)


def dot_tn(a, b):
    return lax.dot_general(a, b, (((0,), (0,)), ((), ())), preferred_element_type=f32)


def norm_parts(rows):
    inv = lax.rsqrt(jnp.mean(rows * rows, axis=-1, keepdims=True) + epsilon)
    return rows * inv, inv


def norm_back(rows, gain, grad):
    unit, inv = norm_parts(rows)
    grad_unit = grad * gain
    grad_rows = inv * (grad_unit - unit * jnp.mean(grad_unit * unit, axis=-1, keepdims=True))
    return grad_rows, jnp.sum(grad * unit, axis=0, keepdims=True)


def at(index, size):
    return pl.ds(pl.multiple_of(index * size, size), size)


def shape(dims, dtype=bf16):
    return jax.ShapeDtypeStruct(dims, dtype)


class Whole:
    def __init__(self, array):
        self.arrays = [array]
        self.scratch = [(array.shape, array.dtype)]
        self.copies = 1

    def plan(self, idx, refs, scr, Q):
        return [(refs[0], scr[0])]

    def view(self, lazy, scr):
        return Late(scr[0], lazy)


class Quarters:
    def __init__(self, pieces, n, first=0):
        self.arrays = list(pieces)
        self.first = first
        d = pieces[0].shape[1]
        self.scratch = [((4 * n, d), pieces[0].dtype)]
        self.copies = 4

    def plan(self, idx, refs, scr, Q):
        y, c = idx[0], idx[1]
        places = (2 * y + c, 2 * (1 - y) + c, 2 * y + 1 - c, 2 * (1 - y) + 1 - c)
        return [(r.at[pl.ds(self.first, Q)], scr[0].at[at(p, Q)]) for r, p in zip(refs, places)]

    def view(self, lazy, scr):
        return Late(scr[0], lazy)


class Joined:
    def __init__(self, own, other, picks, count):
        self.arrays = [own, other]
        self.picks = picks
        self.rows = own.shape[0] // count
        self.scratch = [((2 * self.rows, own.shape[1]), own.dtype) for _ in picks]
        self.copies = 2 * len(picks)

    def plan(self, idx, refs, scr, Q):
        n = self.rows
        out = []
        for s, i in zip(scr, self.picks):
            for half, r in enumerate(refs):
                out.append((r.at[pl.ds(i * n, n)], s.at[pl.ds(half * n, n)]))
        return out

    def view(self, lazy, scr):
        return [Late(s, lazy[2 * i : 2 * i + 2]) for i, s in enumerate(scr)]


class Part:
    def __init__(self, array, first, rows):
        self.arrays = [array]
        self.first, self.rows = first, rows
        self.scratch = [((rows,) + array.shape[1:], array.dtype)]
        self.copies = 1

    def plan(self, idx, refs, scr, Q):
        return [(refs[0].at[pl.ds(self.first, self.rows)], scr[0])]

    def view(self, lazy, scr):
        return Late(scr[0], lazy)


class Late:
    def __init__(self, ref, copies):
        self.ref, self.copies = ref, list(copies)
        self.shape, self.dtype = ref.shape, ref.dtype

    def __getitem__(self, index):
        while self.copies:
            self.copies.pop().wait()
        return self.ref[index]


class Result:
    def __init__(self, ref, copy):
        self.ref, self.copy, self.started = ref, copy, False
        self.shape, self.dtype = ref.shape, ref.dtype

    def __getitem__(self, index):
        return self.ref[index]

    def __setitem__(self, index, value):
        self.ref[index] = value

    def flush(self):
        if not self.started:
            self.copy.start()
            self.started = True


def kernel_call(body, name, outs, *args, scratch=(), Q=128, flops=0):
    specs = [a if not hasattr(a, "dtype") else Whole(a) for a in args]
    arrays = [v for s in specs for v in s.arrays]
    in_scr = [x for s in specs for x in s.scratch]
    n_copies = sum(s.copies for s in specs)

    def whole(*refs):
        refs = list(refs)
        mp, dp = lax.axis_index("mp"), lax.axis_index("dp")
        idx_ref = (mp >> 1, mp & 1, dp & 1, dp >> 1)
        ins = [refs.pop(0) for _ in arrays]
        out_refs = [refs.pop(0) for _ in outs]
        scrs = [refs.pop(0) for _ in in_scr]
        out_scr = [refs.pop(0) for _ in outs]
        in_sem, out_sem = refs.pop(0), refs.pop(0)
        views, sem = [], 0
        for s in specs:
            mine = [ins.pop(0) for _ in s.arrays]
            scr = [scrs.pop(0) for _ in s.scratch]
            copies = []
            for src, dst in s.plan(idx_ref, mine, scr, Q):
                copy = pltpu.make_async_copy(src, dst, in_sem.at[sem])
                copy.start()
                sem += 1
                copies.append(copy)
            views.append((s, copies, scr))
        lates = [s.view(copies, scr) for s, copies, scr in views]
        results = [
            Result(s, pltpu.make_async_copy(s, o, out_sem.at[i]))
            for i, (s, o) in enumerate(zip(out_scr, out_refs))
        ]
        body(idx_ref, *lates, *results, *refs)
        for late in lates:
            for v in late if isinstance(late, list) else [late]:
                while v.copies:
                    v.copies.pop().wait()
        for r in results:
            r.flush()
        for r in results:
            r.copy.wait()

    moved = sum(v.size * v.dtype.itemsize for v in arrays)
    moved += sum(v.size * v.dtype.itemsize for v in outs)
    return pl.pallas_call(
        whole,
        out_shape=outs,
        in_specs=[pl.BlockSpec(memory_space=pl.ANY)] * len(arrays),
        out_specs=[pl.BlockSpec(memory_space=pl.ANY)] * len(outs),
        scratch_shapes=[pltpu.VMEM(d, t) for d, t in in_scr]
        + [pltpu.VMEM(o.shape, o.dtype) for o in outs]
        + [pltpu.SemaphoreType.DMA((n_copies,)), pltpu.SemaphoreType.DMA((len(outs),))]
        + list(scratch),
        compiler_params=pltpu.CompilerParams(vmem_limit_bytes=54 * 1024 * 1024),
        cost_estimate=pl.CostEstimate(flops=flops, bytes_accessed=moved, transcendentals=0),
        name=name,
    )(*arrays)


def pair_masks(dtype):
    lane = lax.broadcasted_iota(jnp.int32, (1, 2 * HEAD_DIM), 1) // HEAD_DIM
    return [(lane == h).astype(f32).astype(dtype) for h in range(2)]


def bucket_rows(bucket_ref, count):
    L = bucket_ref.shape[1]
    return (lax.broadcasted_iota(jnp.int32, (count, L), 0) == bucket_ref[...]).astype(f32)


def backwards(L):
    row = lax.broadcasted_iota(jnp.int32, (L, L), 0)
    col = lax.broadcasted_iota(jnp.int32, (L, L), 1)
    return ((row + col == L) | ((row == 0) & (col == 0))).astype(f32)


def exact_dot(a, b, dims):
    return lax.dot_general(a, b, (dims, ((), ())), precision=highest, preferred_element_type=f32)


def bias_body(idx, to_ref, tp_ref, bucket_ref, segr_ref, enc_ref, near_ref, bias_ref, cross_ref, *, Q):
    core = idx[1]
    L = 4 * Q
    heads, buckets = to_ref.shape
    hot = exact_dot(bucket_rows(bucket_ref, buckets), backwards(L), ((1,), (0,)))
    lines = [exact_dot(t[...], hot, ((1,), (0,))) for t in (to_ref, tp_ref)]
    seg = segr_ref[...]
    columns = jnp.broadcast_to(seg.astype(f32), (Q, L)).T
    for b in range(2):
        rows = pl.ds(b * Q, Q)
        low = columns[2 * b * Q : (2 * b + 1) * Q, 0:1]
        high = columns[(2 * b + 1) * Q : (2 * b + 2) * Q, 0:1]
        segc = jnp.where(core == 0, low, high).astype(jnp.int32)
        cross_ref[rows, :] = jnp.where(segc == enc_ref[...], 0.0, masked_score)
        place = (2 * b + core) * Q + lax.broadcasted_iota(jnp.int32, (Q, L), 0)
        col = lax.broadcasted_iota(jnp.int32, (Q, L), 1)
        allowed = (segc == seg) & (col <= place)
        out, m = (near_ref, 2 * Q) if b == 0 else (bias_ref, L)
        first = lax.broadcasted_iota(jnp.int32, (heads, m), 1) == 0
        for grp in range(2):
            turned = lines[grp] if b else jnp.where(first, lines[grp][:, :m], lines[grp][:, m:])
            turned = pltpu.roll(turned, core * Q + (2 * b * Q) % m, 1)
            for h in range(heads):
                line = jnp.broadcast_to(turned[h : h + 1, :], (Q, m))
                line = pltpu.roll(line, 0, 1, stride=1, stride_axis=0)
                out[grp * heads + h] = jnp.where(allowed[:, :m], line, masked_score)
        out.flush()


def soft_mix(q_ref, k_ref, v_ref, extra, p_ref, o_ref, rows, nk):
    low, wide = pair_masks(bf16), pair_masks(f32)
    keys = pl.ds(0, nk)
    for pair in range(p_ref.shape[0] // 2):
        lanes = pl.ds(pair * 2 * HEAD_DIM, 2 * HEAD_DIM)
        q, k, v = q_ref[rows, lanes], k_ref[keys, lanes], v_ref[keys, lanes]
        mixed = None
        for i in range(2):
            h = 2 * pair + i
            s = dot_nt(q * low[i], k) * key_scale + extra(h)
            top = jnp.max(s, axis=-1, keepdims=True)
            e = jnp.exp(s - top)
            p = (e * (1.0 / jnp.sum(e, axis=-1, keepdims=True))).astype(bf16)
            p_ref[h, rows, keys] = p
            term = dot(p, v) * wide[i]
            mixed = term if mixed is None else mixed + term
        o_ref[rows, lanes] = mixed.astype(bf16)


def self_forward(idx, x_ref, g_ref, w, near_ref, bias_ref, part_ref, h_ref, q_ref, k_ref, v_ref, p_ref, o_ref, *, Q):
    core = idx[1]
    gain = g_ref[0:1, :]
    for t in range(4):
        rows = pl.ds(t * Q, Q)
        unit, _ = norm_parts(x_ref[rows, :].astype(f32))
        h_ref[rows, :] = (unit * gain).astype(bf16)
    h_ref.flush()
    k_ref[...] = dot_nt(h_ref[...], w[1][...]).astype(bf16)
    k_ref.flush()
    v_ref[...] = dot_nt(h_ref[...], w[2][...]).astype(bf16)
    v_ref.flush()
    for b in range(2):
        hb = h_ref[at(2 * b + core, Q), :]
        q_ref[pl.ds(b * Q, Q), :] = dot_nt(hb, w[0][...]).astype(bf16)
    q_ref.flush()
    for i in range(p_ref.shape[0]):
        p_ref[i, pl.ds(0, Q), pl.ds(2 * Q, 2 * Q)] = jnp.zeros((Q, 2 * Q), bf16)
    for b in range(2):
        nk = 2 * Q * (b + 1)
        rows = pl.ds(b * Q, Q)
        soft_mix(q_ref, k_ref, v_ref, (lambda h: bias_ref[h]) if b else (lambda h: near_ref[h]), p_ref, o_ref, rows, nk)
    p_ref.flush()
    o_ref.flush()
    part_ref[...] = dot(o_ref[...], w[3][...]).astype(bf16)


def encoder_keys(idx, e_ref, w, k_ref, v_ref, *, Q):
    k_ref[...] = dot_nt(e_ref[...], w[0][...]).astype(bf16)
    v_ref[...] = dot_nt(e_ref[...], w[1][...]).astype(bf16)


def cross_forward(idx, x_ref, part_ref, recv_ref, g_ref, w, k_ref, v_ref, mask_ref, out_ref, x1_ref, h_ref, q_ref, p_ref, o_ref, *, Q):
    core = idx[1]
    for b in range(2):
        rows = pl.ds(b * Q, Q)
        x1 = x_ref[at(2 * b + core, Q), :].astype(f32) + (
            part_ref[rows, :].astype(f32) + recv_ref[rows, :].astype(f32)
        )
        x1_ref[rows, :] = x1
        unit, _ = norm_parts(x1)
        h_ref[rows, :] = (unit * g_ref[1:2, :]).astype(bf16)
    x1_ref.flush()
    h_ref.flush()
    q_ref[...] = dot_nt(h_ref[...], w[0][...]).astype(bf16)
    q_ref.flush()
    for b in range(2):
        rows = pl.ds(b * Q, Q)
        soft_mix(q_ref, k_ref, v_ref, lambda h: mask_ref[rows, :], p_ref, o_ref, rows, 4 * Q)
    p_ref.flush()
    o_ref.flush()
    out_ref[...] = dot(o_ref[...], w[1][...]).astype(bf16)


gelu_c = 0.7978845608028654
gelu_k = 0.044715


def act_grads(idx, g_ref, w, out_ref, *, Q):
    n = w[0].shape[0] // 2
    core = idx[1]
    for half in range(2):
        for b in range(2):
            out_ref[half, pl.ds(b * Q, Q), :] = dot(
                g_ref[at(2 * b + core, Q), :], w[0][pl.ds(half * n, n), :]
            ).astype(bf16)


def ffn_both(idx, x1_ref, part_ref, recv_ref, g_ref, up, ga_ref, out_ref, x2_ref, a_ref, du_ref, send_ref, *, Q):
    for b in range(2):
        rows = pl.ds(b * Q, Q)
        x2 = x1_ref[rows, :] + (part_ref[rows, :].astype(f32) + recv_ref[rows, :].astype(f32))
        x2_ref[rows, :] = x2
        unit, _ = norm_parts(x2)
        send_ref[0, rows, :] = (unit * g_ref[2:3, :]).astype(bf16)
    x2_ref.flush()
    n = up[0].shape[0] // 2
    for grp in range(2):
        u = dot(send_ref[0], up[0][pl.ds(grp * n, n), :])
        t = jnp.tanh(gelu_c * (u + gelu_k * (u * u * u)))
        half = 0.5 * (1.0 + t)
        a = (u * half).astype(bf16)
        slope = half + 0.5 * u * (1.0 - t * t) * (gelu_c * (1.0 + 3.0 * gelu_k * (u * u)))
        du = (ga_ref[grp].astype(f32) * slope).astype(bf16)
        if grp == 0:
            a_ref[...] = a
            du_ref[...] = du
            a_ref.flush()
            du_ref.flush()
        else:
            send_ref[1] = a
            send_ref[2] = du
            send_ref.flush()
    out_ref[...] = (
        dot_nt(du_ref[...], up[0][pl.ds(0, n), :]) + dot_nt(send_ref[2], up[0][pl.ds(n, n), :])
    ).astype(bf16)


def attend_back(k_ref, v_ref, do_ref, p_ref, ds_ref, dq_ref, rows, nk):
    low, wide = pair_masks(bf16), pair_masks(f32)
    keys = pl.ds(0, nk)
    for pair in range(ds_ref.shape[0] // 2):
        lanes = pl.ds(pair * 2 * HEAD_DIM, 2 * HEAD_DIM)
        go, k, v = do_ref[rows, lanes], k_ref[keys, lanes], v_ref[keys, lanes]
        total = None
        for i in range(2):
            h = 2 * pair + i
            p = p_ref[h, rows, keys].astype(f32)
            gp = dot_nt(go * low[i], v)
            ds = (p * (gp - jnp.sum(p * gp, axis=-1, keepdims=True))).astype(bf16)
            ds_ref[h, rows, keys] = ds
            term = dot(ds, k) * wide[i]
            total = term if total is None else total + term
        dq_ref[rows, lanes] = (total * key_scale).astype(bf16)


def cross_back(idx, gr_ref, part_ref, recv_ref, x2_ref, g_ref, w, k_ref, v_ref, p_ref, h2_ref, out_ref, dx_ref, sendh_ref, do_ref, ds_ref, dq_ref, gain_ref, *, Q):
    core = idx[1]
    total = None
    for b in range(2):
        rows = pl.ds(b * Q, Q)
        dh = part_ref[rows, :].astype(f32) + recv_ref[rows, :].astype(f32)
        grad_rows, grad_gain = norm_back(x2_ref[rows, :], g_ref[2:3, :], dh)
        dx = gr_ref[at(2 * b + core, Q), :].astype(f32) + grad_rows
        dx_ref[rows, :] = dx
        total = grad_gain if total is None else total + grad_gain
        sendh_ref[0, rows, :] = dx.astype(bf16)
    dx_ref.flush()
    do_ref[...] = dot_nt(sendh_ref[0], w[1][...]).astype(bf16)
    do_ref.flush()
    for b in range(2):
        attend_back(k_ref, v_ref, do_ref, p_ref, ds_ref, dq_ref, pl.ds(b * Q, Q), 4 * Q)
    ds_ref.flush()
    dq_ref.flush()
    out_ref[...] = dot(dq_ref[...], w[0][...]).astype(bf16)
    out_ref.flush()
    sendh_ref[1] = h2_ref[...]
    gain_ref[...] = jnp.broadcast_to(total * 0.5, gain_ref.shape)


def key_grads(ds_ref, p_ref, q, go, dkt_ref, dvt_ref):
    qt = q.astype(f32).T.astype(bf16)
    gt = go.astype(f32).T.astype(bf16)
    for h in range(ds_ref.shape[0]):
        rows = pl.ds(h * HEAD_DIM, HEAD_DIM)
        take = slice(h * HEAD_DIM, (h + 1) * HEAD_DIM)
        dkt_ref[rows, :] = dot(qt[take], ds_ref[h]) * key_scale
        dvt_ref[rows, :] = dot(gt[take], p_ref[h])


def pack_keys(dkt_ref, dvt_ref, dq_ref, o_ref, dk_ref, dv_ref, send_ref, Q):
    W = dk_ref.shape[1]
    dk, dv = dkt_ref[...].T, dvt_ref[...].T
    send_ref[pl.ds(0, 4 * Q), 0:W] = dk[:, W:].astype(bf16)
    send_ref[pl.ds(0, 4 * Q), W:] = dv[:, W:].astype(bf16)
    send_ref[pl.ds(4 * Q, 2 * Q), 0:W] = dq_ref[:, W:]
    send_ref[pl.ds(4 * Q, 2 * Q), W:] = o_ref[:, W:]
    send_ref.flush()
    dk_ref[...] = dk[:, :W]
    dv_ref[...] = dv[:, :W]


def keys_body(idx, ds_ref, p_ref, q_ref, do_ref, dq_ref, o_ref, dk_ref, dv_ref, send_ref, dkt_ref, dvt_ref, *, Q):
    key_grads(ds_ref, p_ref, q_ref[...], do_ref[...], dkt_ref, dvt_ref)
    pack_keys(dkt_ref, dvt_ref, dq_ref, o_ref, dk_ref, dv_ref, send_ref, Q)


def self_back(idx, dx_ref, part_ref, recv_ref, x1_ref, g_ref, w, k_ref, v_ref, p_ref, q_ref, o_ref, gain3_ref, dx1_ref, gs_ref, dq_ref, dk_ref, dv_ref, send_ref, gain_ref, ds_ref, do_ref, dkt_ref, dvt_ref, sum_ref, *, Q):
    total = None
    for b in range(2):
        rows = pl.ds(b * Q, Q)
        dh = part_ref[rows, :].astype(f32) + recv_ref[rows, :].astype(f32)
        grad_rows, grad_gain = norm_back(x1_ref[rows, :], g_ref[1:2, :], dh)
        dx = dx_ref[rows, :] + grad_rows
        sum_ref[rows, :] = dx
        total = grad_gain if total is None else total + grad_gain
        gs_ref[rows, :] = dx.astype(bf16)
    gs_ref.flush()
    dx1_ref[...] = sum_ref[at(idx[0], Q), :]
    dx1_ref.flush()
    for i in range(ds_ref.shape[0]):
        ds_ref[i, pl.ds(0, Q), pl.ds(2 * Q, 2 * Q)] = jnp.zeros((Q, 2 * Q), bf16)
    do_ref[...] = dot_nt(gs_ref[...], w[0][...]).astype(bf16)
    for b in range(2):
        attend_back(k_ref, v_ref, do_ref, p_ref, ds_ref, dq_ref, pl.ds(b * Q, Q), 2 * Q * (b + 1))
    ds_ref.flush()
    dq_ref.flush()
    key_grads(ds_ref, p_ref, q_ref[...], do_ref[...], dkt_ref, dvt_ref)
    pack_keys(dkt_ref, dvt_ref, dq_ref, o_ref, dk_ref, dv_ref, send_ref, Q)
    gain_ref[0:1, :] = total * 0.5
    gain_ref[1:, :] = gain3_ref[1:, :]


def table_sums(idx, ds_ref, bucket_ref, Q, buckets, wide):
    y, core = idx[0], idx[1]
    L = 4 * Q
    heads = ds_ref.shape[0]
    lines = []
    for h in range(heads):
        line = ds_ref[h, pl.ds(0, Q), :].astype(f32) + pltpu.roll(
            ds_ref[h, pl.ds(Q, Q), :].astype(f32), L - 2 * Q, 1
        )
        n = Q // 2
        while n >= 1:
            line = line[:n] + pltpu.roll(line[n : 2 * n], L - n, 1)
            n //= 2
        lines.append(line)
    lines.append(jnp.zeros((8 - heads, L), f32))
    lines = pltpu.roll(jnp.concatenate(lines, axis=0), (4 - core) * Q, 1)
    lines = exact_dot(lines, backwards(L), ((1,), (0,)))
    sums = exact_dot(lines, bucket_rows(bucket_ref, buckets), ((1,), (1,)))
    lane = lax.broadcasted_iota(jnp.int32, (buckets, wide), 1)
    spread = (lax.broadcasted_iota(jnp.int32, (buckets, wide), 0) == lane % buckets).astype(f32)
    sums = exact_dot(sums, spread, ((1,), (0,)))
    row = lax.broadcasted_iota(jnp.int32, (8, wide), 0)
    other = (row >= heads // 2).astype(jnp.int32)
    owner = (2 * y + core) * (1 - other) + (2 * y + 1 - core) * other
    head = owner * (heads // 2) + row - other * (heads // 2)
    mine = (row < heads) & (lax.broadcasted_iota(jnp.int32, (8, wide), 1) // buckets == head)
    return jnp.sum(jnp.where(mine, sums, 0.0), axis=0, keepdims=True)


def shares(idx):
    y, core = idx[0], idx[1]
    return (2 * y + core, 2 * (1 - y) + core), (2 * y + 1 - core, 2 * (1 - y) + 1 - core)


def self_weights(idx, h_ref, gs_ref, gsr_ref, o_ref, dq_ref, dk_ref, dv_ref, recv_ref, w_ref, g_ref, ds_ref, bucket_ref, gain23_ref, *rest, Q, split, buckets, wide):
    core = idx[1]
    if split:
        keep_ref, send_ref, in_keep_ref, in_send_ref, small_ref, sum_ref, d_ref = rest
    else:
        sum_ref, in_keep_ref, in_send_ref, small_ref, d_ref = rest
    W = dk_ref.shape[1]
    for b in range(2):
        rows = pl.ds(b * Q, Q)
        d_ref[at(2 * b + core, Q), 0:W] = dq_ref[rows, 0:W]
        d_ref[at(2 * b + 1 - core, Q), 0:W] = recv_ref[pl.ds((4 + b) * Q, Q), 0:W]
    keys = pl.ds(0, 4 * Q)
    d_ref[:, W : 2 * W] = (dk_ref[...] + recv_ref[keys, 0:W].astype(f32)).astype(bf16)
    d_ref[:, 2 * W : 3 * W] = (dv_ref[...] + recv_ref[keys, W:].astype(f32)).astype(bf16)
    total = None
    for out, places in zip((in_keep_ref, in_send_ref), shares(idx)):
        for i, place in enumerate(places):
            rows = at(place, Q)
            grad = dot(d_ref[rows, :], w_ref[...])
            out[i] = grad.astype(out.dtype)
            term = jnp.sum(grad * h_ref[rows, :].astype(f32), axis=0, keepdims=True)
            total = term if total is None else total + term
        out.flush()
    small_ref[...] = jnp.zeros(small_ref.shape, f32)
    small_ref[0:1, :] = total / g_ref[0:1, :]
    small_ref[1:3, :] = gain23_ref[0:2, :]
    small_ref[3:4, 0:wide] = table_sums(idx, ds_ref, bucket_ref, Q, buckets, wide)
    small_ref.flush()
    sum_ref[:, 0 : 3 * W] = dot_tn(h_ref[...], d_ref[...])
    sum_ref[:, 3 * W : 4 * W] = dot_tn(gs_ref[...], o_ref[:, 0:W]) + dot_tn(
        gsr_ref[...], recv_ref[pl.ds(4 * Q, 2 * Q), W:]
    )
    if split:
        last = pl.ds(keep_ref.shape[0] * keep_ref.shape[1], 16)
        small = small_ref[...]
        high = small.astype(bf16)
        send_ref[last, :] = jnp.concatenate([high.astype(f32), small - high.astype(f32)]).astype(bf16)
        split_rows(idx, sum_ref, keep_ref, send_ref)


def split_rows(idx, sum_ref, keep_ref, send_ref):
    x, z_here = idx[2], idx[3]
    n = keep_ref.shape[1]
    places = [lax.bitwise_xor(z_here, i) for i in (0, 2, 1, 3)]
    for i, z in enumerate(places):
        block = sum_ref[at(2 * z + 1 - x, n), :].astype(send_ref.dtype)
        if len(send_ref.shape) == 3:
            send_ref[i] = block
        else:
            send_ref[pl.ds(i * n, n), :] = block
    send_ref.flush()
    for i, z in enumerate(places):
        keep_ref[i] = sum_ref[at(2 * z + x, n), :].astype(keep_ref.dtype)


def cross_weights(idx, sendh_ref, recvh_ref, e_ref, dq_ref, dk_ref, dv_ref, o_ref, recv_ref, wk_ref, wv_ref, a_ref, b_ref, down, x2_ref, *rest, Q, split):
    y = idx[0]
    outs, (d_ref, rows_ref) = list(rest[:-2]), rest[-2:]
    if split:
        keep_ref, send_ref, ekeep_ref, esend_ref, okeep_ref, osend_ref, sum_ref = outs
    else:
        sum_ref, ekeep_ref, esend_ref, okeep_ref, osend_ref = outs
    W = dk_ref.shape[1]
    low, keys = pl.ds(4 * Q, 2 * Q), pl.ds(0, 4 * Q)
    d_ref[:, 0:W] = (dk_ref[...] + recv_ref[keys, 0:W].astype(f32)).astype(bf16)
    d_ref[:, W:] = (dv_ref[...] + recv_ref[keys, W:].astype(f32)).astype(bf16)
    sum_ref[:, W : 3 * W] = dot_tn(e_ref[...], d_ref[...])
    sum_ref[:, 0:W] = dot_tn(sendh_ref[1], dq_ref[:, 0:W]) + dot_tn(recvh_ref[1], recv_ref[low, 0:W])
    sum_ref[:, 3 * W : 4 * W] = dot_tn(sendh_ref[0], o_ref[:, 0:W]) + dot_tn(recvh_ref[0], recv_ref[low, W:])
    if split:
        split_rows(idx, sum_ref, keep_ref, send_ref)
        keep_ref.flush()
    keep, send = shares(idx)
    for out, places in ((esend_ref, send), (ekeep_ref, keep)):
        for i, place in enumerate(places):
            take = d_ref[at(place, Q), :]
            out[i] = (dot(take[:, :W], wk_ref[...]) + dot(take[:, W:], wv_ref[...])).astype(out.dtype)
        out.flush()
    n = down[0].shape[0] // 2
    rows_ref[...] = dot_nt(a_ref[...], down[0][pl.ds(0, n), :]) + dot_nt(b_ref[0], down[0][pl.ds(n, n), :])
    osend_ref[...] = rows_ref[at(1 - y, Q), :].astype(bf16)
    osend_ref.flush()
    okeep_ref[...] = rows_ref[at(y, Q), :] + x2_ref[at(y, Q), :]


def ffn_weights(idx, g_ref, a_ref, h_ref, d_ref, hr_ref, ar_ref, dr_ref, *rest, Q, split):
    core = idx[1]
    F = a_ref.shape[1]
    if split:
        keep_ref, send_ref, sum_ref, all_ref = rest
    else:
        sum_ref, all_ref = rest
    for b in range(2):
        all_ref[at(2 * b + core, Q), :] = a_ref[pl.ds(b * Q, Q), :]
        all_ref[at(2 * b + 1 - core, Q), :] = ar_ref[0, pl.ds(b * Q, Q), :]
    sum_ref[:, F:] = dot_tn(g_ref[...], all_ref[...])
    sum_ref[:, 0:F] = dot_tn(h_ref[0], d_ref[...]) + dot_tn(hr_ref[0], dr_ref[0])
    if split:
        split_rows(idx, sum_ref, keep_ref, send_ref)


def together(*values):
    return lax.optimization_barrier(values)


def local(
    decoder_in,
    encoder_states,
    dec_segments,
    enc_segments,
    offset_buckets,
    norm_gains,
    bias_table,
    self_query,
    self_key,
    self_value,
    self_out,
    cross_query,
    cross_key,
    cross_value,
    cross_out,
    ffn_up,
    ffn_down,
    out_grad,
    dp_size,
):
    Q, D = decoder_in.shape[1:]
    L = 4 * Q
    W = self_query.shape[1]
    F = ffn_up.shape[1]
    heads = bias_table.shape[1]
    buckets = bias_table.shape[0]
    split = dp_size == 8
    mp = lax.axis_index("mp")
    y = mp // 2

    def over_mp(v, flip):
        return lax.ppermute(v, "mp", [(i, i ^ flip) for i in range(4)])

    def over_dp(v, flip):
        return lax.ppermute(v, "dp", [(i, i ^ flip) for i in range(dp_size)])

    def call(body, name, outs, *args, scratch=(), **static):
        static["Q"] = Q
        return kernel_call(functools.partial(body, **static), name, outs, *args, scratch=scratch, Q=Q)

    x_here = decoder_in[0]
    x_core = over_mp(x_here, 1)
    x_across = over_mp(x_here, 2)
    table_p = over_mp(bias_table.T, 1)
    wq, table_p = together(self_query.T, table_p)
    w_self = jnp.concatenate([wq, self_key.T, self_value.T, self_out.T])
    w_self_p = over_mp(w_self, 1)
    bucket_line = offset_buckets.reshape(1, L)
    near_bias, bias, cross_mask = call(
        bias_body,
        "bias",
        [shape((2 * heads, Q, 2 * Q), f32), shape((2 * heads, Q, L), f32), shape((2 * Q, L), f32)],
        bias_table.T,
        table_p,
        bucket_line,
        dec_segments,
        enc_segments,
    )
    x_across, bias = together(x_across, bias)
    x4 = (x_here, x_across, x_core, over_mp(x_across, 1))

    def x_rows():
        return Quarters(x4, Q)

    eg_here = jnp.concatenate([encoder_states[0], out_grad[0]])
    eg_across = over_mp(eg_here, 2)
    w_cross = jnp.concatenate([cross_query.T, cross_key.T, cross_value.T, cross_out.T])

    def e_rows():
        return Quarters(eg4, Q)

    def g_rows():
        return Quarters(eg4, Q, Q)

    def self_w(*picks):
        return Joined(w_self, w_self_p, picks, 4)

    def cross_w(*picks):
        return Joined(w_cross, w_cross_p, picks, 4)

    both_rows, both_all = shape((2 * Q, 2 * W)), shape((L, 2 * W))
    square = shape((2 * heads, 2 * Q, L))
    half = shape((2 * Q, D))
    half_f = shape((2 * Q, D), f32)
    line = shape((8, D), f32)

    part1, h1, q1, k1, v1, p1, o1 = call(
        self_forward,
        "self_forward",
        [half, shape((L, D)), both_rows, both_all, both_all, square, both_rows],
        x_rows(),
        norm_gains,
        self_w(0, 1, 2, 3),
        near_bias,
        bias,
    )
    recv1 = over_mp(part1, 2)
    w_cross_p = over_mp(w_cross, 1)
    eg_across, q1 = together(eg_across, q1)
    eg4 = (eg_here, eg_across, over_mp(eg_here, 1), over_mp(eg_across, 1))
    up = Joined(ffn_up, over_mp(ffn_up, 1), (0,), 1)
    down_p = over_mp(ffn_down, 1)
    k2, v2 = call(encoder_keys, "encoder_keys", [both_all, both_all], e_rows(), cross_w(1, 2))
    part2, x1, h2, q2, p2, o2 = call(
        cross_forward,
        "cross_forward",
        [half, half_f, half, both_rows, square, both_rows],
        x_rows(),
        part1,
        recv1,
        norm_gains,
        cross_w(0, 3),
        k2,
        v2,
        cross_mask,
    )
    recv2 = over_mp(part2, 2)
    down_p, h2 = together(down_p, h2)
    down = Joined(ffn_down, down_p, (0,), 1)
    (grad_act,) = call(act_grads, "act_grads", [shape((2, 2 * Q, F))], g_rows(), down)
    part3, x2, a_own, du_own, send3 = call(
        ffn_both,
        "ffn_both",
        [half, half_f, shape((2 * Q, F)), shape((2 * Q, F)), shape((3, 2 * Q, D))],
        x1,
        part2,
        recv2,
        norm_gains,
        up,
        grad_act,
    )
    recv3 = over_mp(part3, 2)
    recv_ffn = over_mp(send3, 1)
    quarter, quarter_f = shape((Q, D)), shape((Q, D), f32)

    def grad_kernel(body, name, cols, *args, extra=(), scratch=(), send_rows=0, **static):
        if split:
            keep = shape((dp_size // 2, D // dp_size, cols))
            outs = [keep, shape((send_rows, cols)) if send_rows else keep, *extra]
            scratch = [pltpu.VMEM((D, cols), f32), *scratch]
        else:
            outs = [shape((D, cols), f32), *extra]
        res = call(body, name, outs, *args, scratch=scratch, split=split, **static)
        return (res[:2], res[2:]) if split else (res[:1], res[1:])

    def over_x(parts):
        return (parts[0], over_dp(parts[1], 1)) if split else parts

    def first_half(pair):
        return (pair[0][2:].astype(f32) + pair[1][2:].astype(f32)).astype(bf16)

    def second_half(pair, recv):
        return (pair[0][1].astype(f32) + pair[1][1].astype(f32) + recv[1].astype(f32)).astype(bf16)

    def finish(pair, recv, last):
        return pair[0][0].astype(f32) + pair[1][0].astype(f32) + recv[0].astype(f32) + last.astype(f32)

    def scatter(parts):
        return lax.psum_scatter(parts[0], "dp", scatter_dimension=0, tiled=True)

    def columns(total, count):
        width = total.shape[1] // count
        return [total[:, i * width : (i + 1) * width] for i in range(count)]

    ffn_parts, _ = grad_kernel(
        ffn_weights,
        "ffn_weights",
        2 * F,
        g_rows(),
        a_own,
        Part(send3, 0, 1),
        du_own,
        Part(recv_ffn, 0, 1),
        Part(recv_ffn, 1, 1),
        Part(recv_ffn, 2, 1),
        scratch=[pltpu.VMEM((L, F), bf16)],
    )
    own_f = shape((L, W), f32)
    packed = shape((6 * Q, 2 * W))
    turned_f = pltpu.VMEM((2 * W, L), f32)
    if split:
        recv3, ffn_keep = together(recv3, ffn_parts[0])
        ffn_parts = (ffn_keep, ffn_parts[1])
    part4, dx2, send4, do2, ds2, dq2, gain3 = call(
        cross_back,
        "cross_back",
        [half, half_f, shape((2, 2 * Q, D)), both_rows, square, both_rows, line],
        g_rows(),
        part3,
        recv3,
        x2,
        norm_gains,
        cross_w(0, 3),
        k2,
        v2,
        p2,
        h2,
    )
    recv4 = over_mp(part4, 2)
    if split:
        do2, ffn_send = together(do2, ffn_parts[1])
        ffn_parts = (ffn_parts[0], ffn_send)
    recv_h = over_mp(send4, 1)
    dk2, dv2, send_k = call(
        keys_body, "cross_keys", [own_f, own_f, packed], ds2, p2, q2, do2, dq2, o2, scratch=[turned_f, turned_f]
    )
    pair_f, pair = shape((2, Q, D), f32), shape((2, Q, D))
    recv4, dk2 = together(recv4, dk2)
    dx1, gs, dq1, dk1, dv1, send_s, gain23, ds1 = call(
        self_back,
        "self_back",
        [quarter_f, half, both_rows, own_f, own_f, packed, line, square],
        dx2,
        part4,
        recv4,
        x1,
        norm_gains,
        self_w(3),
        k1,
        v1,
        p1,
        q1,
        o1,
        gain3,
        scratch=[pltpu.VMEM((2 * Q, 2 * W), bf16), turned_f, turned_f, pltpu.VMEM((2 * Q, D), f32)],
    )
    recv_s = over_mp(send_s, 1)
    gs_oth = over_mp(gs, 1)
    n = D // dp_size
    send_k, ds1 = together(send_k, ds1)
    recv_k = over_mp(send_k, 1)
    cross_parts, (enc_keep, enc_send, out_keep, out_send) = grad_kernel(
        cross_weights,
        "cross_weights",
        4 * W,
        send4,
        recv_h,
        e_rows(),
        dq2,
        dk2,
        dv2,
        o2,
        recv_k,
        Part(w_cross, W, W),
        Part(w_cross, 2 * W, W),
        a_own,
        Part(send3, 1, 1),
        down,
        x2,
        extra=[pair_f, pair, quarter_f, quarter],
        scratch=[pltpu.VMEM((L, 2 * W), bf16), pltpu.VMEM((2 * Q, D), f32)],
    )
    if split:
        ffn_pair, cross_pair = over_x(ffn_parts), over_x(cross_parts)
        recv_s, cross_keep, ffn_half = together(recv_s, cross_pair[0], first_half(ffn_pair))
        cross_pair = (cross_keep, cross_pair[1])
        ffn_recv = over_dp(ffn_half, 2)
    self_parts, (in_keep, in_send, small) = grad_kernel(
        self_weights,
        "self_weights",
        4 * W,
        h1,
        gs,
        gs_oth,
        o1,
        dq1,
        dk1,
        dv1,
        recv_s,
        Part(w_self, 0, 3 * W),
        norm_gains,
        ds1,
        bucket_line,
        gain23,
        buckets=buckets,
        wide=4 * heads * buckets,
        extra=[pair_f, pair, shape((8, D), f32)],
        scratch=[pltpu.VMEM((L, 3 * W), bf16)],
        send_rows=D // 2 + 16,
    )
    def halves(v):
        high = v.astype(bf16)
        return [high, (v - high.astype(f32)).astype(bf16)]

    def passed_on(keep, recv):
        return (keep[1] + recv[1].astype(f32)).astype(bf16)

    def add_tail(v, tail):
        return v + (tail[:8].astype(f32) + tail[8:].astype(f32))

    if split:
        self_recv = over_dp(self_parts[1], 1)
        in_send, enc_send, ffn_recv = together(in_send, enc_send, ffn_recv)
    in_recv, enc_recv = over_mp(in_send, 1), over_mp(enc_send, 1)
    across = jnp.concatenate([passed_on(in_keep, in_recv), passed_on(enc_keep, enc_recv), out_send])
    across = over_mp(across, 2)
    if split:
        self_recv, in_recv, enc_recv = together(self_recv, in_recv, enc_recv)
        keep, recv = self_parts[0], self_recv
        m = D // 2
        small = add_tail(small, recv[m:])
        tail = halves(small)
        self_total = keep[0].astype(f32) + recv[:n].astype(f32)
        for i in range(1, dp_size // 2):
            block = (keep[i].astype(f32) + recv[i * n : (i + 1) * n].astype(f32)).astype(bf16)
            last = over_dp(jnp.concatenate([block, *tail]), (0, 4, 2, 6)[i])
            self_total = self_total + last[:n].astype(f32)
            small = add_tail(small, last[n:])
        ffn_last = over_dp(second_half(ffn_pair, ffn_recv), 4)
        ffn_total = finish(ffn_pair, ffn_recv, ffn_last)
        cross_recv = over_dp(first_half(cross_pair), 2)
        cross_last = over_dp(second_half(cross_pair, cross_recv), 4)
        small = small + over_mp(small, 1)
        small, across, cross_last = together(small, across, cross_last)
        cross_total = finish(cross_pair, cross_recv, cross_last)
    else:
        small = lax.psum(small, "dp")
        small = small + over_mp(small, 1)
        ffn_total, cross_total, self_total = map(scatter, (ffn_parts, cross_parts, self_parts))
    grad_up, grad_down = ffn_total[:, :F], ffn_total[:, F:]

    def sum_rows(keep, recv, last):
        return keep[0] + recv[0].astype(f32) + last.astype(f32)

    grad_rows, _ = norm_back(decoder_in[0].astype(f32), norm_gains[0:1], sum_rows(in_keep, in_recv, across[:Q]))
    grad_decoder = (dx1 + grad_rows).astype(bf16)
    grad_encoder = sum_rows(enc_keep, enc_recv, across[Q : 2 * Q]).astype(bf16)
    output = (out_keep + across[2 * Q :].astype(f32)).astype(bf16)

    small = small + over_mp(small, 2)
    gain_total = small[:3]
    table_total = small[3, : 4 * heads * buckets].reshape(4 * heads, buckets).T
    grad_cq, grad_ck, grad_cv, grad_co = columns(cross_total, 4)
    grad_sq, grad_sk, grad_sv, grad_so = columns(self_total, 4)

    def row(v):
        return v.reshape((1,) + v.shape)

    return (
        row(output),
        row(grad_decoder),
        row(grad_encoder),
        grad_sq,
        grad_sk,
        grad_sv,
        grad_so,
        grad_cq,
        grad_ck,
        grad_cv,
        grad_co,
        grad_up,
        grad_down,
        gain_total,
        table_total,
    )


def solution(mesh):
    rows = P("dp", "mp", None)
    cols = P(None, "mp")
    grads = P("dp", "mp")
    in_specs = (rows, rows, P("dp", None), P("dp", None), P(), P(), cols) + (cols,) * 10 + (rows,)
    out_specs = (rows, rows, rows) + (grads,) * 10 + (P(), P())
    body = functools.partial(local, dp_size=mesh.shape["dp"])
    return jax.shard_map(body, mesh=mesh, in_specs=in_specs, out_specs=out_specs, check_vma=False)
```
